32 devices in a mesh: seq: 16 (over z, x, core), span: 2 (over y).
Axes of the slice: x: 2, y: 2, z: 4, core: 2. Of those that a mesh axis runs over, the one named last changes fastest.
Arguments:
- tokens: bfloat16 [1, 16384, 768], P(None, ('seq', 'span')), may hold values from -6 to 6
- out_cotangent: bfloat16 [1, 16384, 768], P(None, ('seq', 'span')), may hold values from -6 to 6
- crop_offset: int32 [1, 16], P(None, 'seq'), may hold values from 0 to 255
- start_kept: int32 [1, 16], P(None, 'seq'), may hold values 0 or 1
- norm1_gain: bfloat16 [768], P('span'), may hold values from 0.5 to 1.5
- norm1_bias: bfloat16 [768], P('span'), may hold values from -1.1953125 to 1.1953125
- w_query: bfloat16 [768, 768], P('span'), may hold values from -0.21875 to 0.21875
- b_query: bfloat16 [768], P('span'), may hold values from -1.1953125 to 1.1953125
- w_key: bfloat16 [768, 768], P('span'), may hold values from -0.21875 to 0.21875
- b_key: bfloat16 [768], P('span'), may hold values from -1.1953125 to 1.1953125
- w_value: bfloat16 [768, 768], P('span'), may hold values from -0.21875 to 0.21875
- b_value: bfloat16 [768], P('span'), may hold values from -1.1953125 to 1.1953125
- w_out: bfloat16 [768, 768], P('span'), may hold values from -3.5 to 3.5
- b_out: bfloat16 [768], P('span'), may hold values from -1.1953125 to 1.1953125
- norm2_gain: bfloat16 [768], P('span'), may hold values from 0.5 to 1.5
- norm2_bias: bfloat16 [768], P('span'), may hold values from -1.1953125 to 1.1953125
- w_up: bfloat16 [768, 3072], P('span'), may hold values from -0.21875 to 0.21875
- b_up: bfloat16 [3072], P('span'), may hold values from -1.1953125 to 1.1953125
- w_down: bfloat16 [3072, 768], P('span'), may hold values from -0.109375 to 0.109375
- b_down: bfloat16 [768], P('span'), may hold values from -1.1953125 to 1.1953125
Outputs:
- layer_out: bfloat16 [1, 16384, 768], P(None, ('seq', 'span'))
- input_grad: bfloat16 [1, 16384, 768], P(None, ('seq', 'span'))
- grad_norm1_gain: float32 [768], P('span')
- grad_norm1_bias: float32 [768], P('span')
- grad_w_query: float32 [768, 768], P('span')
- grad_b_query: float32 [768], P('span')
- grad_w_key: float32 [768, 768], P('span')
- grad_b_key: float32 [768], P('span')
- grad_w_value: float32 [768, 768], P('span')
- grad_b_value: float32 [768], P('span')
- grad_w_out: float32 [768, 768], P('span')
- grad_b_out: float32 [768], P('span')
- grad_norm2_gain: float32 [768], P('span')
- grad_norm2_bias: float32 [768], P('span')
- grad_w_up: float32 [768, 3072], P('span')
- grad_b_up: float32 [3072], P('span')
- grad_w_down: float32 [3072, 768], P('span')
- grad_b_down: float32 [768], P('span')
The draws below stay inside these ranges and needn't reach their ends.
Inputs may be any that keep to these rules, and one draw needn't show every extreme that they name: `crop_offset`: keys before a crop's first gene codon are padding only where the crop keeps its start codon.
All inputs are finite; a program needn't handle non-finite values. No bound on the sum of `start_kept` on one device may be relied on, other than what follows from the above.
Results may differ from the reference program's by a relative error of at most 0.017.
Values may be sent and summed in bfloat16 or wider, within the bound.
No kernel may reach another device: no remote copies, remote signals or barrier semaphores. Data moves between devices by JAX's collectives and lax.ppermute only.
A program may use at most 192 MiB of HBM per device.

```python
import math
import jax
import jax.numpy as jnp
from jax import lax

D = 768
HEADS = 12
HEAD_DIM = 64
FF = 3072
SEQ_PER = 1
SEQ_LEN = 1024
SEQS = 16
N_SEQ = 16


def with_ends(entries, stream_key, low, largest):
    longest = entries.shape.index(max(entries.shape))
    spots = []
    for shift in (0, 1):
        where = [jax.random.randint(jax.random.fold_in(stream_key, axis), (), 0, length) for axis, length in enumerate(entries.shape)]
        where[longest] = (where[longest] + shift) % entries.shape[longest]
        spots.append(tuple(where))
    return entries.at[spots[0]].set(low).at[spots[1]].set(largest)


def level_of(own_key, dims, split, low, largest):
    loudness, own = 1.0, jax.random.fold_in(own_key, 6)
    for dim, blocks in split:
        steps = jnp.exp(jax.random.uniform(jax.random.fold_in(own, dim), (blocks,), jnp.float32, low / len(split), largest / len(split)))
        loudness = loudness * jnp.repeat(steps, dims[dim] // blocks).reshape([-1 if axis == dim else 1 for axis in range(len(dims))])
    return loudness


def gaussian(key, extent, width, reach, shards=(), kind=jnp.bfloat16):
    factor_of = level_of(key, extent, shards, -0.22, 0.18) if shards else 1.0
    result = jax.random.normal(key, extent, jnp.float32) * width * factor_of
    return jnp.minimum(jnp.maximum(result, -reach), reach).astype(kind)


def setup_inputs(seed: int = 0) -> dict:
    key_list = jax.random.split(jax.random.key(seed), 21)
    tokens = gaussian(key_list[0], (SEQ_PER, N_SEQ * SEQ_LEN, D), 1.0, 6.0, ((1, 32),))
    out_cotangent = gaussian(key_list[1], (SEQ_PER, N_SEQ * SEQ_LEN, D), 1.0, 6.0, ((1, 32),))
    crop_offset = with_ends(jax.random.randint(key_list[2], (SEQ_PER, N_SEQ), 0, SEQ_LEN // 4), jax.random.fold_in(key_list[2], 1), 0, (SEQ_LEN // 4) - 1).astype(jnp.int32)
    start_kept = with_ends((jax.random.randint(key_list[3], (SEQ_PER, N_SEQ), 0, 2) < 1).astype(jnp.int32), jax.random.fold_in(key_list[3], 1), 0, 1)
    norm1_gain = jnp.clip(1.0 + 0.1 * jax.random.normal(key_list[4], (D,), jnp.float32), 0.5, 1.5).astype(jnp.bfloat16)
    norm1_bias = gaussian(key_list[5], (D,), 0.3, 1.1953125, ((0, 2),))
    w_query = gaussian(key_list[6], (D, D), D ** -0.5, 0.21875, ((0, 2),))
    b_query = gaussian(key_list[7], (D,), 0.3, 1.1953125, ((0, 2),))
    w_key = gaussian(key_list[8], (D, D), D ** -0.5, 0.21875, ((0, 2),))
    b_key = gaussian(key_list[9], (D,), 0.3, 1.1953125, ((0, 2),))
    w_value = gaussian(key_list[10], (D, D), D ** -0.5, 0.21875, ((0, 2),))
    b_value = gaussian(key_list[11], (D,), 0.3, 1.1953125, ((0, 2),))
    w_out = gaussian(key_list[12], (D, D), (max(D // 256, 1)) ** -0.5, 3.5, ((0, 2),))
    b_out = gaussian(key_list[13], (D,), 0.3, 1.1953125, ((0, 2),))
    norm2_gain = jnp.clip(1.0 + 0.1 * jax.random.normal(key_list[14], (D,), jnp.float32), 0.5, 1.5).astype(jnp.bfloat16)
    norm2_bias = gaussian(key_list[15], (D,), 0.3, 1.1953125, ((0, 2),))
    w_up = gaussian(key_list[16], (D, FF), D ** -0.5, 0.21875, ((0, 2),))
    b_up = gaussian(key_list[17], (FF,), 0.3, 1.1953125, ((0, 2),))
    w_down = gaussian(key_list[18], (FF, D), FF ** -0.5, 0.109375, ((0, 2),))
    b_down = gaussian(key_list[19], (D,), 0.3, 1.1953125, ((0, 2),))
    return {"tokens": tokens, "out_cotangent": out_cotangent, "crop_offset": crop_offset, "start_kept": start_kept, "norm1_gain": norm1_gain, "norm1_bias": norm1_bias, "w_query": w_query, "b_query": b_query, "w_key": w_key, "b_key": b_key, "w_value": w_value, "b_value": b_value, "w_out": w_out, "b_out": b_out, "norm2_gain": norm2_gain, "norm2_bias": norm2_bias, "w_up": w_up, "b_up": b_up, "w_down": w_down, "b_down": b_down}


@jax.custom_vjp
def low(v):
    return lax.optimization_barrier(v.astype(jnp.bfloat16)).astype(jnp.float32)

@jax.custom_vjp
def low_back(v):
    return v

def low_keep(v):
    return (low(v), None)

def low_pass(kept, grad):
    return (grad,)

def back_keep(v):
    return (v, None)

def back_low(kept, grad):
    return (low(grad),)
low.defvjp(low_keep, low_pass)
low_back.defvjp(back_keep, back_low)

def layer_norm(rows, gain, shift):
    center = rows - lax.optimization_barrier(jnp.mean(rows, axis=-1, keepdims=True))
    spread = lax.optimization_barrier(jnp.mean(center * center, axis=-1, keepdims=True))
    return center * lax.rsqrt(spread + 1e-05) * gain + shift

def rotate(rows, cosine, sine):
    half = rows.shape[-1] // 2
    first = rows[..., :half]
    second = rows[..., half:]
    return jnp.concatenate([first * cosine - second * sine, second * cosine + first * sine], axis=-1)

def one_sequence(rows, first, weights):
    gain_one, shift_one, wquery, bquery, wkey, bkey, wvalue, bvalue, wproj, bproj, gain_two, shift_two, wupper, bupper, wlower, blower = weights
    highest = lax.Precision.HIGHEST
    half = HEAD_DIM // 2
    normed = low(layer_norm(rows, gain_one, shift_one))
    query_pre = low_back(jnp.dot(normed, wquery, precision=highest) + bquery)
    key_pre = low_back(jnp.dot(normed, wkey, precision=highest) + bkey)
    values = low_back(low(jnp.dot(normed, wvalue, precision=highest) + bvalue))
    places = (jnp.arange(SEQ_LEN, dtype=jnp.int32) - first).astype(jnp.float32)
    rates = jnp.power(jnp.float32(10000.0), -jnp.arange(half, dtype=jnp.float32) / half)
    angle = places[:, None] * rates[None, :]
    cosine = jnp.cos(angle)[:, None, :]
    sine = jnp.sin(angle)[:, None, :]
    query = low_back(low(rotate(query_pre.reshape(SEQ_LEN, HEADS, HEAD_DIM), cosine, sine)))
    keys = low_back(low(rotate(key_pre.reshape(SEQ_LEN, HEADS, HEAD_DIM), cosine, sine)))
    values = values.reshape(SEQ_LEN, HEADS, HEAD_DIM)
    scale = HEAD_DIM ** (-0.5)
    scores = low_back(jnp.einsum('qhd,khd->hqk', query, keys, precision=highest) * scale)
    usable = jnp.arange(SEQ_LEN, dtype=jnp.int32) >= first
    scores = jnp.where(usable[None, None, :], scores, -1e+30)
    top = lax.optimization_barrier(jnp.max(scores, axis=-1, keepdims=True))
    expo = jnp.exp(scores - top)
    probs = low(expo / lax.optimization_barrier(jnp.sum(expo, axis=-1, keepdims=True)))
    mixed = jnp.einsum('hqk,khd->qhd', probs, values, precision=highest).reshape(SEQ_LEN, D)
    mixed = low_back(low(mixed))
    attended = low_back(jnp.dot(mixed, wproj, precision=highest) + bproj)
    hidden = rows + attended
    normed_two = low(layer_norm(hidden, gain_two, shift_two))
    inner = low_back(jnp.dot(normed_two, wupper, precision=highest) + bupper)
    active = low(jax.nn.gelu(inner, approximate=False))
    return hidden + jnp.dot(active, wlower, precision=highest) + blower

def reference(tokens, out_cotangent, crop_offset, start_kept, norm1_gain, norm1_bias, w_query, b_query, w_key, b_key, w_value, b_value, w_out, b_out, norm2_gain, norm2_bias, w_up, b_up, w_down, b_down):
    weights = tuple((item.astype(jnp.float32) for item in (norm1_gain, norm1_bias, w_query, b_query, w_key, b_key, w_value, b_value, w_out, b_out, norm2_gain, norm2_bias, w_up, b_up, w_down, b_down)))
    group = math.gcd(SEQS, max(1, 4096 // SEQ_LEN))
    groups = SEQS // group
    inputs = tokens.astype(jnp.float32).reshape(groups, group, SEQ_LEN, D)
    firsts = (crop_offset * start_kept).astype(jnp.int32).reshape(groups, group)

    def whole(inputs, weights):

        def step(carry, item):
            rows, first = item
            outs = jax.vmap(lambda r, f: one_sequence(r, f, weights))(rows, first)
            return (carry, outs)
        _, outs = lax.scan(jax.checkpoint(step), jnp.zeros((), jnp.float32), (inputs, firsts))
        return outs
    outs, pullback = jax.vjp(whole, inputs, weights)
    cotan = out_cotangent.astype(jnp.float32).reshape(groups, group, SEQ_LEN, D)
    dinputs, dweights = pullback(cotan)
    layer_out = outs.reshape(SEQ_PER, N_SEQ * SEQ_LEN, D).astype(jnp.bfloat16)
    input_grad = dinputs.reshape(SEQ_PER, N_SEQ * SEQ_LEN, D).astype(jnp.bfloat16)
    return (layer_out, input_grad, dweights[0], dweights[1], dweights[2], dweights[3], dweights[4], dweights[5], dweights[6], dweights[7], dweights[8], dweights[9], dweights[10], dweights[11], dweights[12], dweights[13], dweights[14], dweights[15])
```

```python
import functools

import jax
import jax.numpy as jnp
from jax import lax
from jax.experimental import pallas as pl
from jax.experimental.pallas import tpu as pltpu
from jax.sharding import PartitionSpec as P

HEADS = 12
HEAD_DIM = 64
SCALE = HEAD_DIM ** (-0.5)
F32 = jnp.float32
BF16 = jnp.bfloat16
VMEM_BYTES = 60 * 1024 * 1024
COST = pl.CostEstimate(flops=10**11, bytes_accessed=1024, transcendentals=0)


def deep_of(spot):
    return (spot >> 1) | ((spot & 1) << 1)


def dot(left, right, dim_l, dim_r):
    return lax.dot_general(
        left, right, (((dim_l,), (dim_r,)), ((), ())), preferred_element_type=F32
    )


def swap_halves(rows):
    half = rows.shape[-1] // 2
    return jnp.concatenate([rows[:, half:], rows[:, :half]], axis=1)


def own_first(rows, place):
    return jnp.where(place == 0, rows, swap_halves(rows))


def half_swap(tile):
    lane = lax.broadcasted_iota(jnp.int32, tile.shape, 1)
    width = tile.shape[1]
    return jnp.where(
        lane % HEAD_DIM < HEAD_DIM // 2,
        pltpu.roll(tile, width - HEAD_DIM // 2, 1),
        pltpu.roll(tile, HEAD_DIM // 2, 1),
    )


def params(**kw):
    return pltpu.CompilerParams(vmem_limit_bytes=VMEM_BYTES, **kw)


def vmem():
    return pl.BlockSpec(memory_space=pltpu.VMEM)


def anywhere():
    return pl.BlockSpec(memory_space=pl.ANY)


def qkv_kernel(
    scal, own_ref, oth_ref, vec_ref, cos_ref, sin_ref, wq, wk, wv, p0, p1, p2,
    n1t_ref, q_ref, k_ref, v_ref, wall_ref, sems,
):
    step = pl.program_id(0)
    place = scal[0]
    half = wq.shape[0]

    @pl.when(step == 0)
    def _():
        copies = []
        for j, weight in enumerate((wq, wk, wv)):
            target = wall_ref.at[j]
            own = (weight, target.at[pl.ds(0, half)])
            copies += piece_copies(own, (p0, p1, p2), scal, lambda p, j=j: p.at[j], target, half)
        wait_all(start_all(copies, sems, 0))

    rows = jnp.where(step < 2, own_ref[...], oth_ref[...]).astype(F32)
    center = rows - jnp.mean(rows, axis=1, keepdims=True)
    spread = jnp.mean(center * center, axis=1, keepdims=True)
    normed = center * lax.rsqrt(spread + 1e-05) * vec_ref[0:1] + vec_ref[1:2]
    normed = own_first(normed, place).astype(BF16)
    n1t_ref[...] = normed.T

    def rotated(j, ref, factor):
        flat = dot(normed, wall_ref[j], 1, 0) + vec_ref[2 + j : 3 + j]
        for t in range(flat.shape[1] // 128):
            tile = flat[:, t * 128 : (t + 1) * 128]
            turned = (tile * cos_ref[...] + half_swap(tile) * sin_ref[...]).astype(BF16)
            ref[:, t * 128 : (t + 1) * 128] = turned * factor if factor != 1 else turned

    @pl.when(step < 2)
    def _():
        rotated(0, q_ref, SCALE)

    rotated(1, k_ref, 1)
    v_ref[...] = (dot(normed, wall_ref[2], 1, 0) + vec_ref[4:5]).astype(BF16)


def qkv(scal, own, oth, vec, cos, sin, weights, pieces):
    rows, width = own.shape
    block = rows // 2
    grid_spec = pltpu.PrefetchScalarGridSpec(
        num_scalar_prefetch=1,
        grid=(4,),
        in_specs=[
            pl.BlockSpec((block, width), lambda i, s: (jnp.minimum(i, 1), 0)),
            pl.BlockSpec((block, width), lambda i, s: (jnp.maximum(i - 2, 0), 0)),
            pl.BlockSpec(vec.shape, lambda i, s: (0, 0)),
            pl.BlockSpec((block, 128), lambda i, s: (i, 0)),
            pl.BlockSpec((block, 128), lambda i, s: (i, 0)),
        ]
        + [anywhere()] * 6,
        out_specs=[
            pl.BlockSpec((width, block), lambda i, s: (0, i)),
            pl.BlockSpec((block, width), lambda i, s: (jnp.minimum(i, 1), 0)),
            pl.BlockSpec((block, width), lambda i, s: (i, 0)),
            pl.BlockSpec((block, width), lambda i, s: (i, 0)),
            pl.BlockSpec((3, width, width), lambda i, s: (0, 0, 0)),
        ],
        scratch_shapes=[pltpu.SemaphoreType.DMA((15,))],
    )
    shape = jax.ShapeDtypeStruct
    return pl.pallas_call(
        qkv_kernel,
        grid_spec=grid_spec,
        out_shape=[
            shape((width, 2 * rows), BF16),
            shape((rows, width), BF16),
            shape((2 * rows, width), BF16),
            shape((2 * rows, width), BF16),
            shape((3, width, width), BF16),
        ],
        compiler_params=params(),
        cost_estimate=COST,
        name="qkv",
    )(scal, own, oth, vec, cos, sin, *weights, *pieces)


def key_bias(scal, keys):
    place, first = scal[0], scal[3]
    half = keys // 2
    row = lax.broadcasted_iota(jnp.int32, (keys, 128), 0)
    where = jnp.where(row < half, place * half + row, (1 - place) * half + row - half)
    return jnp.where(where < first, -1e30, 0.0).astype(BF16)


def masked_pair(head, keys, query, bias):
    lane_k = lax.broadcasted_iota(jnp.int32, keys.shape, 1)
    lane_q = lax.broadcasted_iota(jnp.int32, query.shape, 1)
    spot = (1 - head) * HEAD_DIM
    zero = jnp.zeros((), BF16)
    keys = jnp.where(
        lane_k // HEAD_DIM == head, keys, jnp.where(lane_k == spot, bias, zero)
    )
    query = jnp.where(
        lane_q // HEAD_DIM == head,
        query,
        jnp.where(lane_q == spot, jnp.ones((), BF16), zero),
    )
    return keys, query


def attend_kernel(scal, q_ref, k_ref, v_ref, *refs):
    o_ref, lse_ref = refs[-2:]
    keys, values, query = k_ref[...], v_ref[...], q_ref[...]
    bias = key_bias(scal, keys.shape[0])
    values_t = values.T
    outs = []
    for head in range(2):
        keys_m, query_m = masked_pair(head, keys, query, bias)
        scores = dot(keys_m, query_m, 1, 1)
        top = jnp.max(scores, axis=0, keepdims=True)
        expo = jnp.exp(scores - top)
        total = jnp.sum(expo, axis=0, keepdims=True)
        mixed = dot(
            values_t[head * HEAD_DIM : (head + 1) * HEAD_DIM], expo.astype(BF16), 1, 0
        )
        outs.append(mixed / total)
        lse_ref[0, head : head + 1] = top + jnp.log(total)
    o_ref[...] = jnp.concatenate(outs, axis=0).T.astype(BF16)


def attend(scal, query, keys, values, begin, earlier=()):
    rows, width = query.shape
    span = keys.shape[0]
    pairs = width // 256
    grid_spec = pltpu.PrefetchScalarGridSpec(
        num_scalar_prefetch=1,
        grid=(pairs,),
        in_specs=[
            pl.BlockSpec((rows, 128), lambda i, s: (0, i + begin)),
            pl.BlockSpec((span, 128), lambda i, s: (0, i + begin)),
            pl.BlockSpec((span, 128), lambda i, s: (0, i + begin)),
        ]
        + [anywhere()] * len(earlier),
        out_specs=[
            pl.BlockSpec((rows, 128), lambda i, s: (0, i + begin)),
            pl.BlockSpec((1, 8, rows), lambda i, s: (i + begin, 0, 0)),
        ],
    )
    return pl.pallas_call(
        attend_kernel,
        grid_spec=grid_spec,
        out_shape=[
            jax.ShapeDtypeStruct((rows, width), BF16),
            jax.ShapeDtypeStruct((2 * pairs, 8, rows), F32),
        ],
        input_output_aliases={4: 0, 5: 1} if earlier else {},
        compiler_params=params(),
        cost_estimate=COST,
        name="attend",
    )(scal, query, keys, values, *earlier)


def attend_back_kernel(
    scal, q_ref, k_ref, v_ref, o_ref, do_ref, lse_ref, cos_ref, sin_ref, *refs
):
    dq_ref, dk_ref, dv_ref, bias_ref = refs[-4:]
    keys, values, query, dout = k_ref[...], v_ref[...], q_ref[...], do_ref[...]
    rows = query.shape[0]
    bias = key_bias(scal, keys.shape[0])
    keys_t = keys.T
    product = (dout.astype(F32) * o_ref[...].astype(F32)).T
    lane = lax.broadcasted_iota(jnp.int32, values.shape, 1)
    parts = []
    for head in range(2):
        keys_m, query_m = masked_pair(head, keys, query, bias)
        values_m = jnp.where(lane // HEAD_DIM == head, values, jnp.zeros((), BF16))
        inner = jnp.sum(
            product[head * HEAD_DIM : (head + 1) * HEAD_DIM], axis=0, keepdims=True
        )
        probs = jnp.exp(dot(keys_m, query_m, 1, 1) - lse_ref[0, head : head + 1])
        grad = dot(values_m, dout, 1, 1)
        score_grad = (probs * (grad - inner)).astype(BF16)
        dv = dot(probs.astype(BF16), dout, 1, 0)
        dk = dot(score_grad, query, 1, 0)
        dq = dot(keys_t[head * HEAD_DIM : (head + 1) * HEAD_DIM], score_grad, 1, 0)
        parts.append((dq, dk, dv))
    dq = (jnp.concatenate([parts[0][0], parts[1][0]], axis=0).T * SCALE).astype(BF16)
    dk = jnp.where(lane // HEAD_DIM == 0, parts[0][1], parts[1][1]).astype(BF16)
    dv = jnp.where(lane // HEAD_DIM == 0, parts[0][2], parts[1][2]).astype(BF16)
    dq, dk = dq.astype(F32), dk.astype(F32)
    dq = (dq * cos_ref[:rows] - half_swap(dq) * sin_ref[:rows]).astype(BF16)
    dk = (dk * cos_ref[...] - half_swap(dk) * sin_ref[...]).astype(BF16)
    dq_ref[...] = dq
    dk_ref[...] = dk
    dv_ref[...] = dv
    bias_ref[0:1] = jnp.sum(dq.astype(F32), axis=0, keepdims=True)
    bias_ref[1:2] = jnp.sum(dk.astype(F32), axis=0, keepdims=True)
    bias_ref[2:3] = jnp.sum(dv.astype(F32), axis=0, keepdims=True)


def attend_back(scal, query, keys, values, mixed, dout, lse, cos, sin, theirs, begin, pairs, earlier=()):
    rows, width = query.shape[0], query.shape[1] // 2
    span = keys.shape[0]

    def at(i, s):
        return begin + i + (width // 128) * (1 - s[1] if theirs else s[1])

    few = pl.BlockSpec((rows, 128), lambda i, s: (0, at(i, s)))
    many = pl.BlockSpec((span, 128), lambda i, s: (0, at(i, s)))
    few_out = pl.BlockSpec((rows, 128), lambda i, s: (0, begin + i))
    many_out = pl.BlockSpec((span, 128), lambda i, s: (0, begin + i))
    table = pl.BlockSpec((span, 128), lambda i, s: (0, 0))
    grid_spec = pltpu.PrefetchScalarGridSpec(
        num_scalar_prefetch=1,
        grid=(pairs,),
        in_specs=[few, many, many, few, few]
        + [pl.BlockSpec((1, 8, rows), lambda i, s: (at(i, s), 0, 0)), table, table]
        + [anywhere()] * len(earlier),
        out_specs=[few_out, many_out, many_out, pl.BlockSpec((8, 128), lambda i, s: (0, begin + i))],
    )
    shape = jax.ShapeDtypeStruct
    return pl.pallas_call(
        attend_back_kernel,
        grid_spec=grid_spec,
        out_shape=[
            shape((rows, width), BF16),
            shape((span, width), BF16),
            shape((span, width), BF16),
            shape((8, width), F32),
        ],
        input_output_aliases={9 + n: n for n in range(len(earlier))},
        compiler_params=params(),
        cost_estimate=COST,
        name="attend_back",
    )(scal, query, keys, values, mixed, dout, lse, cos, sin, *earlier)


def norm_stats(rows):
    center = rows - jnp.mean(rows, axis=1, keepdims=True)
    spread = jnp.mean(center * center, axis=1, keepdims=True)
    return center, lax.rsqrt(spread + 1e-05)


def norm_back(rows, grad, gain):
    center, rate = norm_stats(rows)
    hat = center * rate
    scaled = grad * gain
    out = rate * (
        scaled
        - jnp.mean(scaled, axis=1, keepdims=True)
        - hat * jnp.mean(scaled * hat, axis=1, keepdims=True)
    )
    return (
        out,
        jnp.sum(grad * hat, axis=0, keepdims=True),
        jnp.sum(grad, axis=0, keepdims=True),
    )


def piece_copies(own, pieces, scal, select, target, base):
    bit, core = scal[1], scal[2]
    p0, p1, p2 = pieces
    spots = (
        (p0, 2 * bit + core),
        (p1, 2 * (1 - bit) + core),
        (p2.at[0], 2 * bit + 1 - core),
        (p2.at[1], 2 * (1 - bit) + 1 - core),
    )
    copies = [] if own is None else [own]
    for src, index in spots:
        part = select(src)
        rows = part.shape[0]
        start = pl.multiple_of(base + index * rows, 32)
        copies.append((part, target.at[pl.ds(start, rows)]))
    return copies


def load_out(scal, wo_own, pieces, wo_s):
    half = wo_own.shape[0]
    copies = [(wo_own, wo_s.at[pl.ds(0, half)])]
    for n in range(2):
        target = wo_s.at[:, pl.ds(n * half, half)]
        copies += piece_copies(None, pieces, scal, lambda p, n=n: p.at[8 + n], target, half)
    return copies


def load_chunk(scal, part, t, up_own, down_own, pieces, up_s, down_s):
    place = scal[0]
    core = scal[2] if t == 1 else 1 - scal[2]
    half = up_own.shape[0]
    copies = []
    for n, span in enumerate((1 - place, place)):
        index = 2 * span + core
        column = pl.multiple_of((2 * index + part) * half, 128)
        target = up_s.at[t, :, pl.ds(n * half, half)]
        own = (up_own.at[:, pl.ds(column, half)], target.at[pl.ds(0, half)])
        copies += piece_copies(own, pieces, scal, lambda p, index=index: p.at[index], target, half)
    start = pl.multiple_of((2 * core + part) * half, 128)
    copies.append((down_own.at[pl.ds(start, half)], down_s.at[t, pl.ds(half, half)]))
    for n in range(2):
        target = down_s.at[t, :, pl.ds(n * half, half)]
        copies += piece_copies(
            None, pieces, scal, lambda p, n=n: p.at[4 + 2 * core + n], target, 0
        )
    return copies


def start_all(copies, sems, base):
    started = [
        pltpu.make_async_copy(src, dst, sems.at[base + n]) for n, (src, dst) in enumerate(copies)
    ]
    for copy in started:
        copy.start()
    return started


def wait_all(started):
    for copy in started:
        copy.wait()


def ffn_step(scal, t, part, dy_ref, bup_ref, n2_s, n2t_s, up_s, down_s, acc_s, dacc_s, a_s, du_s, gbup_ref):
    place = scal[0]
    core = scal[2] if t == 1 else 1 - scal[2]
    rows, width = dy_ref.shape
    half = width // 2
    block = rows // 4
    spot = [2 * (2 * span + core) + part for span in (1 - place, place)]
    bias = jnp.concatenate([bup_ref[pl.ds(n, 1)] for n in spot], axis=1)
    total = jnp.zeros((1, width), F32)
    for r in range(0, rows, block):
        at = slice(r, r + block)
        inner = dot(n2_s[at], up_s[t], 1, 0) + bias
        active_grad = dot(dy_ref[at], down_s[t], 1, 1)
        phi = 0.5 + 0.5 * lax.erf(inner * 0.7071067811865476)
        slope = phi + inner * (0.3989422804014327 * jnp.exp(-0.5 * inner * inner))
        a_s[at] = (inner * phi).astype(BF16)
        du = (active_grad * slope).astype(BF16)
        du_s[at] = du
        total = total + jnp.sum(du.astype(F32), axis=0, keepdims=True)
    for n, row in enumerate(spot):
        gbup_ref[pl.ds(row, 1)] = total[:, n * half : (n + 1) * half]
    acc_s[...] += dot(a_s[...], down_s[t], 1, 0)
    dacc_s[...] += dot(du_s[...], up_s[t], 1, 1)
    down_grad = dot(a_s[...], dy_ref[...], 0, 0).astype(BF16)
    up_grad = dot(n2t_s[...], du_s[...], 1, 0).astype(BF16)
    return down_grad, up_grad


def place_grads(scal, down_grad, up_grad, out_ref, gd_s, gu_s, x_first):
    place, bit, deep = scal[0], scal[1], scal[4]
    half = gd_s.shape[0] // 2
    size = half // 4
    gd_s[...] = down_grad
    gu_s[...] = up_grad
    for s in range(2):
        for k in range(2):
            column = bit if k == 0 else 1 - bit
            down_at = pl.multiple_of(column * half, 128)
            up_at = pl.multiple_of(jnp.where(column == place, half, 0), 128)
            i, j = (k, s) if x_first else (s, k)
            for d in range(4):
                row = (deep ^ deep_of(d)) * size
                down_row = pl.multiple_of((1 - s) * half + row, 32)
                up_row = pl.multiple_of(s * half + row, 32)
                out_ref[i, j, d, :size] = gd_s[pl.ds(down_row, size), pl.ds(down_at, half)]
                out_ref[i, j, d, size : 2 * size] = gu_s[pl.ds(up_row, size), pl.ds(up_at, half)]


def ffn_first_kernel(
    scal, x_ref, o_ref, dy_ref, vec_ref, bup_ref, wo_own, up_own, down_own, p0, p1, p2,
    h_ref, n2_ref, acc_ref, dacc_ref, send_ref, keep_ref, gbup_ref, wo_out,
    n2t_s, a_s, du_s, up_s, down_s, gd_s, gu_s, wo_s, sems,
):
    place = scal[0]
    rows, width = x_ref.shape
    half = width // 2
    block = rows // 4
    outs = start_all(load_out(scal, wo_own, (p0, p1, p2), wo_s), sems, 0)
    chunks = []
    for t in range(2):
        copies = load_chunk(scal, 0, t, up_own, down_own, (p0, p1, p2), up_s, down_s)
        chunks.append(start_all(copies, sems, 9 + 19 * t))
    gbup_ref[...] = jnp.zeros_like(gbup_ref)
    wait_all(outs)
    for r in range(0, rows, block):
        at = slice(r, r + block)
        mixed = own_first(o_ref[at], place)
        hidden = x_ref[at].astype(F32) + dot(mixed, wo_s[...], 1, 0) + vec_ref[2:3]
        h_ref[at] = hidden
        center, rate = norm_stats(hidden)
        normed = center * rate * vec_ref[0:1] + vec_ref[1:2]
        n2_ref[at] = own_first(normed, place).astype(BF16)
        acc_ref[at] = hidden + vec_ref[3:4]
        dacc_ref[at] = jnp.zeros((block, width), F32)
    wo_out[...] = wo_s[...]
    n2t_s[...] = n2_ref[...].T
    for t in range(2):
        wait_all(chunks[t])
        grads = ffn_step(
            scal, t, 0, dy_ref, bup_ref, n2_ref, n2t_s, up_s, down_s, acc_ref, dacc_ref,
            a_s, du_s, gbup_ref,
        )
        place_grads(scal, *grads, keep_ref if t == 1 else send_ref, gd_s, gu_s, True)


def ffn_second_kernel(
    scal, o_ref, dy_ref, vec_ref, bup_ref, h_ref, n2_ref, acc_in, dacc_in, wo_ref,
    up_own, down_own, p0, p1, p2,
    out_ref, dh_ref, do_ref, send_ref, keep_ref, gbup_ref, small_ref,
    n2t_s, a_s, du_s, up_s, down_s, gd_s, gu_s, acc_s, dacc_s, g_s, sems,
):
    place, bit, core, deep = scal[0], scal[1], scal[2], scal[4]
    rows, width = dy_ref.shape
    half = width // 2
    block = rows // 4
    chunks = []
    for t in range(2):
        copies = load_chunk(scal, 1, t, up_own, down_own, (p0, p1, p2), up_s, down_s)
        chunks.append(start_all(copies, sems, 19 * t))
    gbup_ref[...] = jnp.zeros_like(gbup_ref)
    n2t_s[...] = n2_ref[...].T
    acc_s[...] = acc_in[...]
    dacc_s[...] = dacc_in[...]
    for t in range(2):
        wait_all(chunks[t])
        grads = ffn_step(
            scal, t, 1, dy_ref, bup_ref, n2_ref, n2t_s, up_s, down_s, acc_s, dacc_s,
            a_s, du_s, gbup_ref,
        )
        place_grads(scal, *grads, keep_ref if t == 1 else send_ref, gd_s, gu_s, False)
    sums = [jnp.zeros((1, width), F32) for _ in range(4)]
    for r in range(0, rows, block):
        at = slice(r, r + block)
        out_ref[at] = acc_s[at].astype(BF16)
        grad = own_first(dacc_s[at], place)
        dy = dy_ref[at].astype(F32)
        part, gain_sum, shift_sum = norm_back(h_ref[at], grad, vec_ref[0:1])
        dh = dy + part
        dh_ref[at] = dh
        branch = dh.astype(BF16)
        a_s[at] = branch
        do_ref[at] = own_first(dot(branch, wo_ref[...], 1, 1), place).astype(BF16)
        terms = (
            gain_sum,
            shift_sum,
            jnp.sum(branch.astype(F32), axis=0, keepdims=True),
            jnp.sum(dy, axis=0, keepdims=True),
        )
        sums = [old + new for old, new in zip(sums, terms)]
    for n, item in enumerate(sums):
        small_ref[n : n + 1] = item
    g_s[...] = own_first(dot(a_s[...], o_ref[...], 0, 0), place).T
    size = half // 8
    for s in range(2):
        for k in range(2):
            column = pl.multiple_of((bit if k == 0 else 1 - bit) * half, 128)
            for d in range(4):
                row = s * half + (deep ^ deep_of(d)) * size
                for out, mine in ((send_ref, 1 - core), (keep_ref, core)):
                    at = pl.multiple_of(row + mine * 4 * size, 16)
                    out[s, k, d, 4 * size :] = g_s[pl.ds(at, size), pl.ds(column, half)].astype(BF16)


def ffn_scratch(rows, width):
    return [
        pltpu.VMEM((width, rows), BF16),
        pltpu.VMEM((rows, width), BF16),
        pltpu.VMEM((rows, width), BF16),
        pltpu.VMEM((2, width, width), BF16),
        pltpu.VMEM((2, width, width), BF16),
        pltpu.VMEM((width, width), BF16),
        pltpu.VMEM((width, width), BF16),
    ]


def ffn_first(scal, tokens, mixed, dy, vec, bup, w_out, w_up, w_down, pieces):
    rows, width = tokens.shape
    half = width // 2
    shape = jax.ShapeDtypeStruct
    buffer = shape((2, 2, 4, half // 2, half), BF16)
    return pl.pallas_call(
        ffn_first_kernel,
        in_specs=[pl.BlockSpec(memory_space=pltpu.SMEM)] + [vmem()] * 5 + [anywhere()] * 6,
        out_specs=[vmem()] * 8,
        out_shape=[
            shape((rows, width), F32),
            shape((rows, width), BF16),
            shape((rows, width), F32),
            shape((rows, width), F32),
            buffer,
            buffer,
            shape((8, half), F32),
            shape((width, width), BF16),
        ],
        scratch_shapes=ffn_scratch(rows, width)
        + [pltpu.VMEM((width, width), BF16), pltpu.SemaphoreType.DMA((47,))],
        compiler_params=params(),
        cost_estimate=COST,
        name="ffn_first",
    )(scal, tokens, mixed, dy, vec, bup, w_out, w_up, w_down, *pieces)


def ffn_second(scal, mixed, dy, vec, bup, hidden, normed, acc, dacc, wo, w_up, w_down, pieces):
    rows, width = mixed.shape
    half = width // 2
    shape = jax.ShapeDtypeStruct
    buffer = shape((2, 2, 4, half // 2 + half // 8, half), BF16)
    return pl.pallas_call(
        ffn_second_kernel,
        in_specs=[pl.BlockSpec(memory_space=pltpu.SMEM)] + [vmem()] * 9 + [anywhere()] * 5,
        out_specs=[vmem()] * 7,
        out_shape=[
            shape((rows, width), BF16),
            shape((rows, width), F32),
            shape((rows, width), BF16),
            buffer,
            buffer,
            shape((8, half), F32),
            shape((8, width), F32),
        ],
        scratch_shapes=ffn_scratch(rows, width)
        + [
            pltpu.VMEM((rows, width), F32),
            pltpu.VMEM((rows, width), F32),
            pltpu.VMEM((width, width), F32),
            pltpu.SemaphoreType.DMA((38,)),
        ],
        compiler_params=params(),
        cost_estimate=COST,
        name="ffn_second",
    )(scal, mixed, dy, vec, bup, hidden, normed, acc, dacc, wo, w_up, w_down, *pieces)


def weight_kernel(scal, n1t_ref, dq_ref, dk_ref, dv_ref, send_ref, keep_ref, g_s):
    core, deep = scal[2], scal[4]
    half = dq_ref.shape[1]
    size = half // 8
    for w, ref in enumerate((dq_ref, dk_ref, dv_ref)):
        g_s[w] = dot(n1t_ref[:, : ref.shape[0]], ref[...], 1, 0).astype(BF16)
        for s in range(2):
            for d in range(4):
                row = s * half + (deep ^ deep_of(d)) * size
                for out, mine in ((send_ref, 1 - core), (keep_ref, core)):
                    at = pl.multiple_of(row + mine * 4 * size, 16)
                    out[s, d, w] = g_s[w, pl.ds(at, size)]


def weight_grads(scal, n1t, back):
    width, half = n1t.shape[0], back[0].shape[1]
    shape = jax.ShapeDtypeStruct((2, 4, 3, half // 8, half), BF16)
    return pl.pallas_call(
        weight_kernel,
        in_specs=[pl.BlockSpec(memory_space=pltpu.SMEM)] + [vmem()] * 4,
        out_specs=[vmem()] * 2,
        out_shape=[shape, shape],
        scratch_shapes=[pltpu.VMEM((3, width, half), BF16)],
        compiler_params=params(),
        cost_estimate=COST,
        name="weight_grads",
    )(scal, n1t, *back[:3])


def norm_grads_kernel(scal, w_ref, *refs):
    parts, (own_ref, oth_ref) = (refs[:3], refs[3:6]), refs[6:]
    step = pl.program_id(0)
    half = refs[0].shape[1]
    total = 0.0
    for theirs in range(2):
        column = pl.multiple_of((1 - scal[1] if theirs else scal[1]) * half, 128)
        dq, dk, dv = parts[theirs]
        total = total + dot(dk[...], w_ref[1, :, pl.ds(column, half)], 1, 1)
        total = total + dot(dv[...], w_ref[2, :, pl.ds(column, half)], 1, 1)

    @pl.when(step < 2)
    def _():
        oth_ref[...] = own_first(total, scal[0]).astype(BF16)

    @pl.when(step >= 2)
    def _():
        more = total
        for theirs in range(2):
            column = pl.multiple_of((1 - scal[1] if theirs else scal[1]) * half, 128)
            more = more + dot(parts[theirs][0][...], w_ref[0, :, pl.ds(column, half)], 1, 1)
        own_ref[...] = own_first(more, scal[0])


def norm_grads(scal, mine, theirs, wall):
    rows, width = mine[0].shape[0], wall.shape[2]
    half, block = width // 2, rows // 2
    shape = jax.ShapeDtypeStruct
    few = pl.BlockSpec((block, half), lambda i, s: (jnp.maximum(i - 2, 0), 0))
    many = pl.BlockSpec((block, half), lambda i, s: (jnp.where(i < 2, i + 2, i - 2), 0))
    grid_spec = pltpu.PrefetchScalarGridSpec(
        num_scalar_prefetch=1,
        grid=(4,),
        in_specs=[pl.BlockSpec(wall.shape, lambda i, s: (0, 0, 0))] + [few, many, many] * 2,
        out_specs=[
            pl.BlockSpec((block, width), lambda i, s: (jnp.maximum(i - 2, 0), 0)),
            pl.BlockSpec((block, width), lambda i, s: (jnp.minimum(i, 1), 0)),
        ],
    )
    return pl.pallas_call(
        norm_grads_kernel,
        grid_spec=grid_spec,
        out_shape=[shape((rows, width), F32), shape((rows, width), BF16)],
        compiler_params=params(),
        cost_estimate=COST,
        name="norm_grads",
    )(scal, wall, *mine[:3], *theirs[:3])


def input_kernel(x_ref, own_ref, recv_ref, dh_ref, vec_ref, out_ref, small_ref):
    step = pl.program_id(0)
    grad = own_ref[...] + recv_ref[...].astype(F32)
    part, gain_sum, shift_sum = norm_back(x_ref[...].astype(F32), grad, vec_ref[0:1])
    out_ref[...] = (dh_ref[...] + part).astype(BF16)

    @pl.when(step == 0)
    def _():
        small_ref[...] = jnp.zeros_like(small_ref)

    small_ref[0:1] += gain_sum
    small_ref[1:2] += shift_sum


def input_grads(tokens, dn_own, dn_recv, dh, vec):
    rows, width = tokens.shape
    block = rows // 4
    tile = pl.BlockSpec((block, width), lambda i: (i, 0))
    return pl.pallas_call(
        input_kernel,
        grid=(4,),
        in_specs=[tile, tile, tile, tile, pl.BlockSpec(vec.shape, lambda i: (0, 0))],
        out_specs=[tile, pl.BlockSpec((8, width), lambda i: (0, 0))],
        out_shape=[
            jax.ShapeDtypeStruct((rows, width), BF16),
            jax.ShapeDtypeStruct((8, width), F32),
        ],
        compiler_params=params(),
        cost_estimate=COST,
        name="input_grads",
    )(tokens, dn_own, dn_recv, dh, vec)


def spot_of(scal, i):
    bit = jnp.where(i % 2 == 0, scal[1], 1 - scal[1])
    core = jnp.where(i < 2, scal[2], 1 - scal[2])
    return core, bit


def finish_ffn_kernel(scal, *refs):
    groups, (down_ref, up_ref, out_ref) = (refs[:4], refs[4:8]), refs[8:]
    step = pl.program_id(0)
    deep = scal[4]
    half = up_ref.shape[0]
    size = half // 4
    for i in range(4):

        @pl.when(step == i)
        def _(i=i):
            for d in range(4):
                row = pl.multiple_of((deep ^ deep_of(d)) * size, 32)
                for part in range(2):
                    piece = groups[part][i]
                    down_at = pl.multiple_of(part * half + row, 32)
                    down_ref[pl.ds(down_at, size)] = piece[d, :size].astype(F32)
                    up_ref[pl.ds(row, size), part * half : (part + 1) * half] = piece[
                        d, size : 2 * size
                    ].astype(F32)
                row = pl.multiple_of((deep ^ deep_of(d)) * (size // 2), 16)
                out_ref[pl.ds(row, size // 2)] = groups[1][i][d, 2 * size :].astype(F32)


def finish_ffn(scal, first, second):
    half = first[0].shape[2]
    width = 2 * half

    def at(i, s):
        return spot_of(s, i)

    grid_spec = pltpu.PrefetchScalarGridSpec(
        num_scalar_prefetch=1,
        grid=(4,),
        in_specs=[
            pl.BlockSpec(item.shape, lambda i, s: (0, 0, 0)) for item in (*first, *second)
        ],
        out_specs=[
            pl.BlockSpec((width, half), at),
            pl.BlockSpec((half, width), lambda i, s: (0, 2 * at(i, s)[1] + at(i, s)[0])),
            pl.BlockSpec((half // 2, half), at),
        ],
    )
    shape = jax.ShapeDtypeStruct
    return pl.pallas_call(
        finish_ffn_kernel,
        grid_spec=grid_spec,
        out_shape=[
            shape((2 * width, width), F32),
            shape((half, 4 * width), F32),
            shape((half, width), F32),
        ],
        compiler_params=params(),
        cost_estimate=COST,
        name="finish_ffn",
    )(scal, *first, *second)


def finish_proj_kernel(scal, *refs):
    parts, outs = refs[:4], refs[4:]
    step = pl.program_id(0)
    deep = scal[4]
    size = outs[0].shape[0] // 4
    for i in range(4):

        @pl.when(step == i)
        def _(i=i):
            for d in range(4):
                row = pl.multiple_of((deep ^ deep_of(d)) * size, 16)
                for n, out in enumerate(outs):
                    out[pl.ds(row, size)] = parts[i][d, n].astype(F32)


def finish_proj(scal, parts):
    half = parts[0].shape[3]
    spec = pl.BlockSpec((half // 2, half), lambda i, s: spot_of(s, i))
    grid_spec = pltpu.PrefetchScalarGridSpec(
        num_scalar_prefetch=1,
        grid=(4,),
        in_specs=[pl.BlockSpec(item.shape, lambda i, s: (0, 0, 0, 0)) for item in parts],
        out_specs=[spec] * 3,
    )
    return pl.pallas_call(
        finish_proj_kernel,
        grid_spec=grid_spec,
        out_shape=[jax.ShapeDtypeStruct((half, 2 * half), F32)] * 3,
        compiler_params=params(),
        cost_estimate=COST,
        name="finish_proj",
    )(scal, *parts)


def add_low(*terms):
    total = terms[0].astype(F32)
    for term in terms[1:]:
        total = total + term.astype(F32)
    return total.astype(BF16)


def to_span(rows):
    return lax.ppermute(rows, "span", [(0, 1), (1, 0)])


def to_seq(rows, bit):
    size = lax.axis_size("seq")
    return lax.ppermute(rows, "seq", [(i, i ^ bit) for i in range(size)])


def after(value, *others):
    return lax.optimization_barrier((value, *others))[0]


def split_send(parts):
    return add_low(*[part[1] for part in parts]), [part[0] for part in parts]


def rest_links():
    link, links = 16, []
    while link < lax.axis_size("seq"):
        links.append(link)
        link *= 2
    return links


def reduce_rest(rows):
    shape = rows.shape
    rows = rows.reshape(-1, shape[-1])
    seq = lax.axis_index("seq")
    for link in rest_links():
        bit = (seq // link) % 2
        two = rows.reshape(2, -1, shape[-1])
        send = lax.dynamic_index_in_dim(two, 1 - bit, 0, False)
        rows = add_low(lax.dynamic_index_in_dim(two, bit, 0, False), to_seq(send, link))
    for link in rest_links()[::-1]:
        bit = (seq // link) % 2
        got = to_seq(rows, link)
        rows = jnp.concatenate([jnp.where(bit == 0, rows, got), jnp.where(bit == 0, got, rows)])
    return rows.reshape(shape)


class Line:
    def __init__(self):
        self.last = None

    def take(self, value):
        return value if self.last is None else after(value, self.last)

    def put(self, value):
        self.last = value
        return value


def shards(
    tokens,
    out_cotangent,
    crop_offset,
    start_kept,
    norm1_gain,
    norm1_bias,
    w_query,
    b_query,
    w_key,
    b_key,
    w_value,
    b_value,
    w_out,
    b_out,
    norm2_gain,
    norm2_bias,
    w_up,
    b_up,
    w_down,
    b_down,
):
    rows, width = tokens.shape[1], tokens.shape[2]
    half = width // 2
    quarter = half // 4
    seqs = lax.axis_size("seq")
    place = lax.axis_index("span")
    seq = lax.axis_index("seq")
    core = seq % 2
    bit = (seq // 2) % 2
    deep = (seq // 4) % 4
    first = (crop_offset * start_kept)[0, 0]
    scal = jnp.stack([place, bit, core, first, deep]).astype(jnp.int32)
    start = (2 * bit + core) * quarter

    tok = tokens[0]
    dy = out_cotangent[0]

    piece = jnp.stack(
        [
            lax.dynamic_slice_in_dim(w, start, quarter, 0)
            for w in (w_query, w_key, w_value)
        ]
    )
    piece0 = to_span(piece)
    piece1 = to_seq(piece0, 2)
    pieces = (piece0, piece1, to_seq(jnp.stack([piece0, piece1]), 1))
    tok_oth = to_span(tok)

    small = jnp.concatenate(
        [
            jnp.stack(
                [
                    norm1_gain,
                    norm1_bias,
                    b_query,
                    b_key,
                    b_value,
                    norm2_gain,
                    norm2_bias,
                    b_out,
                    b_down,
                ]
            ),
            b_up.reshape(4, half),
        ]
    )
    small_oth = to_span(small)
    small_full = jnp.where(
        place == 0,
        jnp.concatenate([small, small_oth], axis=1),
        jnp.concatenate([small_oth, small], axis=1),
    ).astype(F32)
    vec_one = jnp.pad(small_full[:5], ((0, 3), (0, 0)))
    vec_two = jnp.pad(small_full[5:9], ((0, 4), (0, 0)))
    bup = jnp.concatenate([small_full[9:, :half], small_full[9:, half:]])

    out_piece = lax.dynamic_slice_in_dim(after(w_out, piece0), start, quarter, 0)
    out_piece = out_piece.reshape(quarter, 2, half).transpose(1, 0, 2)
    up_piece = lax.dynamic_slice_in_dim(after(w_up, piece0), start, quarter, 0)
    up_piece = up_piece.reshape(quarter, 4, 2, half).transpose(2, 1, 0, 3)
    down_piece = after(w_down, piece0).reshape(2, 2, 4, quarter, 2, half)
    down_piece = lax.dynamic_index_in_dim(down_piece, 2 * bit + core, 2, False)
    down_piece = down_piece.transpose(1, 0, 3, 2, 4).reshape(2, 4, quarter, half)
    one0 = to_span(jnp.concatenate([up_piece[0], down_piece[0], out_piece]))
    two_piece = jnp.concatenate([up_piece[1], down_piece[1]])

    quarter_dim = HEAD_DIM // 2
    here = jnp.arange(rows, dtype=jnp.int32)
    places = jnp.concatenate([place * rows + here, (1 - place) * rows + here]) - first
    rates = jnp.power(
        jnp.float32(10000.0), -jnp.arange(quarter_dim, dtype=F32) / quarter_dim
    )
    angle = places.astype(F32)[:, None] * jnp.tile(rates, 4)[None, :]
    sign = jnp.tile(jnp.repeat(jnp.array([-1.0, 1.0], F32), quarter_dim), 2)
    cos = jnp.cos(angle)
    sin = jnp.sin(angle) * sign[None, :]

    n1t, query, keys, values, wall = qkv(
        scal, tok, tok_oth, vec_one, cos, sin, (w_query, w_key, w_value), pieces
    )
    one1 = to_seq(after(one0, n1t), 2)
    two0 = to_span(after(two_piece, n1t))
    part = attend(scal, after(query, one0), keys, values, 0)
    mixed, lse = attend(scal, after(query, two0), keys, values, width // 256, part)
    two1 = to_seq(after(two0, mixed), 2)
    one2 = to_seq(jnp.stack([one0, after(one1, mixed)]), 1)
    hidden, normed, acc, dacc, send, keep, gbup_first, wo = ffn_first(
        scal, tok, mixed, dy, vec_two, bup, w_out, w_up, w_down, (one0, one1, one2)
    )
    two1 = after(two1, send)
    two2 = to_seq(jnp.stack([two0, two1]), 1)
    recv = to_seq(after(send, two1), 1)
    split = (2, 2, 2, 2, half // 2, half)
    send_first, first_parts = split_send([keep.reshape(split), recv.reshape(split)])
    got_first = to_seq(send_first, 2)
    layer_out, dh, do, send, keep, gbup_second, small_two = ffn_second(
        scal, mixed, dy, vec_two, bup, after(hidden, send_first), normed, acc, dacc, wo, w_up, w_down,
        (two0, two1, two2),
    )
    recv = to_seq(send, 1)
    split = (2, 2, 2, 2, half // 2 + half // 8, half)
    second_parts = [keep.reshape(split)]

    def back(theirs, dout, begin, pairs, earlier=()):
        return attend_back(
            scal, query, keys, values, mixed, dout, lse, cos, sin, theirs, begin, pairs, earlier
        )

    pairs = width // 256
    back_one = back(1, do, 0, pairs)
    send, keep_one = weight_grads(scal, n1t, back_one)
    recv_one = to_seq(send, 1)
    send_first, first_parts = split_send(first_parts + [after(got_first, send)])
    got_first = to_span(send_first)
    recv = after(recv, send_first).reshape(split)
    send_second, second_parts = split_send(second_parts + [recv])
    got_second = to_span(send_second)
    back_two = back(0, after(do, send_second), 0, pairs - 1)

    split = (2, 2, 2, 3, half // 8, half)
    send_over = add_low(keep_one, after(recv_one, back_two)).reshape(split)
    over_x = to_seq(send_over, 2)
    back_two = back(0, after(do, send_over), pairs - 1, 1, back_two)

    send, keep = weight_grads(scal, n1t, back_two)
    recv = to_seq(send, 1)
    send_first, first_parts = split_send(first_parts + [after(got_first, send)])
    got_first = to_seq(send_first, 4)
    dn_own, dn_oth = norm_grads(scal, after(back_two, send_first), back_one, wall)
    dn_recv = to_span(dn_oth)

    line = Line()
    line.put(dn_oth)
    send_second, second_parts = split_send(second_parts + [line.take(got_second)])
    got_second = to_seq(line.put(send_second), 2)
    proj_parts = [item.reshape(split) for item in (keep, line.take(recv))] + [over_x]
    send_proj, proj_parts = split_send(proj_parts)
    got_proj = to_span(line.put(send_proj))
    send_first, first_parts = split_send(first_parts + [line.take(got_first)])
    got_first = to_seq(line.put(send_first), 8)
    send_proj, proj_parts = split_send(proj_parts + [line.take(got_proj)])
    got_proj = to_seq(line.put(send_proj), 4)
    send_second, second_parts = split_send(second_parts + [line.take(got_second)])
    got_second = to_seq(line.put(send_second), 4)
    first = line.put(reduce_rest(add_low(*first_parts, line.take(got_first))))
    got_first = to_seq(first, 8)
    send_proj, proj_parts = split_send(proj_parts + [line.take(got_proj)])
    got_proj = to_seq(line.put(send_proj), 8)

    input_grad, small_zero = input_grads(tok, dn_own, line.take(dn_recv), dh, vec_one)
    lower = jnp.where(bit == 0, back_two[3][:3], back_one[3][:3])
    upper = jnp.where(bit == 0, back_one[3][:3], back_two[3][:3])
    small_one = jnp.concatenate([lower, upper], axis=1)
    smalls = jnp.concatenate([small_zero[:2], small_one, small_two[:4]])
    gbup = gbup_first + gbup_second
    left = jnp.concatenate([smalls[:, :half], gbup[:4]])
    right = jnp.concatenate([smalls[:, half:], gbup[4:]])
    total = jnp.where(place == 0, left, right)
    got_small = to_span(line.put(jnp.where(place == 0, right, left)))

    send_second, second_parts = split_send(second_parts + [line.take(got_second)])
    got_second = to_seq(line.put(send_second), 8)
    first = line.put(jnp.stack([first, line.take(got_first)]))
    got_first = to_seq(first, 4)
    proj = line.put(reduce_rest(add_low(*proj_parts, line.take(got_proj))))
    got_proj = [to_seq(proj, 8), to_seq(proj, 4), to_seq(proj, 12)]
    total = line.put(total + line.take(got_small))
    got_small = to_seq(total, 1)
    second = line.put(reduce_rest(add_low(*second_parts, line.take(got_second))))
    got_second = to_seq(second, 8)
    total = line.put(total + line.take(got_small))
    got_small = to_seq(total, 2)
    first = line.put(jnp.stack([first, line.take(got_first)]).reshape(4, -1, half))
    first_x, first_core = to_seq(first, 2), to_seq(first, 1)
    total = line.put(total + line.take(got_small))
    got_small = to_seq(total, 4)
    proj = line.put(jnp.stack([proj, line.take(got_proj[0]), *got_proj[1:]]))
    proj_x, proj_core = to_seq(proj, 2), to_seq(proj, 1)
    second = line.put(jnp.stack([second, line.take(got_second)]))
    got_second = to_seq(second, 4)
    total = line.put(total + line.take(got_small))
    got_small = to_seq(total, 8)
    first_x = line.put(line.take(first_x))
    firsts = (first, first_x, first_core, to_seq(first_x, 1))
    second = line.put(jnp.stack([second, line.take(got_second)]).reshape(4, -1, half))
    second_x, second_core = to_seq(second, 2), to_seq(second, 1)
    proj_x = line.put(line.take(proj_x))
    projs = (proj, proj_x, proj_core, to_seq(proj_x, 1))
    total = line.put(total + line.take(got_small))
    for link in rest_links():
        total = total + to_seq(total, link)
    second_x = line.take(second_x)
    seconds = (second, second_x, second_core, to_seq(second_x, 1))
    proj = finish_proj(scal, projs)
    down_grad, up_grad, out_grad = finish_ffn(scal, firsts, seconds)

    return (
        layer_out[None],
        input_grad[None],
        total[0],
        total[1],
        proj[0],
        total[2],
        proj[1],
        total[3],
        proj[2],
        total[4],
        out_grad,
        total[7],
        total[5],
        total[6],
        up_grad,
        total[9:].reshape(-1),
        down_grad,
        total[8],
    )


def solution(mesh):
    row, col = P(None, ("seq", "span"), None), P(None, "seq")
    vec, mat = P("span"), P("span", None)
    weights = (vec, vec, mat, vec, mat, vec, mat, vec, mat, vec, vec, vec, mat, vec, mat, vec)
    return jax.shard_map(
        shards,
        mesh=mesh,
        in_specs=(row, row, col, col) + weights,
        out_specs=(row, row) + weights,
        check_vma=False,
    )
```

```python
import functools

import jax
import jax.numpy as jnp
from jax import lax
from jax.experimental import pallas as pl
from jax.experimental.pallas import tpu as pltpu
from jax.sharding import PartitionSpec as P

HEADS = 12
HEAD_DIM = 64
SCALE = HEAD_DIM ** (-0.5)
F32 = jnp.float32
BF16 = jnp.bfloat16
VMEM_BYTES = 60 * 1024 * 1024
COST = pl.CostEstimate(flops=10**11, bytes_accessed=1024, transcendentals=0)


def deep_of(spot):
    return (spot >> 1) | ((spot & 1) << 1)


def dot(left, right, dim_l, dim_r):
    return lax.dot_general(
        left, right, (((dim_l,), (dim_r,)), ((), ())), preferred_element_type=F32
    )


def swap_halves(rows):
    half = rows.shape[-1] // 2
    return jnp.concatenate([rows[:, half:], rows[:, :half]], axis=1)


def own_first(rows, place):
    return jnp.where(place == 0, rows, swap_halves(rows))


def half_swap(tile):
    lane = lax.broadcasted_iota(jnp.int32, tile.shape, 1)
    width = tile.shape[1]
    return jnp.where(
        lane % HEAD_DIM < HEAD_DIM // 2,
        pltpu.roll(tile, width - HEAD_DIM // 2, 1),
        pltpu.roll(tile, HEAD_DIM // 2, 1),
    )


def params(**kw):
    return pltpu.CompilerParams(vmem_limit_bytes=VMEM_BYTES, **kw)


def vmem():
    return pl.BlockSpec(memory_space=pltpu.VMEM)


def anywhere():
    return pl.BlockSpec(memory_space=pl.ANY)


def qkv_kernel(
    scal, own_ref, oth_ref, vec_ref, cos_ref, sin_ref, wq, wk, wv, p0, p1, p2, p3,
    n1t_ref, q_ref, k_ref, v_ref, wall_ref, sems,
):
    step = pl.program_id(0)
    place = scal[0]
    half = wq.shape[0]

    @pl.when(step == 0)
    def _():
        copies = []
        for j, weight in enumerate((wq, wk, wv)):
            target = wall_ref.at[j]
            own = (weight, target.at[pl.ds(0, half)])
            copies += piece_copies(
                own, (p0, p1, p2, p3), scal, lambda p, j=j: p.at[j], target, half
            )
        wait_all(start_all(copies, sems, 0))

    rows = jnp.where(step < 2, own_ref[...], oth_ref[...]).astype(F32)
    center = rows - jnp.mean(rows, axis=1, keepdims=True)
    spread = jnp.mean(center * center, axis=1, keepdims=True)
    normed = center * lax.rsqrt(spread + 1e-05) * vec_ref[0:1] + vec_ref[1:2]
    normed = own_first(normed, place).astype(BF16)
    n1t_ref[...] = normed.T

    def rotated(j, ref, factor):
        flat = dot(normed, wall_ref[j], 1, 0) + vec_ref[2 + j : 3 + j]
        for t in range(flat.shape[1] // 128):
            tile = flat[:, t * 128 : (t + 1) * 128]
            turned = (tile * cos_ref[...] + half_swap(tile) * sin_ref[...]).astype(BF16)
            ref[:, t * 128 : (t + 1) * 128] = turned * factor if factor != 1 else turned

    @pl.when(step < 2)
    def _():
        rotated(0, q_ref, SCALE)

    rotated(1, k_ref, 1)
    v_ref[...] = (dot(normed, wall_ref[2], 1, 0) + vec_ref[4:5]).astype(BF16)


def qkv(scal, own, oth, vec, cos, sin, weights, pieces):
    rows, width = own.shape
    block = rows // 2
    grid_spec = pltpu.PrefetchScalarGridSpec(
        num_scalar_prefetch=1,
        grid=(4,),
        in_specs=[
            pl.BlockSpec((block, width), lambda i, s: (jnp.minimum(i, 1), 0)),
            pl.BlockSpec((block, width), lambda i, s: (jnp.maximum(i - 2, 0), 0)),
            pl.BlockSpec(vec.shape, lambda i, s: (0, 0)),
            pl.BlockSpec((block, 128), lambda i, s: (i, 0)),
            pl.BlockSpec((block, 128), lambda i, s: (i, 0)),
        ]
        + [anywhere()] * 7,
        out_specs=[
            pl.BlockSpec((width, block), lambda i, s: (0, i)),
            pl.BlockSpec((block, width), lambda i, s: (jnp.minimum(i, 1), 0)),
            pl.BlockSpec((block, width), lambda i, s: (i, 0)),
            pl.BlockSpec((block, width), lambda i, s: (i, 0)),
            pl.BlockSpec((3, width, width), lambda i, s: (0, 0, 0)),
        ],
        scratch_shapes=[pltpu.SemaphoreType.DMA((15,))],
    )
    shape = jax.ShapeDtypeStruct
    return pl.pallas_call(
        qkv_kernel,
        grid_spec=grid_spec,
        out_shape=[
            shape((width, 2 * rows), BF16),
            shape((rows, width), BF16),
            shape((2 * rows, width), BF16),
            shape((2 * rows, width), BF16),
            shape((3, width, width), BF16),
        ],
        compiler_params=params(),
        cost_estimate=COST,
        name="qkv",
    )(scal, own, oth, vec, cos, sin, *weights, *pieces)


def key_bias(scal, keys):
    place, first = scal[0], scal[3]
    half = keys // 2
    row = lax.broadcasted_iota(jnp.int32, (keys, 128), 0)
    where = jnp.where(row < half, place * half + row, (1 - place) * half + row - half)
    return jnp.where(where < first, -1e30, 0.0).astype(BF16)


def masked_pair(head, keys, query, bias):
    lane_k = lax.broadcasted_iota(jnp.int32, keys.shape, 1)
    lane_q = lax.broadcasted_iota(jnp.int32, query.shape, 1)
    spot = (1 - head) * HEAD_DIM
    zero = jnp.zeros((), BF16)
    keys = jnp.where(
        lane_k // HEAD_DIM == head, keys, jnp.where(lane_k == spot, bias, zero)
    )
    query = jnp.where(
        lane_q // HEAD_DIM == head,
        query,
        jnp.where(lane_q == spot, jnp.ones((), BF16), zero),
    )
    return keys, query


def attend_kernel(scal, q_ref, k_ref, v_ref, *refs):
    o_ref, lse_ref = refs[-2:]
    keys, values, query = k_ref[...], v_ref[...], q_ref[...]
    bias = key_bias(scal, keys.shape[0])
    values_t = values.T
    outs = []
    for head in range(2):
        keys_m, query_m = masked_pair(head, keys, query, bias)
        scores = dot(keys_m, query_m, 1, 1)
        top = jnp.max(scores, axis=0, keepdims=True)
        expo = jnp.exp(scores - top)
        total = jnp.sum(expo, axis=0, keepdims=True)
        mixed = dot(
            values_t[head * HEAD_DIM : (head + 1) * HEAD_DIM], expo.astype(BF16), 1, 0
        )
        outs.append(mixed / total)
        lse_ref[0, head : head + 1] = top + jnp.log(total)
    o_ref[...] = jnp.concatenate(outs, axis=0).T.astype(BF16)


def attend(scal, query, keys, values, begin, earlier=()):
    rows, width = query.shape
    span = keys.shape[0]
    pairs = width // 256
    grid_spec = pltpu.PrefetchScalarGridSpec(
        num_scalar_prefetch=1,
        grid=(pairs,),
        in_specs=[
            pl.BlockSpec((rows, 128), lambda i, s: (0, i + begin)),
            pl.BlockSpec((span, 128), lambda i, s: (0, i + begin)),
            pl.BlockSpec((span, 128), lambda i, s: (0, i + begin)),
        ]
        + [anywhere()] * len(earlier),
        out_specs=[
            pl.BlockSpec((rows, 128), lambda i, s: (0, i + begin)),
            pl.BlockSpec((1, 8, rows), lambda i, s: (i + begin, 0, 0)),
        ],
    )
    return pl.pallas_call(
        attend_kernel,
        grid_spec=grid_spec,
        out_shape=[
            jax.ShapeDtypeStruct((rows, width), BF16),
            jax.ShapeDtypeStruct((2 * pairs, 8, rows), F32),
        ],
        input_output_aliases={4: 0, 5: 1} if earlier else {},
        compiler_params=params(),
        cost_estimate=COST,
        name="attend",
    )(scal, query, keys, values, *earlier)


def attend_back_kernel(
    scal, q_ref, k_ref, v_ref, o_ref, do_ref, lse_ref, cos_ref, sin_ref, n1t_ref,
    dq_ref, dk_ref, dv_ref, bias_ref, send_ref, keep_ref, g_s,
):
    step = pl.program_id(0)
    pairs = dq_ref.shape[1] // 128

    @pl.when(step < pairs)
    def _():
        at = pl.ds(pl.multiple_of(step * 128, 128), 128)
        keys, values, query, dout = k_ref[...], v_ref[...], q_ref[...], do_ref[...]
        rows = query.shape[0]
        bias = key_bias(scal, keys.shape[0])
        keys_t = keys.T
        product = (dout.astype(F32) * o_ref[...].astype(F32)).T
        lane = lax.broadcasted_iota(jnp.int32, values.shape, 1)
        parts = []
        for head in range(2):
            keys_m, query_m = masked_pair(head, keys, query, bias)
            values_m = jnp.where(lane // HEAD_DIM == head, values, jnp.zeros((), BF16))
            inner = jnp.sum(
                product[head * HEAD_DIM : (head + 1) * HEAD_DIM], axis=0, keepdims=True
            )
            probs = jnp.exp(dot(keys_m, query_m, 1, 1) - lse_ref[0, head : head + 1])
            grad = dot(values_m, dout, 1, 1)
            score_grad = (probs * (grad - inner)).astype(BF16)
            dv = dot(probs.astype(BF16), dout, 1, 0)
            dk = dot(score_grad, query, 1, 0)
            dq = dot(keys_t[head * HEAD_DIM : (head + 1) * HEAD_DIM], score_grad, 1, 0)
            parts.append((dq, dk, dv))
        dq = (jnp.concatenate([parts[0][0], parts[1][0]], axis=0).T * SCALE).astype(BF16)
        dk = jnp.where(lane // HEAD_DIM == 0, parts[0][1], parts[1][1]).astype(BF16)
        dv = jnp.where(lane // HEAD_DIM == 0, parts[0][2], parts[1][2]).astype(BF16)
        dq, dk = dq.astype(F32), dk.astype(F32)
        dq = (dq * cos_ref[:rows] - half_swap(dq) * sin_ref[:rows]).astype(BF16)
        dk = (dk * cos_ref[...] - half_swap(dk) * sin_ref[...]).astype(BF16)
        dq_ref[:, at] = dq
        dk_ref[:, at] = dk
        dv_ref[:, at] = dv
        bias_ref[0:1, at] = jnp.sum(dq.astype(F32), axis=0, keepdims=True)
        bias_ref[1:2, at] = jnp.sum(dk.astype(F32), axis=0, keepdims=True)
        bias_ref[2:3, at] = jnp.sum(dv.astype(F32), axis=0, keepdims=True)

    @pl.when(step == pairs)
    def _():
        core, deep = scal[2], scal[4]
        half = dq_ref.shape[1]
        size = half // 8
        for w, ref in enumerate((dq_ref, dk_ref, dv_ref)):
            g_s[w] = dot(n1t_ref[:, : ref.shape[0]], ref[...], 1, 0).astype(BF16)
        for w in range(3):
            for s in range(2):
                for d in range(4):
                    row = s * half + (deep ^ deep_of(d)) * size
                    for out, mine in ((send_ref, 1 - core), (keep_ref, core)):
                        at = pl.multiple_of(row + mine * 4 * size, 16)
                        out[s, d, w] = g_s[w, pl.ds(at, size)]


def attend_back(scal, query, keys, values, mixed, dout, lse, cos, sin, n1t, theirs):
    rows, width = query.shape[0], query.shape[1] // 2
    span = keys.shape[0]
    pairs = width // 128

    def at(i, s):
        return jnp.minimum(i, pairs - 1) + pairs * (1 - s[1] if theirs else s[1])

    def fixed(shape):
        return pl.BlockSpec(shape, lambda i, s: tuple(0 for _ in shape))

    few = pl.BlockSpec((rows, 128), lambda i, s: (0, at(i, s)))
    many = pl.BlockSpec((span, 128), lambda i, s: (0, at(i, s)))
    buffer = (2, 4, 3, width // 8, width)
    outs = [(rows, width), (span, width), (span, width), (8, width), buffer, buffer]
    grid_spec = pltpu.PrefetchScalarGridSpec(
        num_scalar_prefetch=1,
        grid=(pairs + 1,),
        in_specs=[few, many, many, few, few]
        + [pl.BlockSpec((1, 8, rows), lambda i, s: (at(i, s), 0, 0))]
        + [fixed((span, 128)), fixed((span, 128)), fixed(n1t.shape)],
        out_specs=[fixed(item) for item in outs],
        scratch_shapes=[pltpu.VMEM((3, 2 * width, width), BF16)],
    )
    return pl.pallas_call(
        attend_back_kernel,
        grid_spec=grid_spec,
        out_shape=[
            jax.ShapeDtypeStruct(item, F32 if n == 3 else BF16) for n, item in enumerate(outs)
        ],
        compiler_params=params(),
        cost_estimate=COST,
        name="attend_back",
    )(scal, query, keys, values, mixed, dout, lse, cos, sin, n1t)


def norm_stats(rows):
    center = rows - jnp.mean(rows, axis=1, keepdims=True)
    spread = jnp.mean(center * center, axis=1, keepdims=True)
    return center, lax.rsqrt(spread + 1e-05)


def norm_back(rows, grad, gain):
    center, rate = norm_stats(rows)
    hat = center * rate
    scaled = grad * gain
    out = rate * (
        scaled
        - jnp.mean(scaled, axis=1, keepdims=True)
        - hat * jnp.mean(scaled * hat, axis=1, keepdims=True)
    )
    return (
        out,
        jnp.sum(grad * hat, axis=0, keepdims=True),
        jnp.sum(grad, axis=0, keepdims=True),
    )


def piece_copies(own, pieces, scal, select, target, base):
    bit, core = scal[1], scal[2]
    p0, p1, p2, p3 = pieces
    spots = (
        (p0, 2 * bit + core),
        (p1, 2 * (1 - bit) + core),
        (p2, 2 * bit + 1 - core),
        (p3, 2 * (1 - bit) + 1 - core),
    )
    copies = [] if own is None else [own]
    for src, index in spots:
        part = select(src)
        rows = part.shape[0]
        start = pl.multiple_of(base + index * rows, 32)
        copies.append((part, target.at[pl.ds(start, rows)]))
    return copies


def load_out(scal, wo_own, pieces, wo_s):
    half = wo_own.shape[0]
    own = (wo_own, wo_s.at[pl.ds(0, half)])
    return piece_copies(own, pieces, scal, lambda p: p, wo_s, half)


def load_chunk(scal, part, t, up_own, down_own, ups, downs, chunk, up_s, down_s):
    place = scal[0]
    core = scal[2] if t == 1 else 1 - scal[2]
    half = up_own.shape[0]
    copies = []
    for n, span in enumerate((1 - place, place)):
        index = 2 * span + core
        column = pl.multiple_of((2 * index + part) * half, 128)
        target = up_s.at[chunk, :, pl.ds(n * half, half)]
        own = (up_own.at[:, pl.ds(column, half)], target.at[pl.ds(0, half)])
        copies += piece_copies(own, ups, scal, lambda p, index=index: p.at[index], target, half)
    start = pl.multiple_of((2 * core + part) * half, 128)
    copies.append((down_own.at[pl.ds(start, half)], down_s.at[chunk, pl.ds(half, half)]))
    copies += piece_copies(None, downs, scal, lambda p: p.at[core], down_s.at[chunk], 0)
    return copies


def start_all(copies, sems, base):
    started = [
        pltpu.make_async_copy(src, dst, sems.at[base + n]) for n, (src, dst) in enumerate(copies)
    ]
    for copy in started:
        copy.start()
    return started


def wait_all(started):
    for copy in started:
        copy.wait()


def chunk_spots(scal, t, part):
    place = scal[0]
    core = scal[2] if t == 1 else 1 - scal[2]
    return [2 * (2 * span + core) + part for span in (1 - place, place)]


def ffn_products(n, chunk, dy_ref, n2_ref, up_s, down_s, u_s, da_s):
    u_s[n] = dot(n2_ref[...], up_s[chunk], 1, 0)
    da_s[n] = dot(dy_ref[...], down_s[chunk], 1, 1)


def ffn_elements(scal, n, t, part, bup_ref, u_s, da_s, a_s, du_s, gbup_ref):
    rows, width = a_s.shape[1:]
    half = width // 2
    block = rows // 8
    spots = chunk_spots(scal, t, part)
    bias = jnp.concatenate([bup_ref[pl.ds(n, 1)] for n in spots], axis=1)
    total = jnp.zeros((8, width), F32)
    for r in range(0, rows, block):
        at = slice(r, r + block)
        inner = u_s[n, at] + bias
        phi = 0.5 + 0.5 * lax.erf(inner * 0.7071067811865476)
        slope = phi + inner * (0.3989422804014327 * jnp.exp(-0.5 * inner * inner))
        a_s[n, at] = (inner * phi).astype(BF16)
        du = (da_s[n, at] * slope).astype(BF16)
        du_s[n, at] = du
        total = total + jnp.sum(du.astype(F32).reshape(block // 8, 8, width), axis=0)
    total = jnp.sum(total, axis=0, keepdims=True)
    for n, row in enumerate(spots):
        gbup_ref[pl.ds(row, 1)] = total[:, n * half : (n + 1) * half]


def ffn_grads(
    scal, n, chunk, part, dy_ref, n2t_ref, up_s, down_s, acc_s, dacc_s, a_s, du_s, down_out, up_out, g_s
):
    acc_s[...] += dot(a_s[n], down_s[chunk], 1, 0)
    dacc_s[...] += dot(du_s[n], up_s[chunk], 1, 1)
    place, bit, deep = scal[0], scal[1], scal[4]
    half = g_s.shape[1] // 2
    size = half // 4
    g_s[0] = dot(a_s[n], dy_ref[...], 0, 0).astype(BF16)
    g_s[1] = dot(n2t_ref[...], du_s[n], 1, 0).astype(BF16)
    rows = slice(part * size, (part + 1) * size)
    for s in range(2):
        for k in range(2):
            column = bit if k == 0 else 1 - bit
            down_at = pl.multiple_of(column * half, 128)
            up_at = pl.multiple_of(jnp.where(column == place, half, 0), 128)
            for d in range(4):
                row = (deep ^ deep_of(d)) * size
                down_row = pl.multiple_of((1 - s) * half + row, 32)
                up_row = pl.multiple_of(s * half + row, 32)
                down_out[k, s, d, rows] = g_s[0, pl.ds(down_row, size), pl.ds(down_at, half)]
                up_out[s, k, d, rows] = g_s[1, pl.ds(up_row, size), pl.ds(up_at, half)]


def hidden_kernel(
    scal, x_ref, o_ref, vec_ref, wo_own, p0, p1, p2, p3, h_ref, n2_ref, n2t_ref, wo_s, sems
):
    place = scal[0]
    rows = x_ref.shape[0]
    block = rows // 8
    wait_all(start_all(load_out(scal, wo_own, (p0, p1, p2, p3), wo_s), sems, 0))
    h_ref[...] = dot(own_first(o_ref[...], place), wo_s[...], 1, 0)
    for r in range(0, rows, block):
        at = slice(r, r + block)
        hidden = h_ref[at] + (x_ref[at].astype(F32) + vec_ref[2:3])
        h_ref[at] = hidden
        center, rate = norm_stats(hidden)
        normed = center * rate * vec_ref[0:1] + vec_ref[1:2]
        n2_ref[at] = own_first(normed, place).astype(BF16)
    n2t_ref[...] = n2_ref[...].T


def hidden_rows(scal, tokens, mixed, vec, w_out, pieces):
    rows, width = tokens.shape
    shape = jax.ShapeDtypeStruct
    return pl.pallas_call(
        hidden_kernel,
        in_specs=[pl.BlockSpec(memory_space=pltpu.SMEM)] + [vmem()] * 3 + [anywhere()] * 5,
        out_specs=[vmem()] * 4,
        out_shape=[
            shape((rows, width), F32),
            shape((rows, width), BF16),
            shape((width, rows), BF16),
            shape((width, width), BF16),
        ],
        scratch_shapes=[pltpu.SemaphoreType.DMA((5,))],
        compiler_params=params(),
        cost_estimate=COST,
        name="hidden_rows",
    )(scal, tokens, mixed, vec, w_out, *pieces)


def ffn_kernel(
    scal, o_ref, dy_ref, vec_ref, bup_ref, h_ref, n2_ref, n2t_ref, up_own, down_own, *refs
):
    pieces, refs = refs[:16], refs[16:]
    (
        out_ref, dh_ref, branch_ref, sdown_ref, sup_ref, kdown_ref, kup_ref, gbup_ref, small_ref,
        u_s, da_s, a_s, du_s, up_s, down_s, g_s, acc_s, dacc_s, go_s, sems,
    ) = refs
    place, bit, core, deep = scal[0], scal[1], scal[2], scal[4]
    rows, width = dy_ref.shape
    half = width // 2
    block = rows // 8
    order = [(part, t) for t in range(2) for part in range(2)]
    waits = []
    for chunk, (part, t) in enumerate(order):
        ups, downs = pieces[4 * part : 4 * part + 4], pieces[8 + 4 * part : 12 + 4 * part]
        copies = load_chunk(
            scal, part, t, up_own, down_own, ups, downs, chunk, up_s, down_s
        )
        waits.append(start_all(copies, sems, 15 * chunk))
    acc_s[...] = h_ref[...] + vec_ref[3:4]
    dacc_s[...] = jnp.zeros_like(dacc_s)
    wait_all(waits[0])
    ffn_products(0, 0, dy_ref, n2_ref, up_s, down_s, u_s, da_s)
    for chunk, (part, t) in enumerate(order):
        n = chunk % 2
        if chunk + 1 < len(order):
            wait_all(waits[chunk + 1])
            ffn_products(1 - n, chunk + 1, dy_ref, n2_ref, up_s, down_s, u_s, da_s)
        ffn_elements(scal, n, t, part, bup_ref, u_s, da_s, a_s, du_s, gbup_ref)
        down_out, up_out = (kdown_ref, kup_ref) if t == 1 else (sdown_ref, sup_ref)
        ffn_grads(
            scal, n, chunk, part, dy_ref, n2t_ref, up_s, down_s, acc_s, dacc_s, a_s, du_s,
            down_out, up_out, g_s,
        )
    sums = [jnp.zeros((1, width), F32) for _ in range(4)]
    for r in range(0, rows, block):
        at = slice(r, r + block)
        out_ref[at] = acc_s[at].astype(BF16)
        grad = own_first(dacc_s[at], place)
        dy = dy_ref[at].astype(F32)
        part, gain_sum, shift_sum = norm_back(h_ref[at], grad, vec_ref[0:1])
        dh = dy + part
        dh_ref[at] = dh
        branch = dh.astype(BF16)
        branch_ref[at] = branch
        terms = (
            gain_sum,
            shift_sum,
            jnp.sum(branch.astype(F32), axis=0, keepdims=True),
            jnp.sum(dy, axis=0, keepdims=True),
        )
        sums = [old + new for old, new in zip(sums, terms)]
    for n, item in enumerate(sums):
        small_ref[n : n + 1] = item
    go_s[...] = dot(own_first(o_ref[...], place), branch_ref[...], 0, 0)
    size = half // 8
    for s in range(2):
        for k in range(2):
            column = pl.multiple_of((bit if k == 0 else 1 - bit) * half, 128)
            for d in range(4):
                row = s * half + (deep ^ deep_of(d)) * size
                for out, mine in ((sdown_ref, 1 - core), (kdown_ref, core)):
                    at = pl.multiple_of(row + mine * 4 * size, 16)
                    out[k, s, d, 4 * size :] = go_s[pl.ds(at, size), pl.ds(column, half)].astype(BF16)


def ffn(scal, mixed, dy, vec, bup, hidden, normed, normed_t, w_up, w_down, pieces):
    rows, width = mixed.shape
    half = width // 2
    shape = jax.ShapeDtypeStruct
    down = shape((2, 2, 4, half // 2 + half // 8, half), BF16)
    up = shape((2, 2, 4, half // 2, half), BF16)
    return pl.pallas_call(
        ffn_kernel,
        in_specs=[pl.BlockSpec(memory_space=pltpu.SMEM)] + [vmem()] * 7 + [anywhere()] * 18,
        out_specs=[vmem()] * 9,
        out_shape=[
            shape((rows, width), BF16),
            shape((rows, width), F32),
            shape((rows, width), BF16),
            down,
            up,
            down,
            up,
            shape((8, half), F32),
            shape((8, width), F32),
        ],
        scratch_shapes=[
            pltpu.VMEM((2, rows, width), F32),
            pltpu.VMEM((2, rows, width), F32),
            pltpu.VMEM((2, rows, width), BF16),
            pltpu.VMEM((2, rows, width), BF16),
            pltpu.VMEM((4, width, width), BF16),
            pltpu.VMEM((4, width, width), BF16),
            pltpu.VMEM((2, width, width), BF16),
            pltpu.VMEM((rows, width), F32),
            pltpu.VMEM((rows, width), F32),
            pltpu.VMEM((width, width), F32),
            pltpu.SemaphoreType.DMA((60,)),
        ],
        compiler_params=params(),
        cost_estimate=COST,
        name="ffn",
    )(scal, mixed, dy, vec, bup, hidden, normed, normed_t, w_up, w_down, *pieces)


def out_back_kernel(scal, branch_ref, wo_ref, do_ref):
    do_ref[...] = own_first(dot(branch_ref[...], wo_ref[...], 1, 1), scal[0]).astype(BF16)


def out_back(scal, branch, wo):
    return pl.pallas_call(
        out_back_kernel,
        in_specs=[pl.BlockSpec(memory_space=pltpu.SMEM), vmem(), vmem()],
        out_specs=vmem(),
        out_shape=jax.ShapeDtypeStruct(branch.shape, BF16),
        compiler_params=params(),
        cost_estimate=COST,
        name="out_back",
    )(scal, branch, wo)


def columns_of(scal, theirs, half):
    return pl.ds(pl.multiple_of((1 - scal[1] if theirs else scal[1]) * half, 128), half)


def norm_products(scal, w_ref, parts, first):
    total = 0.0
    for theirs in range(2):
        for n, ref in enumerate(parts[theirs]):
            at = columns_of(scal, theirs, ref.shape[1])
            total = total + dot(ref[...], w_ref[first + n, :, at], 1, 1)
    return own_first(total, scal[0])


def norm_sums(x_ref, grad):
    block = grad.shape[0] // 4
    gain, shift = 0.0, 0.0
    for r in range(0, grad.shape[0], block):
        center, rate = norm_stats(x_ref[r : r + block].astype(F32))
        part = grad[r : r + block]
        gain = gain + jnp.sum(part * (center * rate), axis=0, keepdims=True)
        shift = shift + jnp.sum(part, axis=0, keepdims=True)
    return gain, shift


def fixed_spec(shape):
    return pl.BlockSpec(shape, lambda i, s: tuple(0 for _ in shape))


def other_kernel(scal, w_ref, dk_ref, dv_ref, *refs):
    theirs = len(refs) == 1
    at = columns_of(scal, theirs, dk_ref.shape[1])
    total = dot(dk_ref[...], w_ref[1, :, at], 1, 1) + dot(dv_ref[...], w_ref[2, :, at], 1, 1)
    if theirs:
        refs[0][...] = total
    else:
        earlier_ref, x_ref, out_ref, sum_ref = refs
        grad = own_first(total + earlier_ref[...], scal[0])
        out_ref[...] = grad.astype(BF16)
        gain, shift = norm_sums(x_ref, grad)
        sum_ref[0:1] = gain
        sum_ref[1:2] = shift


def other_rows(scal, wall, back, *rest):
    width = wall.shape[2]
    rows = back[1].shape[0] // 2
    part = pl.BlockSpec((rows, width // 2), lambda i, s: (1, 0))
    shapes = [((rows, width), BF16), ((8, width), F32)] if rest else [((rows, width), F32)]
    return pl.pallas_call(
        other_kernel,
        grid_spec=pltpu.PrefetchScalarGridSpec(
            num_scalar_prefetch=1,
            grid=(1,),
            in_specs=[fixed_spec(wall.shape), part, part] + [fixed_spec(item.shape) for item in rest],
            out_specs=[fixed_spec(item) for item, _ in shapes],
        ),
        out_shape=[jax.ShapeDtypeStruct(*item) for item in shapes],
        compiler_params=params(),
        cost_estimate=COST,
        name="other_rows",
    )(scal, wall, back[1], back[2], *rest)


def own_kernel(
    scal, w_ref, q1, k1, v1, q0, k0, v0, x_ref, other_sum, bias_one, bias_two, two_ref, bup_ref,
    out_ref, small_ref, send_ref,
):
    place, bit = scal[0], scal[1]
    half = x_ref.shape[1] // 2
    grad = norm_products(scal, w_ref, ((q1, k1, v1), (q0, k0, v0)), 0)
    out_ref[...] = grad
    gain, shift = norm_sums(x_ref, grad)
    ends = jnp.concatenate([gain, shift], axis=0) + other_sum[0:2]
    blank = jnp.zeros((3, half), F32)
    sides = []
    for n in range(2):
        at = slice(n * half, (n + 1) * half)
        same = bias_two[0:3] if n == 0 else bias_one[0:3]
        swap = bias_one[0:3] if n == 0 else bias_two[0:3]
        bias = jnp.where(bit == 0, same, swap)
        sides.append(
            jnp.concatenate(
                [ends[:, at], bias, two_ref[0:4, at], bup_ref[4 * n : 4 * n + 4], blank], axis=0
            )
        )
    small_ref[...] = jnp.where(place == 0, sides[0], sides[1])
    send_ref[...] = jnp.where(place == 0, sides[1], sides[0])


def own_rows(scal, wall, mine, theirs, *rest):
    rows, width = rest[0].shape
    part = fixed_spec((rows, width // 2))
    shapes = [(rows, width), (16, width // 2), (16, width // 2)]
    return pl.pallas_call(
        own_kernel,
        grid_spec=pltpu.PrefetchScalarGridSpec(
            num_scalar_prefetch=1,
            grid=(1,),
            in_specs=[fixed_spec(wall.shape)] + [part] * 6 + [fixed_spec(item.shape) for item in rest],
            out_specs=[fixed_spec(item) for item in shapes],
        ),
        out_shape=[jax.ShapeDtypeStruct(item, F32) for item in shapes],
        compiler_params=params(),
        cost_estimate=COST,
        name="own_rows",
    )(scal, wall, *mine[:3], *theirs[:3], *rest)


def input_kernel(x_ref, own_ref, recv_ref, dh_ref, vec_ref, out_ref):
    grad = own_ref[...] + recv_ref[...].astype(F32)
    part, _, _ = norm_back(x_ref[...].astype(F32), grad, vec_ref[0:1])
    out_ref[...] = (dh_ref[...] + part).astype(BF16)


def input_grads(tokens, dn_own, dn_recv, dh, vec):
    rows, width = tokens.shape
    tile = pl.BlockSpec((rows // 4, width), lambda i: (i, 0))
    return pl.pallas_call(
        input_kernel,
        grid=(4,),
        in_specs=[tile, tile, tile, tile, pl.BlockSpec(vec.shape, lambda i: (0, 0))],
        out_specs=tile,
        out_shape=jax.ShapeDtypeStruct((rows, width), BF16),
        compiler_params=params(),
        cost_estimate=COST,
        name="input_grads",
    )(tokens, dn_own, dn_recv, dh, vec)


def spot_of(scal, i):
    bit = jnp.where(i % 2 == 0, scal[1], 1 - scal[1])
    core = jnp.where(i < 2, scal[2], 1 - scal[2])
    return core, bit


def finish_down_kernel(scal, *refs):
    parts, (down_ref, out_ref) = refs[:4], refs[4:]
    step = pl.program_id(0)
    deep = scal[4]
    half = down_ref.shape[1]
    size = half // 4
    count = 2 * size + size // 2
    for i in range(4):

        @pl.when(step == i)
        def _(i=i):
            for d in range(4):
                start = d * count
                for part in range(2):
                    row = pl.multiple_of(part * half + (deep ^ deep_of(d)) * size, 32)
                    at = start + part * size
                    down_ref[pl.ds(row, size)] = parts[i][at : at + size].astype(F32)
                row = pl.multiple_of((deep ^ deep_of(d)) * (size // 2), 16)
                at = start + 2 * size
                out_ref[pl.ds(row, size // 2)] = parts[i][at : at + size // 2].astype(F32)


def finish_up_kernel(scal, *refs):
    parts, up_ref = refs[:4], refs[4]
    step = pl.program_id(0)
    deep = scal[4]
    half = up_ref.shape[0]
    size = half // 4
    for i in range(4):

        @pl.when(step == i)
        def _(i=i):
            for d in range(4):
                row = pl.multiple_of((deep ^ deep_of(d)) * size, 32)
                for part in range(2):
                    at = (2 * d + part) * size
                    up_ref[pl.ds(row, size), part * half : (part + 1) * half] = parts[i][
                        at : at + size
                    ].astype(F32)


def finish_call(body, scal, parts, out_specs, out_shape, name):
    return pl.pallas_call(
        body,
        grid_spec=pltpu.PrefetchScalarGridSpec(
            num_scalar_prefetch=1,
            grid=(4,),
            in_specs=[pl.BlockSpec(item.shape, lambda i, s: (0, 0)) for item in parts],
            out_specs=out_specs,
        ),
        out_shape=[jax.ShapeDtypeStruct(item, F32) for item in out_shape],
        compiler_params=params(),
        cost_estimate=COST,
        name=name,
    )(scal, *parts)


def finish_down(scal, parts):
    half = parts[0].shape[1]
    specs = [pl.BlockSpec((count, half), lambda i, s: spot_of(s, i)) for count in (2 * half, half // 2)]
    shapes = [(4 * half, 2 * half), (half, 2 * half)]
    return finish_call(finish_down_kernel, scal, parts, specs, shapes, "finish_down")


def finish_up(scal, parts):
    half = parts[0].shape[1]

    def at(i, s):
        core, bit = spot_of(s, i)
        return (0, 2 * bit + core)

    specs = [pl.BlockSpec((half, 2 * half), at)]
    return finish_call(finish_up_kernel, scal, parts, specs, [(half, 8 * half)], "finish_up")[0]


def finish_proj_kernel(scal, *refs):
    parts, outs = refs[:4], refs[4:]
    step = pl.program_id(0)
    deep = scal[4]
    size = outs[0].shape[0] // 4
    for i in range(4):

        @pl.when(step == i)
        def _(i=i):
            for d in range(4):
                row = pl.multiple_of((deep ^ deep_of(d)) * size, 16)
                for n, out in enumerate(outs):
                    out[pl.ds(row, size)] = parts[i][d, n].astype(F32)


def finish_proj(scal, parts):
    half = parts[0].shape[3]
    spec = pl.BlockSpec((half // 2, half), lambda i, s: spot_of(s, i))
    grid_spec = pltpu.PrefetchScalarGridSpec(
        num_scalar_prefetch=1,
        grid=(4,),
        in_specs=[pl.BlockSpec(item.shape, lambda i, s: (0, 0, 0, 0)) for item in parts],
        out_specs=[spec] * 3,
    )
    return pl.pallas_call(
        finish_proj_kernel,
        grid_spec=grid_spec,
        out_shape=[jax.ShapeDtypeStruct((half, 2 * half), F32)] * 3,
        compiler_params=params(),
        cost_estimate=COST,
        name="finish_proj",
    )(scal, *parts)


def add_low(*terms):
    total = terms[0].astype(F32)
    for term in terms[1:]:
        total = total + term.astype(F32)
    return total.astype(BF16)


def to_span(rows):
    return lax.ppermute(rows, "span", [(0, 1), (1, 0)])


def to_seq(rows, bit):
    size = lax.axis_size("seq")
    return lax.ppermute(rows, "seq", [(i, i ^ bit) for i in range(size)])


def after(value, *others):
    return lax.optimization_barrier((value, *others))[0]


def split_send(parts):
    return add_low(*[part[1] for part in parts]), [part[0] for part in parts]


def high_low(total):
    low = total - lax.reduce_precision(total, 8, 7)
    return jnp.concatenate([total.astype(BF16), low.astype(BF16)])


def sum_of(rows):
    half = rows.shape[0] // 2
    return rows[:half].astype(F32) + rows[half:].astype(F32)


def rest_links():
    link, links = 16, []
    while link < lax.axis_size("seq"):
        links.append(link)
        link *= 2
    return links


def reduce_rest(rows):
    shape = rows.shape
    rows = rows.reshape(-1, shape[-1])
    seq = lax.axis_index("seq")
    for link in rest_links():
        bit = (seq // link) % 2
        two = rows.reshape(2, -1, shape[-1])
        send = lax.dynamic_index_in_dim(two, 1 - bit, 0, False)
        rows = add_low(lax.dynamic_index_in_dim(two, bit, 0, False), to_seq(send, link))
    for link in rest_links()[::-1]:
        bit = (seq // link) % 2
        got = to_seq(rows, link)
        rows = jnp.concatenate([jnp.where(bit == 0, rows, got), jnp.where(bit == 0, got, rows)])
    return rows.reshape(shape)


class Line:
    def __init__(self):
        self.last = None

    def take(self, value):
        return value if self.last is None else after(value, self.last)

    def put(self, value):
        self.last = value
        return value


def shards(
    tokens,
    out_cotangent,
    crop_offset,
    start_kept,
    norm1_gain,
    norm1_bias,
    w_query,
    b_query,
    w_key,
    b_key,
    w_value,
    b_value,
    w_out,
    b_out,
    norm2_gain,
    norm2_bias,
    w_up,
    b_up,
    w_down,
    b_down,
):
    rows, width = tokens.shape[1], tokens.shape[2]
    half = width // 2
    quarter = half // 4
    seqs = lax.axis_size("seq")
    place = lax.axis_index("span")
    seq = lax.axis_index("seq")
    core = seq % 2
    bit = (seq // 2) % 2
    deep = (seq // 4) % 4
    first = (crop_offset * start_kept)[0, 0]
    scal = jnp.stack([place, bit, core, first, deep]).astype(jnp.int32)
    start = (2 * bit + core) * quarter

    tok = tokens[0]
    dy = out_cotangent[0]

    piece = jnp.stack(
        [
            lax.dynamic_slice_in_dim(w, start, quarter, 0)
            for w in (w_query, w_key, w_value)
        ]
    )
    piece0 = to_span(piece)
    piece1 = to_seq(piece0, 2)
    pieces = (piece0, piece1, to_seq(piece0, 1), to_seq(piece1, 1))
    tok_oth = to_span(tok)

    small = jnp.concatenate(
        [
            jnp.stack(
                [
                    norm1_gain,
                    norm1_bias,
                    b_query,
                    b_key,
                    b_value,
                    norm2_gain,
                    norm2_bias,
                    b_out,
                    b_down,
                ]
            ),
            b_up.reshape(4, half),
        ]
    )
    small_oth = to_span(small)
    small_full = jnp.where(
        place == 0,
        jnp.concatenate([small, small_oth], axis=1),
        jnp.concatenate([small_oth, small], axis=1),
    ).astype(F32)
    vec_one = jnp.pad(small_full[:5], ((0, 3), (0, 0)))
    vec_two = jnp.pad(small_full[5:9], ((0, 4), (0, 0)))
    bup = jnp.concatenate([small_full[9:, :half], small_full[9:, half:]])

    out_piece = lax.dynamic_slice_in_dim(after(w_out, piece0), start, quarter, 0)
    up_piece = lax.dynamic_slice_in_dim(after(w_up, piece0), start, quarter, 0)
    up_piece = up_piece.reshape(quarter, 4, 2, half).transpose(2, 1, 0, 3)
    down_piece = lax.dynamic_slice_in_dim(
        after(w_down, piece0).reshape(4, half, width), start, quarter, 1
    )
    down_piece = [down_piece[0::2], down_piece[1::2]]
    out0 = to_span(out_piece)
    up0 = [to_span(up_piece[0]), None]
    down0 = [to_span(down_piece[0]), None]

    quarter_dim = HEAD_DIM // 2
    here = jnp.arange(rows, dtype=jnp.int32)
    places = jnp.concatenate([place * rows + here, (1 - place) * rows + here]) - first
    rates = jnp.power(
        jnp.float32(10000.0), -jnp.arange(quarter_dim, dtype=F32) / quarter_dim
    )
    angle = places.astype(F32)[:, None] * jnp.tile(rates, 4)[None, :]
    sign = jnp.tile(jnp.repeat(jnp.array([-1.0, 1.0], F32), quarter_dim), 2)
    cos = jnp.cos(angle)
    sin = jnp.sin(angle) * sign[None, :]

    n1t, query, keys, values, wall = qkv(
        scal, tok, tok_oth, vec_one, cos, sin, (w_query, w_key, w_value), pieces
    )
    out0, up_a = after(out0, n1t), after(up0[0], n1t)
    out_x, up_x = to_seq(out0, 2), to_seq(up_a, 2)
    up_b = to_span(after(up_piece[1], n1t))
    down_b = to_span(after(down_piece[1], n1t))
    part = attend(scal, after(query, out0, up_a), keys, values, 0)
    out_x, down_a = after(out_x, part[0]), after(down0[0], part[0])
    down_x = to_seq(down_a, 2)
    outs = (out0, out_x, to_seq(after(out0, part[0]), 1), to_seq(out_x, 1))
    up_core, down_core = to_seq(after(up_a, part[0]), 1), to_seq(down_a, 1)
    mixed, lse = attend(scal, after(query, out_x, down_a), keys, values, width // 256, part)
    up_x, down_x = after(up_x, mixed), after(down_x, mixed)
    ups = (up_a, up_x, up_core, to_seq(up_x, 1))
    downs = (down_a, down_x, down_core, to_seq(down_x, 1))
    up_b, down_b = after(up_b, mixed), after(down_b, mixed)
    up_bx, down_bx = to_seq(up_b, 2), to_seq(down_b, 2)
    up_bc, down_bc = to_seq(up_b, 1), to_seq(down_b, 1)
    hidden, normed, normed_t, wo = hidden_rows(
        scal, after(tok, up_x, down_x, up_b, down_b), mixed, vec_two, w_out, outs
    )
    up_bx, down_bx = after(up_bx, hidden), after(down_bx, hidden)
    ups = ups + (up_b, up_bx, up_bc, to_seq(up_bx, 1))
    downs = downs + (down_b, down_bx, down_bc, to_seq(down_bx, 1))
    layer_out, dh, branch, sdown, sup, kdown, kup, gbup, small_two = ffn(
        scal, mixed, dy, vec_two, bup, hidden, normed, normed_t, w_up, w_down, (*ups, *downs)
    )

    def deeper(item):
        return item.reshape(2, 2, 2, 2, *item.shape[3:])

    got_up, got_down = to_seq(sup, 1), to_seq(sdown, 1)
    do = out_back(scal, branch, wo)
    send_up, ups = split_send([deeper(kup), deeper(after(got_up, do))])
    got_up = to_span(send_up)
    send_down, downs = split_send([deeper(kdown), deeper(after(got_down, send_up))])
    got_down = to_seq(send_down, 2)

    def back(theirs, dout):
        return attend_back(
            scal, query, keys, values, mixed, dout, lse, cos, sin, n1t, theirs
        )

    split = (2, 2, 2, 3, half // 8, half)
    back_one = back(1, after(do, send_up, send_down))
    send, keep_one = back_one[4:]
    recv = to_seq(send, 1)
    (other,) = other_rows(scal, wall, back_one)
    send_over, over = split_send([keep_one.reshape(split), after(recv, other).reshape(split)])
    got_over = to_span(send_over)
    back_two = back(0, after(do, send_over))
    send, keep = back_two[4:]
    recv = to_seq(send, 1)
    send_up, ups = split_send(ups + [after(got_up, send)])
    got_up = to_seq(send_up, 2)
    send_over = add_low(*over, after(got_over, send_up))
    over_x = to_seq(send_over, 2)
    dn_oth, other_sum = other_rows(scal, after(wall, send_over), back_two, other, tok_oth)
    line = Line()
    line.put(dn_oth)
    send_proj, projs = split_send([item.reshape(split) for item in (keep, line.take(recv))])
    got_proj = to_span(line.put(send_proj))
    send_down, downs = split_send(downs + [line.take(got_down)])
    got_down = to_span(line.put(send_down))
    dn_own, small, small_oth = own_rows(
        scal, after(wall, send_down), back_two, back_one, tok,
        other_sum, back_one[3], back_two[3], small_two, gbup,
    )
    line.put(dn_own)
    dn_recv = to_span(after(dn_oth, dn_own))
    got_small = to_span(small_oth)

    send_up, ups = split_send(ups + [line.take(got_up)])
    got_up = to_seq(line.put(send_up), 4)
    projs = [item.reshape(4, *split[3:]) for item in projs + [line.take(got_proj), over_x]]
    sends = [add_low(*[item[d] for item in projs]) for d in range(1, 4)]
    got_proj = [to_seq(line.put(item), link) for item, link in zip(sends, (8, 4, 12))]
    send_down, downs = split_send(downs + [line.take(got_down)])
    got_down = to_seq(line.put(send_down), 4)
    send_up, ups = split_send(ups + [line.take(got_up)])
    got_up = to_seq(line.put(send_up), 8)
    small = line.put(small + line.take(got_small))
    got_small = to_seq(small, 1)
    proj = [item[0] for item in projs] + [line.take(got_proj[0]), *got_proj[1:]]
    proj = line.put(reduce_rest(add_low(*proj)))
    got_proj = [to_seq(proj, 8), to_seq(proj, 4), to_seq(proj, 12)]
    send_down, downs = split_send(downs + [line.take(got_down)])
    got_down = to_seq(line.put(send_down), 8)
    up = line.put(reduce_rest(add_low(*ups, line.take(got_up))))
    got_up = to_seq(up, 8)
    small = small + line.take(got_small)
    for link in rest_links():
        small = small + to_seq(small, link)
    small = high_low(small)
    down = reduce_rest(add_low(*downs, line.take(got_down)))
    down = line.put(jnp.concatenate([down, small]))
    got_down = to_seq(down, 8)
    proj = line.put(jnp.stack([proj, line.take(got_proj[0]), *got_proj[1:]]))
    proj_x, proj_core = to_seq(proj, 2), to_seq(proj, 1)

    def ride(mine, got):
        count = mine.shape[0] - small.shape[0]
        total = high_low(sum_of(mine[count:]) + sum_of(got[count:]))
        return jnp.concatenate([mine[:count], got[:count], total])

    up = line.put(jnp.concatenate([up, line.take(got_up)]))
    got_up = to_seq(up, 4)
    down = line.put(ride(down, line.take(got_down)))
    got_down = to_seq(down, 4)
    input_grad = line.put(input_grads(tok, dn_own, line.take(dn_recv), dh, vec_one))
    proj_x = line.put(line.take(proj_x))
    projs = (proj, proj_x, proj_core, to_seq(proj_x, 1))
    up = line.put(jnp.concatenate([up, line.take(got_up)]))
    up_x, up_core = to_seq(up, 2), to_seq(up, 1)
    down = line.put(ride(down, line.take(got_down)))
    down_x, down_core = to_seq(down, 2), to_seq(down, 1)
    proj = finish_proj(scal, projs)
    up_x = line.put(after(line.take(up_x), proj[0]))
    up_grad = finish_up(scal, (up, up_x, up_core, to_seq(up_x, 1)))
    down_x = after(line.take(down_x), up_grad)
    count = down.shape[0] - small.shape[0]
    total = sum_of(down[count:]) + sum_of(down_x[count:])
    down_grad, out_grad = finish_down(scal, (down, down_x, down_core, to_seq(down_x, 1)))

    return (
        layer_out[None],
        input_grad[None],
        total[0],
        total[1],
        proj[0],
        total[2],
        proj[1],
        total[3],
        proj[2],
        total[4],
        out_grad,
        total[7],
        total[5],
        total[6],
        up_grad,
        total[9:13].reshape(-1),
        down_grad,
        total[8],
    )


def solution(mesh):
    row, col = P(None, ("seq", "span"), None), P(None, "seq")
    vec, mat = P("span"), P("span", None)
    weights = (vec, vec, mat, vec, mat, vec, mat, vec, mat, vec, vec, vec, mat, vec, mat, vec)
    return jax.shard_map(
        shards,
        mesh=mesh,
        in_specs=(row, row, col, col) + weights,
        out_specs=(row, row) + weights,
        check_vma=False,
    )
```

```python
import functools

import jax
import jax.numpy as jnp
from jax import lax
from jax.experimental import pallas as pl
from jax.experimental.pallas import tpu as pltpu
from jax.sharding import PartitionSpec as P

HEADS = 12
HEAD_DIM = 64
SCALE = HEAD_DIM ** (-0.5)
F32 = jnp.float32
BF16 = jnp.bfloat16
VMEM_BYTES = 60 * 1024 * 1024
COST = pl.CostEstimate(flops=10**11, bytes_accessed=1024, transcendentals=0)


def deep_of(spot):
    return (spot >> 1) | ((spot & 1) << 1)


def dot(left, right, dim_l, dim_r):
    return lax.dot_general(
        left, right, (((dim_l,), (dim_r,)), ((), ())), preferred_element_type=F32
    )


def swap_halves(rows):
    half = rows.shape[-1] // 2
    return jnp.concatenate([rows[:, half:], rows[:, :half]], axis=1)


def own_first(rows, place):
    return jnp.where(place == 0, rows, swap_halves(rows))


def half_swap(tile):
    lane = lax.broadcasted_iota(jnp.int32, tile.shape, 1)
    width = tile.shape[1]
    return jnp.where(
        lane % HEAD_DIM < HEAD_DIM // 2,
        pltpu.roll(tile, width - HEAD_DIM // 2, 1),
        pltpu.roll(tile, HEAD_DIM // 2, 1),
    )


def params(**kw):
    return pltpu.CompilerParams(vmem_limit_bytes=VMEM_BYTES, **kw)


def vmem():
    return pl.BlockSpec(memory_space=pltpu.VMEM)


def anywhere():
    return pl.BlockSpec(memory_space=pl.ANY)


def qkv_kernel(
    scal, own_ref, oth_ref, vec_ref, cos_ref, sin_ref, wq, wk, wv, p0, p1, p2, p3,
    n1t_ref, q_ref, k_ref, v_ref, wall_ref, sems,
):
    step = pl.program_id(0)
    place = scal[0]
    half = wq.shape[0]

    @pl.when(step == 0)
    def _():
        copies = []
        for j, weight in enumerate((wq, wk, wv)):
            target = wall_ref.at[j]
            own = (weight, target.at[pl.ds(0, half)])
            copies += piece_copies(
                own, (p0, p1, p2, p3), scal, lambda p, j=j: p.at[j], target, half
            )
        wait_all(start_all(copies, sems, 0))

    rows = jnp.where(step < 2, own_ref[...], oth_ref[...]).astype(F32)
    center = rows - jnp.mean(rows, axis=1, keepdims=True)
    spread = jnp.mean(center * center, axis=1, keepdims=True)
    normed = center * lax.rsqrt(spread + 1e-05) * vec_ref[0:1] + vec_ref[1:2]
    normed = own_first(normed, place).astype(BF16)
    n1t_ref[...] = normed.T

    def rotated(j, ref, factor):
        flat = dot(normed, wall_ref[j], 1, 0) + vec_ref[2 + j : 3 + j]
        for t in range(flat.shape[1] // 128):
            tile = flat[:, t * 128 : (t + 1) * 128]
            turned = (tile * cos_ref[...] + half_swap(tile) * sin_ref[...]).astype(BF16)
            ref[:, t * 128 : (t + 1) * 128] = turned * factor if factor != 1 else turned

    @pl.when(step < 2)
    def _():
        rotated(0, q_ref, SCALE)

    rotated(1, k_ref, 1)
    v_ref[...] = (dot(normed, wall_ref[2], 1, 0) + vec_ref[4:5]).astype(BF16)


def qkv(scal, own, oth, vec, cos, sin, weights, pieces):
    rows, width = own.shape
    block = rows // 2
    grid_spec = pltpu.PrefetchScalarGridSpec(
        num_scalar_prefetch=1,
        grid=(4,),
        in_specs=[
            pl.BlockSpec((block, width), lambda i, s: (jnp.minimum(i, 1), 0)),
            pl.BlockSpec((block, width), lambda i, s: (jnp.maximum(i - 2, 0), 0)),
            pl.BlockSpec(vec.shape, lambda i, s: (0, 0)),
            pl.BlockSpec((block, 128), lambda i, s: (i, 0)),
            pl.BlockSpec((block, 128), lambda i, s: (i, 0)),
        ]
        + [anywhere()] * 7,
        out_specs=[
            pl.BlockSpec((width, block), lambda i, s: (0, i)),
            pl.BlockSpec((block, width), lambda i, s: (jnp.minimum(i, 1), 0)),
            pl.BlockSpec((block, width), lambda i, s: (i, 0)),
            pl.BlockSpec((block, width), lambda i, s: (i, 0)),
            pl.BlockSpec((3, width, width), lambda i, s: (0, 0, 0)),
        ],
        scratch_shapes=[pltpu.SemaphoreType.DMA((15,))],
    )
    shape = jax.ShapeDtypeStruct
    return pl.pallas_call(
        qkv_kernel,
        grid_spec=grid_spec,
        out_shape=[
            shape((width, 2 * rows), BF16),
            shape((rows, width), BF16),
            shape((2 * rows, width), BF16),
            shape((2 * rows, width), BF16),
            shape((3, width, width), BF16),
        ],
        compiler_params=params(),
        cost_estimate=COST,
        name="qkv",
    )(scal, own, oth, vec, cos, sin, *weights, *pieces)


def key_bias(scal, keys):
    place, first = scal[0], scal[3]
    half = keys // 2
    row = lax.broadcasted_iota(jnp.int32, (keys, 128), 0)
    where = jnp.where(row < half, place * half + row, (1 - place) * half + row - half)
    return jnp.where(where < first, -1e30, 0.0).astype(BF16)


def masked_pair(head, keys, query, bias):
    lane_k = lax.broadcasted_iota(jnp.int32, keys.shape, 1)
    lane_q = lax.broadcasted_iota(jnp.int32, query.shape, 1)
    spot = (1 - head) * HEAD_DIM
    zero = jnp.zeros((), BF16)
    keys = jnp.where(
        lane_k // HEAD_DIM == head, keys, jnp.where(lane_k == spot, bias, zero)
    )
    query = jnp.where(
        lane_q // HEAD_DIM == head,
        query,
        jnp.where(lane_q == spot, jnp.ones((), BF16), zero),
    )
    return keys, query


def attend_kernel(scal, q_ref, k_ref, v_ref, *refs):
    o_ref, lse_ref = refs[-2:]
    keys, values, query = k_ref[...], v_ref[...], q_ref[...]
    bias = key_bias(scal, keys.shape[0])
    values_t = values.T
    outs = []
    for head in range(2):
        keys_m, query_m = masked_pair(head, keys, query, bias)
        scores = dot(keys_m, query_m, 1, 1)
        top = jnp.max(scores, axis=0, keepdims=True)
        expo = jnp.exp(scores - top)
        total = jnp.sum(expo, axis=0, keepdims=True)
        mixed = dot(
            values_t[head * HEAD_DIM : (head + 1) * HEAD_DIM], expo.astype(BF16), 1, 0
        )
        outs.append(mixed / total)
        lse_ref[0, head : head + 1] = top + jnp.log(total)
    o_ref[...] = jnp.concatenate(outs, axis=0).T.astype(BF16)


def attend(scal, query, keys, values, begin, earlier=()):
    rows, width = query.shape
    span = keys.shape[0]
    pairs = width // 256
    grid_spec = pltpu.PrefetchScalarGridSpec(
        num_scalar_prefetch=1,
        grid=(pairs,),
        in_specs=[
            pl.BlockSpec((rows, 128), lambda i, s: (0, i + begin)),
            pl.BlockSpec((span, 128), lambda i, s: (0, i + begin)),
            pl.BlockSpec((span, 128), lambda i, s: (0, i + begin)),
        ]
        + [anywhere()] * len(earlier),
        out_specs=[
            pl.BlockSpec((rows, 128), lambda i, s: (0, i + begin)),
            pl.BlockSpec((1, 8, rows), lambda i, s: (i + begin, 0, 0)),
        ],
    )
    return pl.pallas_call(
        attend_kernel,
        grid_spec=grid_spec,
        out_shape=[
            jax.ShapeDtypeStruct((rows, width), BF16),
            jax.ShapeDtypeStruct((2 * pairs, 8, rows), F32),
        ],
        input_output_aliases={4: 0, 5: 1} if earlier else {},
        compiler_params=params(),
        cost_estimate=COST,
        name="attend",
    )(scal, query, keys, values, *earlier)


def attend_back_kernel(
    scal, q_ref, k_ref, v_ref, o_ref, do_ref, lse_ref, cos_ref, sin_ref, n1t_ref,
    dq_ref, dk_ref, dv_ref, bias_ref, send_ref, keep_ref, g_s,
):
    step = pl.program_id(0)
    pairs = dq_ref.shape[1] // 128

    @pl.when(step < pairs)
    def _():
        at = pl.ds(pl.multiple_of(step * 128, 128), 128)
        keys, values, query, dout = k_ref[...], v_ref[...], q_ref[...], do_ref[...]
        rows = query.shape[0]
        bias = key_bias(scal, keys.shape[0])
        keys_t = keys.T
        product = (dout.astype(F32) * o_ref[...].astype(F32)).T
        lane = lax.broadcasted_iota(jnp.int32, values.shape, 1)
        parts = []
        for head in range(2):
            keys_m, query_m = masked_pair(head, keys, query, bias)
            values_m = jnp.where(lane // HEAD_DIM == head, values, jnp.zeros((), BF16))
            inner = jnp.sum(
                product[head * HEAD_DIM : (head + 1) * HEAD_DIM], axis=0, keepdims=True
            )
            probs = jnp.exp(dot(keys_m, query_m, 1, 1) - lse_ref[0, head : head + 1])
            grad = dot(values_m, dout, 1, 1)
            score_grad = (probs * (grad - inner)).astype(BF16)
            dv = dot(probs.astype(BF16), dout, 1, 0)
            dk = dot(score_grad, query, 1, 0)
            dq = dot(keys_t[head * HEAD_DIM : (head + 1) * HEAD_DIM], score_grad, 1, 0)
            parts.append((dq, dk, dv))
        dq = (jnp.concatenate([parts[0][0], parts[1][0]], axis=0).T * SCALE).astype(BF16)
        dk = jnp.where(lane // HEAD_DIM == 0, parts[0][1], parts[1][1]).astype(BF16)
        dv = jnp.where(lane // HEAD_DIM == 0, parts[0][2], parts[1][2]).astype(BF16)
        dq, dk = dq.astype(F32), dk.astype(F32)
        dq = (dq * cos_ref[:rows] - half_swap(dq) * sin_ref[:rows]).astype(BF16)
        dk = (dk * cos_ref[...] - half_swap(dk) * sin_ref[...]).astype(BF16)
        dq_ref[:, at] = dq
        dk_ref[:, at] = dk
        dv_ref[:, at] = dv
        bias_ref[0:1, at] = jnp.sum(dq.astype(F32), axis=0, keepdims=True)
        bias_ref[1:2, at] = jnp.sum(dk.astype(F32), axis=0, keepdims=True)
        bias_ref[2:3, at] = jnp.sum(dv.astype(F32), axis=0, keepdims=True)

    @pl.when(step == pairs)
    def _():
        core, deep = scal[2], scal[4]
        half = dq_ref.shape[1]
        size = half // 8
        for w, ref in enumerate((dq_ref, dk_ref, dv_ref)):
            g_s[w] = dot(n1t_ref[:, : ref.shape[0]], ref[...], 1, 0).astype(BF16)
        for w in range(3):
            for s in range(2):
                for d in range(4):
                    row = s * half + (deep ^ deep_of(d)) * size
                    for out, mine in ((send_ref, 1 - core), (keep_ref, core)):
                        at = pl.multiple_of(row + mine * 4 * size, 16)
                        out[s, d, w] = g_s[w, pl.ds(at, size)]


def attend_back(scal, query, keys, values, mixed, dout, lse, cos, sin, n1t, theirs):
    rows, width = query.shape[0], query.shape[1] // 2
    span = keys.shape[0]
    pairs = width // 128

    def at(i, s):
        return jnp.minimum(i, pairs - 1) + pairs * (1 - s[1] if theirs else s[1])

    def fixed(shape):
        return pl.BlockSpec(shape, lambda i, s: tuple(0 for _ in shape))

    few = pl.BlockSpec((rows, 128), lambda i, s: (0, at(i, s)))
    many = pl.BlockSpec((span, 128), lambda i, s: (0, at(i, s)))
    buffer = (2, 4, 3, width // 8, width)
    outs = [(rows, width), (span, width), (span, width), (8, width), buffer, buffer]
    grid_spec = pltpu.PrefetchScalarGridSpec(
        num_scalar_prefetch=1,
        grid=(pairs + 1,),
        in_specs=[few, many, many, few, few]
        + [pl.BlockSpec((1, 8, rows), lambda i, s: (at(i, s), 0, 0))]
        + [fixed((span, 128)), fixed((span, 128)), fixed(n1t.shape)],
        out_specs=[fixed(item) for item in outs],
        scratch_shapes=[pltpu.VMEM((3, 2 * width, width), BF16)],
    )
    return pl.pallas_call(
        attend_back_kernel,
        grid_spec=grid_spec,
        out_shape=[
            jax.ShapeDtypeStruct(item, F32 if n == 3 else BF16) for n, item in enumerate(outs)
        ],
        compiler_params=params(),
        cost_estimate=COST,
        name="attend_back",
    )(scal, query, keys, values, mixed, dout, lse, cos, sin, n1t)


def norm_stats(rows):
    center = rows - jnp.mean(rows, axis=1, keepdims=True)
    spread = jnp.mean(center * center, axis=1, keepdims=True)
    return center, lax.rsqrt(spread + 1e-05)


def norm_back(rows, grad, gain):
    center, rate = norm_stats(rows)
    hat = center * rate
    scaled = grad * gain
    out = rate * (
        scaled
        - jnp.mean(scaled, axis=1, keepdims=True)
        - hat * jnp.mean(scaled * hat, axis=1, keepdims=True)
    )
    return (
        out,
        jnp.sum(grad * hat, axis=0, keepdims=True),
        jnp.sum(grad, axis=0, keepdims=True),
    )


def piece_copies(own, pieces, scal, select, target, base):
    bit, core = scal[1], scal[2]
    p0, p1, p2, p3 = pieces
    spots = (
        (p0, 2 * bit + core),
        (p1, 2 * (1 - bit) + core),
        (p2, 2 * bit + 1 - core),
        (p3, 2 * (1 - bit) + 1 - core),
    )
    copies = [] if own is None else [own]
    for src, index in spots:
        part = select(src)
        rows = part.shape[0]
        start = pl.multiple_of(base + index * rows, 32)
        copies.append((part, target.at[pl.ds(start, rows)]))
    return copies


def load_out(scal, wo_own, pieces, wo_s):
    half = wo_own.shape[0]
    own = (wo_own, wo_s.at[pl.ds(0, half)])
    return piece_copies(own, pieces, scal, lambda p: p, wo_s, half)


def load_chunk(scal, part, t, up_own, down_own, ups, downs, chunk, up_s, down_s):
    place = scal[0]
    core = scal[2] if t == 1 else 1 - scal[2]
    half = up_own.shape[0]
    copies = []
    for n, span in enumerate((1 - place, place)):
        index = 2 * span + core
        column = pl.multiple_of((2 * index + part) * half, 128)
        target = up_s.at[chunk, :, pl.ds(n * half, half)]
        own = (up_own.at[:, pl.ds(column, half)], target.at[pl.ds(0, half)])
        copies += piece_copies(own, ups, scal, lambda p, index=index: p.at[index], target, half)
    start = pl.multiple_of((2 * core + part) * half, 128)
    copies.append((down_own.at[pl.ds(start, half)], down_s.at[chunk, pl.ds(half, half)]))
    copies += piece_copies(None, downs, scal, lambda p: p.at[core], down_s.at[chunk], 0)
    return copies


def start_all(copies, sems, base):
    started = [
        pltpu.make_async_copy(src, dst, sems.at[base + n]) for n, (src, dst) in enumerate(copies)
    ]
    for copy in started:
        copy.start()
    return started


def wait_all(started):
    for copy in started:
        copy.wait()


def chunk_spots(scal, t, part):
    place = scal[0]
    core = scal[2] if t == 1 else 1 - scal[2]
    return [2 * (2 * span + core) + part for span in (1 - place, place)]


def product_tasks(n, chunk, dy_ref, n2_ref, up_s, down_s, u_s, da_s):
    def one(c):
        at = slice(c, c + 256)
        u_s[n, :, at] = dot(n2_ref[...], up_s[chunk, :, at], 1, 0)

    def two(c):
        at = slice(c, c + 256)
        da_s[n, :, at] = dot(dy_ref[...], down_s[chunk, at], 1, 1)

    columns = range(0, u_s.shape[2], 256)
    return [functools.partial(task, c) for task in (one, two) for c in columns]


def element_tasks(scal, n, t, part, bup_ref, u_s, da_s, a_s, du_s, gbup_ref):
    rows, width = a_s.shape[1:]
    half = width // 2
    block = rows // 16
    spots = chunk_spots(scal, t, part)
    sums = [jnp.zeros((8, width), F32)]

    def one(r):
        at = slice(r, r + block)
        bias = jnp.concatenate([bup_ref[pl.ds(n, 1)] for n in spots], axis=1)
        inner = u_s[n, at] + bias
        phi = 0.5 + 0.5 * lax.erf(inner * 0.7071067811865476)
        slope = phi + inner * (0.3989422804014327 * jnp.exp(-0.5 * inner * inner))
        a_s[n, at] = (inner * phi).astype(BF16)
        du = (da_s[n, at] * slope).astype(BF16)
        du_s[n, at] = du
        sums[0] = sums[0] + jnp.sum(du.astype(F32).reshape(block // 8, 8, width), axis=0)
        if r + block == rows:
            total = jnp.sum(sums[0], axis=0, keepdims=True)
            for j, row in enumerate(spots):
                gbup_ref[pl.ds(row, 1)] = total[:, j * half : (j + 1) * half]

    return [functools.partial(one, r) for r in range(0, rows, block)]


def grad_tasks(
    scal, n, chunk, part, dy_ref, n2t_ref, up_s, down_s, acc_s, dacc_s, a_s, du_s, down_out, up_out, g_s
):
    place, bit, deep = scal[0], scal[1], scal[4]
    half = g_s.shape[1] // 2
    size = half // 4
    rows = slice(part * size, (part + 1) * size)

    def layer(c):
        at = slice(c, c + 256)
        acc_s[:, at] += dot(a_s[n], down_s[chunk, :, at], 1, 0)

    def back(c):
        at = slice(c, c + 256)
        dacc_s[:, at] += dot(du_s[n], up_s[chunk, at], 1, 1)

    def down(c):
        at = slice(c, c + 256)
        g_s[0, :, at] = dot(a_s[n], dy_ref[:, at], 0, 0).astype(BF16)

    def up(c):
        at = slice(c, c + 256)
        g_s[1, :, at] = dot(n2t_ref[...], du_s[n, :, at], 1, 0).astype(BF16)

    def place_down():
        for s in range(2):
            for k in range(2):
                at = pl.multiple_of((bit if k == 0 else 1 - bit) * half, 128)
                for d in range(4):
                    row = (1 - s) * half + (deep ^ deep_of(d)) * size
                    row = pl.multiple_of(row, 32)
                    down_out[k, s, d, rows] = g_s[0, pl.ds(row, size), pl.ds(at, half)]

    def place_up():
        for s in range(2):
            for k in range(2):
                column = bit if k == 0 else 1 - bit
                at = pl.multiple_of(jnp.where(column == place, half, 0), 128)
                for d in range(4):
                    row = pl.multiple_of(s * half + (deep ^ deep_of(d)) * size, 32)
                    up_out[s, k, d, rows] = g_s[1, pl.ds(row, size), pl.ds(at, half)]

    columns = range(0, acc_s.shape[1], 256)
    tasks = []
    for task, then in ((down, place_down), (up, place_up), (layer, None), (back, None)):
        tasks += [functools.partial(task, c) for c in columns]
        if then is not None:
            tasks.append(then)
    return tasks


def interleave(first, second):
    done = 0
    for i, task in enumerate(first):
        task()
        upto = (i + 1) * len(second) // len(first)
        for other in second[done:upto]:
            other()
        done = upto


def hidden_kernel(
    scal, x_ref, o_ref, vec_ref, wo_own, p0, p1, p2, p3, h_ref, n2_ref, n2t_ref, wo_s, sems
):
    place = scal[0]
    rows = x_ref.shape[0]
    block = rows // 8
    wait_all(start_all(load_out(scal, wo_own, (p0, p1, p2, p3), wo_s), sems, 0))
    h_ref[...] = dot(own_first(o_ref[...], place), wo_s[...], 1, 0)
    for r in range(0, rows, block):
        at = slice(r, r + block)
        hidden = h_ref[at] + (x_ref[at].astype(F32) + vec_ref[2:3])
        h_ref[at] = hidden
        center, rate = norm_stats(hidden)
        normed = center * rate * vec_ref[0:1] + vec_ref[1:2]
        n2_ref[at] = own_first(normed, place).astype(BF16)
    n2t_ref[...] = n2_ref[...].T


def hidden_rows(scal, tokens, mixed, vec, w_out, pieces):
    rows, width = tokens.shape
    shape = jax.ShapeDtypeStruct
    return pl.pallas_call(
        hidden_kernel,
        in_specs=[pl.BlockSpec(memory_space=pltpu.SMEM)] + [vmem()] * 3 + [anywhere()] * 5,
        out_specs=[vmem()] * 4,
        out_shape=[
            shape((rows, width), F32),
            shape((rows, width), BF16),
            shape((width, rows), BF16),
            shape((width, width), BF16),
        ],
        scratch_shapes=[pltpu.SemaphoreType.DMA((5,))],
        compiler_params=params(),
        cost_estimate=COST,
        name="hidden_rows",
    )(scal, tokens, mixed, vec, w_out, *pieces)


def ffn_kernel(
    scal, o_ref, dy_ref, vec_ref, bup_ref, h_ref, n2_ref, n2t_ref, up_own, down_own, *refs
):
    pieces, refs = refs[:16], refs[16:]
    (
        out_ref, dh_ref, branch_ref, sdown_ref, sup_ref, kdown_ref, kup_ref, gbup_ref, small_ref,
        u_s, da_s, a_s, du_s, up_s, down_s, g_s, acc_s, dacc_s, go_s, sems,
    ) = refs
    place, bit, core, deep = scal[0], scal[1], scal[2], scal[4]
    rows, width = dy_ref.shape
    half = width // 2
    block = rows // 8
    order = [(part, t) for t in range(2) for part in range(2)]
    waits = []
    for chunk, (part, t) in enumerate(order):
        ups, downs = pieces[4 * part : 4 * part + 4], pieces[8 + 4 * part : 12 + 4 * part]
        copies = load_chunk(
            scal, part, t, up_own, down_own, ups, downs, chunk, up_s, down_s
        )
        waits.append(start_all(copies, sems, 15 * chunk))
    acc_s[...] = h_ref[...] + vec_ref[3:4]
    dacc_s[...] = jnp.zeros_like(dacc_s)
    def products(chunk):
        wait_all(waits[chunk])
        return product_tasks(chunk % 2, chunk, dy_ref, n2_ref, up_s, down_s, u_s, da_s)

    def grads(chunk):
        part, t = order[chunk]
        down_out, up_out = (kdown_ref, kup_ref) if t == 1 else (sdown_ref, sup_ref)
        return grad_tasks(
            scal, chunk % 2, chunk, part, dy_ref, n2t_ref, up_s, down_s, acc_s, dacc_s, a_s, du_s,
            down_out, up_out, g_s,
        )

    for task in products(0):
        task()
    for chunk, (part, t) in enumerate(order):
        tasks = products(chunk + 1) if chunk + 1 < len(order) else []
        tasks = tasks + (grads(chunk - 1) if chunk > 0 else [])
        interleave(
            element_tasks(scal, chunk % 2, t, part, bup_ref, u_s, da_s, a_s, du_s, gbup_ref), tasks
        )
    for task in grads(len(order) - 1):
        task()
    sums = [jnp.zeros((1, width), F32) for _ in range(4)]
    for r in range(0, rows, block):
        at = slice(r, r + block)
        out_ref[at] = acc_s[at].astype(BF16)
        grad = own_first(dacc_s[at], place)
        dy = dy_ref[at].astype(F32)
        part, gain_sum, shift_sum = norm_back(h_ref[at], grad, vec_ref[0:1])
        dh = dy + part
        dh_ref[at] = dh
        branch = dh.astype(BF16)
        branch_ref[at] = branch
        terms = (
            gain_sum,
            shift_sum,
            jnp.sum(branch.astype(F32), axis=0, keepdims=True),
            jnp.sum(dy, axis=0, keepdims=True),
        )
        sums = [old + new for old, new in zip(sums, terms)]
    for n, item in enumerate(sums):
        small_ref[n : n + 1] = item
    go_s[...] = dot(own_first(o_ref[...], place), branch_ref[...], 0, 0)
    size = half // 8
    for s in range(2):
        for k in range(2):
            column = pl.multiple_of((bit if k == 0 else 1 - bit) * half, 128)
            for d in range(4):
                row = s * half + (deep ^ deep_of(d)) * size
                for out, mine in ((sdown_ref, 1 - core), (kdown_ref, core)):
                    at = pl.multiple_of(row + mine * 4 * size, 16)
                    out[k, s, d, 4 * size :] = go_s[pl.ds(at, size), pl.ds(column, half)].astype(BF16)


def ffn(scal, mixed, dy, vec, bup, hidden, normed, normed_t, w_up, w_down, pieces):
    rows, width = mixed.shape
    half = width // 2
    shape = jax.ShapeDtypeStruct
    down = shape((2, 2, 4, half // 2 + half // 8, half), BF16)
    up = shape((2, 2, 4, half // 2, half), BF16)
    return pl.pallas_call(
        ffn_kernel,
        in_specs=[pl.BlockSpec(memory_space=pltpu.SMEM)] + [vmem()] * 7 + [anywhere()] * 18,
        out_specs=[vmem()] * 9,
        out_shape=[
            shape((rows, width), BF16),
            shape((rows, width), F32),
            shape((rows, width), BF16),
            down,
            up,
            down,
            up,
            shape((8, half), F32),
            shape((8, width), F32),
        ],
        scratch_shapes=[
            pltpu.VMEM((2, rows, width), F32),
            pltpu.VMEM((2, rows, width), F32),
            pltpu.VMEM((2, rows, width), BF16),
            pltpu.VMEM((2, rows, width), BF16),
            pltpu.VMEM((4, width, width), BF16),
            pltpu.VMEM((4, width, width), BF16),
            pltpu.VMEM((2, width, width), BF16),
            pltpu.VMEM((rows, width), F32),
            pltpu.VMEM((rows, width), F32),
            pltpu.VMEM((width, width), F32),
            pltpu.SemaphoreType.DMA((60,)),
        ],
        compiler_params=params(),
        cost_estimate=COST,
        name="ffn",
    )(scal, mixed, dy, vec, bup, hidden, normed, normed_t, w_up, w_down, *pieces)


def out_back_kernel(scal, branch_ref, wo_ref, do_ref):
    do_ref[...] = own_first(dot(branch_ref[...], wo_ref[...], 1, 1), scal[0]).astype(BF16)


def out_back(scal, branch, wo):
    return pl.pallas_call(
        out_back_kernel,
        in_specs=[pl.BlockSpec(memory_space=pltpu.SMEM), vmem(), vmem()],
        out_specs=vmem(),
        out_shape=jax.ShapeDtypeStruct(branch.shape, BF16),
        compiler_params=params(),
        cost_estimate=COST,
        name="out_back",
    )(scal, branch, wo)


def columns_of(scal, theirs, half):
    return pl.ds(pl.multiple_of((1 - scal[1] if theirs else scal[1]) * half, 128), half)


def norm_products(scal, w_ref, parts, first):
    total = 0.0
    for theirs in range(2):
        for n, ref in enumerate(parts[theirs]):
            at = columns_of(scal, theirs, ref.shape[1])
            total = total + dot(ref[...], w_ref[first + n, :, at], 1, 1)
    return own_first(total, scal[0])


def norm_sums(x_ref, grad):
    block = grad.shape[0] // 4
    gain, shift = 0.0, 0.0
    for r in range(0, grad.shape[0], block):
        center, rate = norm_stats(x_ref[r : r + block].astype(F32))
        part = grad[r : r + block]
        gain = gain + jnp.sum(part * (center * rate), axis=0, keepdims=True)
        shift = shift + jnp.sum(part, axis=0, keepdims=True)
    return gain, shift


def fixed_spec(shape):
    return pl.BlockSpec(shape, lambda i, s: tuple(0 for _ in shape))


def other_kernel(scal, w_ref, dk_ref, dv_ref, *refs):
    theirs = len(refs) == 1
    at = columns_of(scal, theirs, dk_ref.shape[1])
    total = dot(dk_ref[...], w_ref[1, :, at], 1, 1) + dot(dv_ref[...], w_ref[2, :, at], 1, 1)
    if theirs:
        refs[0][...] = total
    else:
        earlier_ref, x_ref, out_ref, sum_ref = refs
        grad = own_first(total + earlier_ref[...], scal[0])
        out_ref[...] = grad.astype(BF16)
        gain, shift = norm_sums(x_ref, grad)
        sum_ref[0:1] = gain
        sum_ref[1:2] = shift


def other_rows(scal, wall, back, *rest):
    width = wall.shape[2]
    rows = back[1].shape[0] // 2
    part = pl.BlockSpec((rows, width // 2), lambda i, s: (1, 0))
    shapes = [((rows, width), BF16), ((8, width), F32)] if rest else [((rows, width), F32)]
    return pl.pallas_call(
        other_kernel,
        grid_spec=pltpu.PrefetchScalarGridSpec(
            num_scalar_prefetch=1,
            grid=(1,),
            in_specs=[fixed_spec(wall.shape), part, part] + [fixed_spec(item.shape) for item in rest],
            out_specs=[fixed_spec(item) for item, _ in shapes],
        ),
        out_shape=[jax.ShapeDtypeStruct(*item) for item in shapes],
        compiler_params=params(),
        cost_estimate=COST,
        name="other_rows",
    )(scal, wall, back[1], back[2], *rest)


def own_kernel(
    scal, w_ref, q1, k1, v1, q0, k0, v0, x_ref, other_sum, bias_one, bias_two, two_ref, bup_ref,
    out_ref, small_ref, send_ref,
):
    place, bit = scal[0], scal[1]
    half = x_ref.shape[1] // 2
    grad = norm_products(scal, w_ref, ((q1, k1, v1), (q0, k0, v0)), 0)
    out_ref[...] = grad
    gain, shift = norm_sums(x_ref, grad)
    ends = jnp.concatenate([gain, shift], axis=0) + other_sum[0:2]
    blank = jnp.zeros((3, half), F32)
    sides = []
    for n in range(2):
        at = slice(n * half, (n + 1) * half)
        same = bias_two[0:3] if n == 0 else bias_one[0:3]
        swap = bias_one[0:3] if n == 0 else bias_two[0:3]
        bias = jnp.where(bit == 0, same, swap)
        sides.append(
            jnp.concatenate(
                [ends[:, at], bias, two_ref[0:4, at], bup_ref[4 * n : 4 * n + 4], blank], axis=0
            )
        )
    small_ref[...] = jnp.where(place == 0, sides[0], sides[1])
    send_ref[...] = jnp.where(place == 0, sides[1], sides[0])


def own_rows(scal, wall, mine, theirs, *rest):
    rows, width = rest[0].shape
    part = fixed_spec((rows, width // 2))
    shapes = [(rows, width), (16, width // 2), (16, width // 2)]
    return pl.pallas_call(
        own_kernel,
        grid_spec=pltpu.PrefetchScalarGridSpec(
            num_scalar_prefetch=1,
            grid=(1,),
            in_specs=[fixed_spec(wall.shape)] + [part] * 6 + [fixed_spec(item.shape) for item in rest],
            out_specs=[fixed_spec(item) for item in shapes],
        ),
        out_shape=[jax.ShapeDtypeStruct(item, F32) for item in shapes],
        compiler_params=params(),
        cost_estimate=COST,
        name="own_rows",
    )(scal, wall, *mine[:3], *theirs[:3], *rest)


def input_kernel(x_ref, own_ref, recv_ref, dh_ref, vec_ref, out_ref):
    grad = own_ref[...] + recv_ref[...].astype(F32)
    part, _, _ = norm_back(x_ref[...].astype(F32), grad, vec_ref[0:1])
    out_ref[...] = (dh_ref[...] + part).astype(BF16)


def input_grads(tokens, dn_own, dn_recv, dh, vec):
    rows, width = tokens.shape
    tile = pl.BlockSpec((rows // 4, width), lambda i: (i, 0))
    return pl.pallas_call(
        input_kernel,
        grid=(4,),
        in_specs=[tile, tile, tile, tile, pl.BlockSpec(vec.shape, lambda i: (0, 0))],
        out_specs=tile,
        out_shape=jax.ShapeDtypeStruct((rows, width), BF16),
        compiler_params=params(),
        cost_estimate=COST,
        name="input_grads",
    )(tokens, dn_own, dn_recv, dh, vec)


def spot_of(scal, i):
    bit = jnp.where(i % 2 == 0, scal[1], 1 - scal[1])
    core = jnp.where(i < 2, scal[2], 1 - scal[2])
    return core, bit


def finish_down_kernel(scal, *refs):
    parts, (down_ref, out_ref) = refs[:4], refs[4:]
    step = pl.program_id(0)
    deep = scal[4]
    half = down_ref.shape[1]
    size = half // 4
    count = 2 * size + size // 2
    for i in range(4):

        @pl.when(step == i)
        def _(i=i):
            for d in range(4):
                start = d * count
                for part in range(2):
                    row = pl.multiple_of(part * half + (deep ^ deep_of(d)) * size, 32)
                    at = start + part * size
                    down_ref[pl.ds(row, size)] = parts[i][at : at + size].astype(F32)
                row = pl.multiple_of((deep ^ deep_of(d)) * (size // 2), 16)
                at = start + 2 * size
                out_ref[pl.ds(row, size // 2)] = parts[i][at : at + size // 2].astype(F32)


def finish_up_kernel(scal, *refs):
    parts, up_ref = refs[:4], refs[4]
    step = pl.program_id(0)
    deep = scal[4]
    half = up_ref.shape[0]
    size = half // 4
    for i in range(4):

        @pl.when(step == i)
        def _(i=i):
            for d in range(4):
                row = pl.multiple_of((deep ^ deep_of(d)) * size, 32)
                for part in range(2):
                    at = (2 * d + part) * size
                    up_ref[pl.ds(row, size), part * half : (part + 1) * half] = parts[i][
                        at : at + size
                    ].astype(F32)


def finish_call(body, scal, parts, out_specs, out_shape, name):
    return pl.pallas_call(
        body,
        grid_spec=pltpu.PrefetchScalarGridSpec(
            num_scalar_prefetch=1,
            grid=(4,),
            in_specs=[pl.BlockSpec(item.shape, lambda i, s: (0, 0)) for item in parts],
            out_specs=out_specs,
        ),
        out_shape=[jax.ShapeDtypeStruct(item, F32) for item in out_shape],
        compiler_params=params(),
        cost_estimate=COST,
        name=name,
    )(scal, *parts)


def finish_down(scal, parts):
    half = parts[0].shape[1]
    specs = [pl.BlockSpec((count, half), lambda i, s: spot_of(s, i)) for count in (2 * half, half // 2)]
    shapes = [(4 * half, 2 * half), (half, 2 * half)]
    return finish_call(finish_down_kernel, scal, parts, specs, shapes, "finish_down")


def finish_up(scal, parts):
    half = parts[0].shape[1]

    def at(i, s):
        core, bit = spot_of(s, i)
        return (0, 2 * bit + core)

    specs = [pl.BlockSpec((half, 2 * half), at)]
    return finish_call(finish_up_kernel, scal, parts, specs, [(half, 8 * half)], "finish_up")[0]


def finish_proj_kernel(scal, *refs):
    parts, outs = refs[:4], refs[4:]
    step = pl.program_id(0)
    deep = scal[4]
    size = outs[0].shape[0] // 4
    for i in range(4):

        @pl.when(step == i)
        def _(i=i):
            for d in range(4):
                row = pl.multiple_of((deep ^ deep_of(d)) * size, 16)
                for n, out in enumerate(outs):
                    out[pl.ds(row, size)] = parts[i][d, n].astype(F32)


def finish_proj(scal, parts):
    half = parts[0].shape[3]
    spec = pl.BlockSpec((half // 2, half), lambda i, s: spot_of(s, i))
    grid_spec = pltpu.PrefetchScalarGridSpec(
        num_scalar_prefetch=1,
        grid=(4,),
        in_specs=[pl.BlockSpec(item.shape, lambda i, s: (0, 0, 0, 0)) for item in parts],
        out_specs=[spec] * 3,
    )
    return pl.pallas_call(
        finish_proj_kernel,
        grid_spec=grid_spec,
        out_shape=[jax.ShapeDtypeStruct((half, 2 * half), F32)] * 3,
        compiler_params=params(),
        cost_estimate=COST,
        name="finish_proj",
    )(scal, *parts)


def add_low(*terms):
    total = terms[0].astype(F32)
    for term in terms[1:]:
        total = total + term.astype(F32)
    return total.astype(BF16)


def to_span(rows):
    return lax.ppermute(rows, "span", [(0, 1), (1, 0)])


def to_seq(rows, bit):
    size = lax.axis_size("seq")
    return lax.ppermute(rows, "seq", [(i, i ^ bit) for i in range(size)])


def after(value, *others):
    return lax.optimization_barrier((value, *others))[0]


def split_send(parts):
    return add_low(*[part[1] for part in parts]), [part[0] for part in parts]


def high_low(total):
    low = total - lax.reduce_precision(total, 8, 7)
    return jnp.concatenate([total.astype(BF16), low.astype(BF16)])


def sum_of(rows):
    half = rows.shape[0] // 2
    return rows[:half].astype(F32) + rows[half:].astype(F32)


def rest_links():
    link, links = 16, []
    while link < lax.axis_size("seq"):
        links.append(link)
        link *= 2
    return links


def reduce_rest(rows):
    shape = rows.shape
    rows = rows.reshape(-1, shape[-1])
    seq = lax.axis_index("seq")
    for link in rest_links():
        bit = (seq // link) % 2
        two = rows.reshape(2, -1, shape[-1])
        send = lax.dynamic_index_in_dim(two, 1 - bit, 0, False)
        rows = add_low(lax.dynamic_index_in_dim(two, bit, 0, False), to_seq(send, link))
    for link in rest_links()[::-1]:
        bit = (seq // link) % 2
        got = to_seq(rows, link)
        rows = jnp.concatenate([jnp.where(bit == 0, rows, got), jnp.where(bit == 0, got, rows)])
    return rows.reshape(shape)


class Line:
    def __init__(self):
        self.last = None

    def take(self, value):
        return value if self.last is None else after(value, self.last)

    def put(self, value):
        self.last = value
        return value


def shards(
    tokens,
    out_cotangent,
    crop_offset,
    start_kept,
    norm1_gain,
    norm1_bias,
    w_query,
    b_query,
    w_key,
    b_key,
    w_value,
    b_value,
    w_out,
    b_out,
    norm2_gain,
    norm2_bias,
    w_up,
    b_up,
    w_down,
    b_down,
):
    rows, width = tokens.shape[1], tokens.shape[2]
    half = width // 2
    quarter = half // 4
    seqs = lax.axis_size("seq")
    place = lax.axis_index("span")
    seq = lax.axis_index("seq")
    core = seq % 2
    bit = (seq // 2) % 2
    deep = (seq // 4) % 4
    first = (crop_offset * start_kept)[0, 0]
    scal = jnp.stack([place, bit, core, first, deep]).astype(jnp.int32)
    start = (2 * bit + core) * quarter

    tok = tokens[0]
    dy = out_cotangent[0]

    piece = jnp.stack(
        [
            lax.dynamic_slice_in_dim(w, start, quarter, 0)
            for w in (w_query, w_key, w_value)
        ]
    )
    piece0 = to_span(piece)
    piece1 = to_seq(piece0, 2)
    pieces = (piece0, piece1, to_seq(piece0, 1), to_seq(piece1, 1))
    tok_oth = to_span(tok)

    small = jnp.concatenate(
        [
            jnp.stack(
                [
                    norm1_gain,
                    norm1_bias,
                    b_query,
                    b_key,
                    b_value,
                    norm2_gain,
                    norm2_bias,
                    b_out,
                    b_down,
                ]
            ),
            b_up.reshape(4, half),
        ]
    )
    small_oth = to_span(small)
    small_full = jnp.where(
        place == 0,
        jnp.concatenate([small, small_oth], axis=1),
        jnp.concatenate([small_oth, small], axis=1),
    ).astype(F32)
    vec_one = jnp.pad(small_full[:5], ((0, 3), (0, 0)))
    vec_two = jnp.pad(small_full[5:9], ((0, 4), (0, 0)))
    bup = jnp.concatenate([small_full[9:, :half], small_full[9:, half:]])

    out_piece = lax.dynamic_slice_in_dim(after(w_out, piece0), start, quarter, 0)
    up_piece = lax.dynamic_slice_in_dim(after(w_up, piece0), start, quarter, 0)
    up_piece = up_piece.reshape(quarter, 4, 2, half).transpose(2, 1, 0, 3)
    down_piece = lax.dynamic_slice_in_dim(
        after(w_down, piece0).reshape(4, half, width), start, quarter, 1
    )
    down_piece = [down_piece[0::2], down_piece[1::2]]
    out0 = to_span(out_piece)
    up0 = [to_span(up_piece[0]), None]
    down0 = [to_span(down_piece[0]), None]
    up_b, down_b = to_span(up_piece[1]), to_span(down_piece[1])

    quarter_dim = HEAD_DIM // 2
    here = jnp.arange(rows, dtype=jnp.int32)
    places = jnp.concatenate([place * rows + here, (1 - place) * rows + here]) - first
    rates = jnp.power(
        jnp.float32(10000.0), -jnp.arange(quarter_dim, dtype=F32) / quarter_dim
    )
    angle = places.astype(F32)[:, None] * jnp.tile(rates, 4)[None, :]
    sign = jnp.tile(jnp.repeat(jnp.array([-1.0, 1.0], F32), quarter_dim), 2)
    cos = jnp.cos(angle)
    sin = jnp.sin(angle) * sign[None, :]

    n1t, query, keys, values, wall = qkv(
        scal, tok, tok_oth, vec_one, cos, sin, (w_query, w_key, w_value), pieces
    )
    out0, up_a = after(out0, n1t), after(up0[0], n1t)
    out_x, up_x = to_seq(out0, 2), to_seq(up_a, 2)
    part = attend(scal, after(query, out0, up_a), keys, values, 0)
    out_x, down_a = after(out_x, part[0]), after(down0[0], part[0])
    down_x = to_seq(down_a, 2)
    outs = (out0, out_x, to_seq(after(out0, part[0]), 1), to_seq(out_x, 1))
    up_core, down_core = to_seq(after(up_a, part[0]), 1), to_seq(down_a, 1)
    up_b, down_b = after(up_b, part[0]), after(down_b, part[0])
    up_bx, down_bx = to_seq(up_b, 2), to_seq(down_b, 2)
    up_bc, down_bc = to_seq(up_b, 1), to_seq(down_b, 1)
    mixed, lse = attend(
        scal, after(query, out_x, down_a, up_b, down_b), keys, values, width // 256, part
    )
    up_x, down_x = after(up_x, mixed), after(down_x, mixed)
    ups = (up_a, up_x, up_core, to_seq(up_x, 1))
    downs = (down_a, down_x, down_core, to_seq(down_x, 1))
    hidden, normed, normed_t, wo = hidden_rows(
        scal, after(tok, up_x, down_x), mixed, vec_two, w_out, outs
    )
    up_bx, down_bx = after(up_bx, hidden), after(down_bx, hidden)
    ups = ups + (up_b, up_bx, up_bc, to_seq(up_bx, 1))
    downs = downs + (down_b, down_bx, down_bc, to_seq(down_bx, 1))
    layer_out, dh, branch, sdown, sup, kdown, kup, gbup, small_two = ffn(
        scal, mixed, dy, vec_two, bup, hidden, normed, normed_t, w_up, w_down, (*ups, *downs)
    )

    def deeper(item):
        return item.reshape(2, 2, 2, 2, *item.shape[3:])

    got_up, got_down = to_seq(sup, 1), to_seq(sdown, 1)
    do = out_back(scal, branch, wo)
    send_up, ups = split_send([deeper(kup), deeper(after(got_up, do))])
    got_up = to_span(send_up)
    send_down, downs = split_send([deeper(kdown), deeper(after(got_down, send_up))])
    got_down = to_seq(send_down, 2)

    def back(theirs, dout):
        return attend_back(
            scal, query, keys, values, mixed, dout, lse, cos, sin, n1t, theirs
        )

    split = (2, 2, 2, 3, half // 8, half)
    back_one = back(1, after(do, send_up, send_down))
    send, keep_one = back_one[4:]
    recv = to_seq(send, 1)
    (other,) = other_rows(scal, wall, back_one)
    send_over, over = split_send([keep_one.reshape(split), after(recv, other).reshape(split)])
    got_over = to_span(send_over)
    send_up, ups = split_send(ups + [after(got_up, send_over)])
    got_up = to_seq(send_up, 2)
    back_two = back(0, after(do, send_over, send_up))
    send, keep = back_two[4:]
    recv = to_seq(send, 1)
    send_over = add_low(*over, after(got_over, send))
    over_x = to_seq(send_over, 2)
    send_down, downs = split_send(downs + [after(got_down, send_over)])
    got_down = to_span(send_down)
    send_up, ups = split_send(ups + [after(got_up, send_down)])
    got_up = to_seq(send_up, 4)
    dn_oth, other_sum = other_rows(scal, after(wall, send_up), back_two, other, tok_oth)
    line = Line()
    line.put(dn_oth)
    send_proj, projs = split_send([item.reshape(split) for item in (keep, line.take(recv))])
    got_proj = to_span(line.put(send_proj))
    send_up, ups = split_send(ups + [line.take(got_up)])
    got_up = to_seq(line.put(send_up), 8)
    dn_own, small, small_oth = own_rows(
        scal, after(wall, send_up), back_two, back_one, tok,
        other_sum, back_one[3], back_two[3], small_two, gbup,
    )
    line.put(dn_own)
    dn_recv = to_span(after(dn_oth, dn_own))
    got_small = to_span(small_oth)

    send_down, downs = split_send(downs + [line.take(got_down)])
    got_down = to_seq(line.put(send_down), 4)
    projs = [item.reshape(4, *split[3:]) for item in projs + [line.take(got_proj), over_x]]
    sends = [add_low(*[item[d] for item in projs]) for d in range(1, 4)]
    got_proj = [to_seq(line.put(item), link) for item, link in zip(sends, (8, 4, 12))]
    up = line.put(reduce_rest(add_low(*ups, line.take(got_up))))
    got_up = to_seq(up, 8)
    small = line.put(small + line.take(got_small))
    got_small = to_seq(small, 1)
    send_down, downs = split_send(downs + [line.take(got_down)])
    got_down = to_seq(line.put(send_down), 8)
    proj = [item[0] for item in projs] + [line.take(got_proj[0]), *got_proj[1:]]
    proj = line.put(reduce_rest(add_low(*proj)))
    got_proj = [to_seq(proj, 8), to_seq(proj, 4), to_seq(proj, 12)]
    up = line.put(jnp.concatenate([up, line.take(got_up)]))
    got_up = to_seq(up, 4)
    small = small + line.take(got_small)
    for link in rest_links():
        small = small + to_seq(small, link)
    small = high_low(small)
    down = reduce_rest(add_low(*downs, line.take(got_down)))
    down = line.put(jnp.concatenate([down, small]))
    got_down = to_seq(down, 8)
    up = line.put(jnp.concatenate([up, line.take(got_up)]))
    up_x, up_core = to_seq(up, 2), to_seq(up, 1)
    proj = line.put(jnp.stack([proj, line.take(got_proj[0]), *got_proj[1:]]))
    proj_x, proj_core = to_seq(proj, 2), to_seq(proj, 1)

    def ride(mine, got):
        count = mine.shape[0] - small.shape[0]
        total = high_low(sum_of(mine[count:]) + sum_of(got[count:]))
        return jnp.concatenate([mine[:count], got[:count], total])

    down = line.put(ride(down, line.take(got_down)))
    got_down = to_seq(down, 4)
    input_grad = line.put(input_grads(tok, dn_own, line.take(dn_recv), dh, vec_one))
    up_x = line.put(line.take(up_x))
    ups = (up, up_x, up_core, to_seq(up_x, 1))
    proj_x = line.put(line.take(proj_x))
    projs = (proj, proj_x, proj_core, to_seq(proj_x, 1))
    down = line.put(ride(down, line.take(got_down)))
    down_x, down_core = to_seq(down, 2), to_seq(down, 1)
    up_grad = finish_up(scal, ups)
    proj = finish_proj(scal, [line.take(projs[0]), *projs[1:]])
    down_x = after(line.take(down_x), up_grad, proj[0])
    count = down.shape[0] - small.shape[0]
    total = sum_of(down[count:]) + sum_of(down_x[count:])
    down_grad, out_grad = finish_down(scal, (down, down_x, down_core, to_seq(down_x, 1)))

    return (
        layer_out[None],
        input_grad[None],
        total[0],
        total[1],
        proj[0],
        total[2],
        proj[1],
        total[3],
        proj[2],
        total[4],
        out_grad,
        total[7],
        total[5],
        total[6],
        up_grad,
        total[9:13].reshape(-1),
        down_grad,
        total[8],
    )


def solution(mesh):
    row, col = P(None, ("seq", "span"), None), P(None, "seq")
    vec, mat = P("span"), P("span", None)
    weights = (vec, vec, mat, vec, mat, vec, mat, vec, mat, vec, vec, vec, mat, vec, mat, vec)
    return jax.shard_map(
        shards,
        mesh=mesh,
        in_specs=(row, row, col, col) + weights,
        out_specs=(row, row) + weights,
        check_vma=False,
    )
```

```python
import functools

import jax
import jax.numpy as jnp
from jax import lax
from jax.experimental import pallas as pl
from jax.experimental.pallas import tpu as pltpu
from jax.sharding import PartitionSpec as P

HEADS = 12
HEAD_DIM = 64
SCALE = HEAD_DIM ** (-0.5)
F32 = jnp.float32
BF16 = jnp.bfloat16
VMEM_BYTES = 60 * 1024 * 1024
COST = pl.CostEstimate(flops=10**11, bytes_accessed=1024, transcendentals=0)


def deep_of(spot):
    return (spot >> 1) | ((spot & 1) << 1)


def dot(left, right, dim_l, dim_r):
    return lax.dot_general(
        left, right, (((dim_l,), (dim_r,)), ((), ())), preferred_element_type=F32
    )


def swap_halves(rows):
    half = rows.shape[-1] // 2
    return jnp.concatenate([rows[:, half:], rows[:, :half]], axis=1)


def own_first(rows, place):
    return jnp.where(place == 0, rows, swap_halves(rows))


def half_swap(tile):
    lane = lax.broadcasted_iota(jnp.int32, tile.shape, 1)
    width = tile.shape[1]
    return jnp.where(
        lane % HEAD_DIM < HEAD_DIM // 2,
        pltpu.roll(tile, width - HEAD_DIM // 2, 1),
        pltpu.roll(tile, HEAD_DIM // 2, 1),
    )


def params(**kw):
    return pltpu.CompilerParams(vmem_limit_bytes=VMEM_BYTES, **kw)


def vmem():
    return pl.BlockSpec(memory_space=pltpu.VMEM)


def anywhere():
    return pl.BlockSpec(memory_space=pl.ANY)


def qkv_kernel(
    scal, own_ref, oth_ref, vec_ref, cos_ref, sin_ref, wq, wk, wv, p0, p1, p2, p3,
    n1t_ref, q_ref, k_ref, v_ref, wall_ref, sems,
):
    step = pl.program_id(0)
    place = scal[0]
    half = wq.shape[0]

    @pl.when(step == 0)
    def _():
        copies = []
        for j, weight in enumerate((wq, wk, wv)):
            target = wall_ref.at[j]
            own = (weight, target.at[pl.ds(0, half)])
            copies += piece_copies(
                own, (p0, p1, p2, p3), scal, lambda p, j=j: p.at[j], target, half
            )
        wait_all(start_all(copies, sems, 0))

    rows = jnp.where(step < 2, own_ref[...], oth_ref[...]).astype(F32)
    center = rows - jnp.mean(rows, axis=1, keepdims=True)
    spread = jnp.mean(center * center, axis=1, keepdims=True)
    normed = center * lax.rsqrt(spread + 1e-05) * vec_ref[0:1] + vec_ref[1:2]
    normed = own_first(normed, place).astype(BF16)
    n1t_ref[...] = normed.T

    def rotated(j, ref, factor):
        flat = dot(normed, wall_ref[j], 1, 0) + vec_ref[2 + j : 3 + j]
        for t in range(flat.shape[1] // 128):
            tile = flat[:, t * 128 : (t + 1) * 128]
            turned = (tile * cos_ref[...] + half_swap(tile) * sin_ref[...]).astype(BF16)
            ref[:, t * 128 : (t + 1) * 128] = turned * factor if factor != 1 else turned

    @pl.when(step < 2)
    def _():
        rotated(0, q_ref, SCALE)

    rotated(1, k_ref, 1)
    v_ref[...] = (dot(normed, wall_ref[2], 1, 0) + vec_ref[4:5]).astype(BF16)


def qkv(scal, own, oth, vec, cos, sin, weights, pieces):
    rows, width = own.shape
    block = rows // 2
    grid_spec = pltpu.PrefetchScalarGridSpec(
        num_scalar_prefetch=1,
        grid=(4,),
        in_specs=[
            pl.BlockSpec((block, width), lambda i, s: (jnp.minimum(i, 1), 0)),
            pl.BlockSpec((block, width), lambda i, s: (jnp.maximum(i - 2, 0), 0)),
            pl.BlockSpec(vec.shape, lambda i, s: (0, 0)),
            pl.BlockSpec((block, 128), lambda i, s: (i, 0)),
            pl.BlockSpec((block, 128), lambda i, s: (i, 0)),
        ]
        + [anywhere()] * 7,
        out_specs=[
            pl.BlockSpec((width, block), lambda i, s: (0, i)),
            pl.BlockSpec((block, width), lambda i, s: (jnp.minimum(i, 1), 0)),
            pl.BlockSpec((block, width), lambda i, s: (i, 0)),
            pl.BlockSpec((block, width), lambda i, s: (i, 0)),
            pl.BlockSpec((3, width, width), lambda i, s: (0, 0, 0)),
        ],
        scratch_shapes=[pltpu.SemaphoreType.DMA((15,))],
    )
    shape = jax.ShapeDtypeStruct
    return pl.pallas_call(
        qkv_kernel,
        grid_spec=grid_spec,
        out_shape=[
            shape((width, 2 * rows), BF16),
            shape((rows, width), BF16),
            shape((2 * rows, width), BF16),
            shape((2 * rows, width), BF16),
            shape((3, width, width), BF16),
        ],
        compiler_params=params(),
        cost_estimate=COST,
        name="qkv",
    )(scal, own, oth, vec, cos, sin, *weights, *pieces)


def key_bias(scal, keys):
    place, first = scal[0], scal[3]
    half = keys // 2
    row = lax.broadcasted_iota(jnp.int32, (keys, 128), 0)
    where = jnp.where(row < half, place * half + row, (1 - place) * half + row - half)
    return jnp.where(where < first, -1e30, 0.0).astype(BF16)


def masked_pair(head, keys, query, bias):
    lane_k = lax.broadcasted_iota(jnp.int32, keys.shape, 1)
    lane_q = lax.broadcasted_iota(jnp.int32, query.shape, 1)
    spot = (1 - head) * HEAD_DIM
    zero = jnp.zeros((), BF16)
    keys = jnp.where(
        lane_k // HEAD_DIM == head, keys, jnp.where(lane_k == spot, bias, zero)
    )
    query = jnp.where(
        lane_q // HEAD_DIM == head,
        query,
        jnp.where(lane_q == spot, jnp.ones((), BF16), zero),
    )
    return keys, query


def attend_kernel(scal, q_ref, k_ref, v_ref, *refs):
    o_ref, lse_ref = refs[-2:]
    keys, values, query = k_ref[...], v_ref[...], q_ref[...]
    bias = key_bias(scal, keys.shape[0])
    values_t = values.T
    outs = []
    for head in range(2):
        keys_m, query_m = masked_pair(head, keys, query, bias)
        scores = dot(keys_m, query_m, 1, 1)
        top = jnp.max(scores, axis=0, keepdims=True)
        expo = jnp.exp(scores - top)
        total = jnp.sum(expo, axis=0, keepdims=True)
        mixed = dot(
            values_t[head * HEAD_DIM : (head + 1) * HEAD_DIM], expo.astype(BF16), 1, 0
        )
        outs.append(mixed / total)
        lse_ref[0, head : head + 1] = top + jnp.log(total)
    o_ref[...] = jnp.concatenate(outs, axis=0).T.astype(BF16)


def attend(scal, query, keys, values, begin, earlier=()):
    rows, width = query.shape
    span = keys.shape[0]
    pairs = width // 256
    grid_spec = pltpu.PrefetchScalarGridSpec(
        num_scalar_prefetch=1,
        grid=(pairs,),
        in_specs=[
            pl.BlockSpec((rows, 128), lambda i, s: (0, i + begin)),
            pl.BlockSpec((span, 128), lambda i, s: (0, i + begin)),
            pl.BlockSpec((span, 128), lambda i, s: (0, i + begin)),
        ]
        + [anywhere()] * len(earlier),
        out_specs=[
            pl.BlockSpec((rows, 128), lambda i, s: (0, i + begin)),
            pl.BlockSpec((1, 8, rows), lambda i, s: (i + begin, 0, 0)),
        ],
    )
    return pl.pallas_call(
        attend_kernel,
        grid_spec=grid_spec,
        out_shape=[
            jax.ShapeDtypeStruct((rows, width), BF16),
            jax.ShapeDtypeStruct((2 * pairs, 8, rows), F32),
        ],
        input_output_aliases={4: 0, 5: 1} if earlier else {},
        compiler_params=params(),
        cost_estimate=COST,
        name="attend",
    )(scal, query, keys, values, *earlier)


def attend_back_kernel(
    scal, q_ref, k_ref, v_ref, o_ref, do_ref, lse_ref, cos_ref, sin_ref, n1t_ref,
    dq_ref, dk_ref, dv_ref, bias_ref, send_ref, keep_ref, g_s,
):
    step = pl.program_id(0)
    pairs = dq_ref.shape[1] // 128

    @pl.when(step < pairs)
    def _():
        at = pl.ds(pl.multiple_of(step * 128, 128), 128)
        keys, values, query, dout = k_ref[...], v_ref[...], q_ref[...], do_ref[...]
        rows = query.shape[0]
        bias = key_bias(scal, keys.shape[0])
        keys_t = keys.T
        product = (dout.astype(F32) * o_ref[...].astype(F32)).T
        lane = lax.broadcasted_iota(jnp.int32, values.shape, 1)
        parts = []
        for head in range(2):
            keys_m, query_m = masked_pair(head, keys, query, bias)
            values_m = jnp.where(lane // HEAD_DIM == head, values, jnp.zeros((), BF16))
            inner = jnp.sum(
                product[head * HEAD_DIM : (head + 1) * HEAD_DIM], axis=0, keepdims=True
            )
            probs = jnp.exp(dot(keys_m, query_m, 1, 1) - lse_ref[0, head : head + 1])
            grad = dot(values_m, dout, 1, 1)
            score_grad = (probs * (grad - inner)).astype(BF16)
            dv = dot(probs.astype(BF16), dout, 1, 0)
            dk = dot(score_grad, query, 1, 0)
            dq = dot(keys_t[head * HEAD_DIM : (head + 1) * HEAD_DIM], score_grad, 1, 0)
            parts.append((dq, dk, dv))
        dq = (jnp.concatenate([parts[0][0], parts[1][0]], axis=0).T * SCALE).astype(BF16)
        dk = jnp.where(lane // HEAD_DIM == 0, parts[0][1], parts[1][1]).astype(BF16)
        dv = jnp.where(lane // HEAD_DIM == 0, parts[0][2], parts[1][2]).astype(BF16)
        dq, dk = dq.astype(F32), dk.astype(F32)
        dq = (dq * cos_ref[:rows] - half_swap(dq) * sin_ref[:rows]).astype(BF16)
        dk = (dk * cos_ref[...] - half_swap(dk) * sin_ref[...]).astype(BF16)
        dq_ref[:, at] = dq
        dk_ref[:, at] = dk
        dv_ref[:, at] = dv
        bias_ref[0:1, at] = jnp.sum(dq.astype(F32), axis=0, keepdims=True)
        bias_ref[1:2, at] = jnp.sum(dk.astype(F32), axis=0, keepdims=True)
        bias_ref[2:3, at] = jnp.sum(dv.astype(F32), axis=0, keepdims=True)

    @pl.when(step == pairs)
    def _():
        core, deep = scal[2], scal[4]
        half = dq_ref.shape[1]
        size = half // 8
        for w, ref in enumerate((dq_ref, dk_ref, dv_ref)):
            g_s[w] = dot(n1t_ref[:, : ref.shape[0]], ref[...], 1, 0).astype(BF16)
        for w in range(3):
            for s in range(2):
                for d in range(4):
                    row = s * half + (deep ^ deep_of(d)) * size
                    for out, mine in ((send_ref, 1 - core), (keep_ref, core)):
                        at = pl.multiple_of(row + mine * 4 * size, 16)
                        out[s, d, w] = g_s[w, pl.ds(at, size)]


def attend_back(scal, query, keys, values, mixed, dout, lse, cos, sin, n1t, theirs):
    rows, width = query.shape[0], query.shape[1] // 2
    span = keys.shape[0]
    pairs = width // 128

    def at(i, s):
        return jnp.minimum(i, pairs - 1) + pairs * (1 - s[1] if theirs else s[1])

    def fixed(shape):
        return pl.BlockSpec(shape, lambda i, s: tuple(0 for _ in shape))

    few = pl.BlockSpec((rows, 128), lambda i, s: (0, at(i, s)))
    many = pl.BlockSpec((span, 128), lambda i, s: (0, at(i, s)))
    buffer = (2, 4, 3, width // 8, width)
    outs = [(rows, width), (span, width), (span, width), (8, width), buffer, buffer]
    grid_spec = pltpu.PrefetchScalarGridSpec(
        num_scalar_prefetch=1,
        grid=(pairs + 1,),
        in_specs=[few, many, many, few, few]
        + [pl.BlockSpec((1, 8, rows), lambda i, s: (at(i, s), 0, 0))]
        + [fixed((span, 128)), fixed((span, 128)), fixed(n1t.shape)],
        out_specs=[fixed(item) for item in outs],
        scratch_shapes=[pltpu.VMEM((3, 2 * width, width), BF16)],
    )
    return pl.pallas_call(
        attend_back_kernel,
        grid_spec=grid_spec,
        out_shape=[
            jax.ShapeDtypeStruct(item, F32 if n == 3 else BF16) for n, item in enumerate(outs)
        ],
        compiler_params=params(),
        cost_estimate=COST,
        name="attend_back",
    )(scal, query, keys, values, mixed, dout, lse, cos, sin, n1t)


def norm_stats(rows):
    center = rows - jnp.mean(rows, axis=1, keepdims=True)
    spread = jnp.mean(center * center, axis=1, keepdims=True)
    return center, lax.rsqrt(spread + 1e-05)


def norm_back(rows, grad, gain):
    center, rate = norm_stats(rows)
    hat = center * rate
    scaled = grad * gain
    out = rate * (
        scaled
        - jnp.mean(scaled, axis=1, keepdims=True)
        - hat * jnp.mean(scaled * hat, axis=1, keepdims=True)
    )
    return (
        out,
        jnp.sum(grad * hat, axis=0, keepdims=True),
        jnp.sum(grad, axis=0, keepdims=True),
    )


def piece_copies(own, pieces, scal, select, target, base):
    bit, core = scal[1], scal[2]
    p0, p1, p2, p3 = pieces
    spots = (
        (p0, 2 * bit + core),
        (p1, 2 * (1 - bit) + core),
        (p2, 2 * bit + 1 - core),
        (p3, 2 * (1 - bit) + 1 - core),
    )
    copies = [] if own is None else [own]
    for src, index in spots:
        part = select(src)
        rows = part.shape[0]
        start = pl.multiple_of(base + index * rows, 32)
        copies.append((part, target.at[pl.ds(start, rows)]))
    return copies


def load_out(scal, wo_own, pieces, wo_s):
    half = wo_own.shape[0]
    own = (wo_own, wo_s.at[pl.ds(0, half)])
    return piece_copies(own, pieces, scal, lambda p: p, wo_s, half)


def load_chunk(scal, part, t, up_own, down_own, ups, downs, chunk, up_s, down_s):
    place = scal[0]
    core = scal[2] if t == 1 else 1 - scal[2]
    half = up_own.shape[0]
    copies = []
    for n, span in enumerate((1 - place, place)):
        index = 2 * span + core
        column = pl.multiple_of((2 * index + part) * half, 128)
        target = up_s.at[chunk, :, pl.ds(n * half, half)]
        own = (up_own.at[:, pl.ds(column, half)], target.at[pl.ds(0, half)])
        copies += piece_copies(own, ups, scal, lambda p, index=index: p.at[index], target, half)
    start = pl.multiple_of((2 * core + part) * half, 128)
    copies.append((down_own.at[pl.ds(start, half)], down_s.at[chunk, pl.ds(half, half)]))
    copies += piece_copies(None, downs, scal, lambda p: p.at[core], down_s.at[chunk], 0)
    return copies


def start_all(copies, sems, base):
    started = [
        pltpu.make_async_copy(src, dst, sems.at[base + n]) for n, (src, dst) in enumerate(copies)
    ]
    for copy in started:
        copy.start()
    return started


def wait_all(started):
    for copy in started:
        copy.wait()


def chunk_spots(scal, t, part):
    place = scal[0]
    core = scal[2] if t == 1 else 1 - scal[2]
    return [2 * (2 * span + core) + part for span in (1 - place, place)]


def product_tasks(n, chunk, dy_ref, n2_ref, up_s, down_s, u_s, da_s):
    def one(c):
        at = slice(c, c + 256)
        u_s[n, :, at] = dot(n2_ref[...], up_s[chunk, :, at], 1, 0)

    def two(c):
        at = slice(c, c + 256)
        da_s[n, :, at] = dot(dy_ref[...], down_s[chunk, at], 1, 1)

    columns = range(0, u_s.shape[2], 256)
    return [functools.partial(task, c) for task in (one, two) for c in columns]


def element_tasks(scal, n, t, part, bup_ref, u_s, da_s, a_s, du_s, gbup_ref):
    rows, width = a_s.shape[1:]
    half = width // 2
    block = rows // 16
    spots = chunk_spots(scal, t, part)
    sums = [jnp.zeros((8, width), F32)]

    def one(r):
        at = slice(r, r + block)
        bias = jnp.concatenate([bup_ref[pl.ds(n, 1)] for n in spots], axis=1)
        inner = u_s[n, at] + bias
        phi = 0.5 + 0.5 * lax.erf(inner * 0.7071067811865476)
        slope = phi + inner * (0.3989422804014327 * jnp.exp(-0.5 * inner * inner))
        a_s[n, at] = (inner * phi).astype(BF16)
        du = (da_s[n, at] * slope).astype(BF16)
        du_s[n, at] = du
        sums[0] = sums[0] + jnp.sum(du.astype(F32).reshape(block // 8, 8, width), axis=0)
        if r + block == rows:
            total = jnp.sum(sums[0], axis=0, keepdims=True)
            for j, row in enumerate(spots):
                gbup_ref[pl.ds(row, 1)] = total[:, j * half : (j + 1) * half]

    return [functools.partial(one, r) for r in range(0, rows, block)]


def grad_tasks(
    scal, n, chunk, part, dy_ref, n2t_ref, up_s, down_s, acc_s, dacc_s, a_s, du_s, down_out, up_out, g_s
):
    place, bit, deep = scal[0], scal[1], scal[4]
    half = g_s.shape[1] // 2
    size = half // 4
    rows = slice(part * size, (part + 1) * size)

    def layer(c):
        at = slice(c, c + 256)
        acc_s[:, at] += dot(a_s[n], down_s[chunk, :, at], 1, 0)

    def back(c):
        at = slice(c, c + 256)
        dacc_s[:, at] += dot(du_s[n], up_s[chunk, at], 1, 1)

    def down(c):
        at = slice(c, c + 256)
        g_s[0, :, at] = dot(a_s[n], dy_ref[:, at], 0, 0).astype(BF16)

    def up(c):
        at = slice(c, c + 256)
        g_s[1, :, at] = dot(n2t_ref[...], du_s[n, :, at], 1, 0).astype(BF16)

    def place_down():
        for s in range(2):
            for k in range(2):
                at = pl.multiple_of((bit if k == 0 else 1 - bit) * half, 128)
                for d in range(4):
                    row = (1 - s) * half + (deep ^ deep_of(d)) * size
                    row = pl.multiple_of(row, 32)
                    down_out[k, s, d, rows] = g_s[0, pl.ds(row, size), pl.ds(at, half)]

    def place_up():
        for s in range(2):
            for k in range(2):
                column = bit if k == 0 else 1 - bit
                at = pl.multiple_of(jnp.where(column == place, half, 0), 128)
                for d in range(4):
                    row = pl.multiple_of(s * half + (deep ^ deep_of(d)) * size, 32)
                    up_out[s, k, d, rows] = g_s[1, pl.ds(row, size), pl.ds(at, half)]

    columns = range(0, acc_s.shape[1], 256)
    tasks = []
    for task, then in ((down, place_down), (up, place_up), (layer, None), (back, None)):
        tasks += [functools.partial(task, c) for c in columns]
        if then is not None:
            tasks.append(then)
    return tasks


def interleave(first, second):
    done = 0
    for i, task in enumerate(first):
        task()
        upto = (i + 1) * len(second) // len(first)
        for other in second[done:upto]:
            other()
        done = upto


def hidden_kernel(
    scal, x_ref, o_ref, vec_ref, wo_own, p0, p1, p2, p3, h_ref, n2_ref, n2t_ref, wo_s, sems
):
    place = scal[0]
    rows = x_ref.shape[0]
    block = rows // 8
    wait_all(start_all(load_out(scal, wo_own, (p0, p1, p2, p3), wo_s), sems, 0))
    h_ref[...] = dot(own_first(o_ref[...], place), wo_s[...], 1, 0)
    for r in range(0, rows, block):
        at = slice(r, r + block)
        hidden = h_ref[at] + (x_ref[at].astype(F32) + vec_ref[2:3])
        h_ref[at] = hidden
        center, rate = norm_stats(hidden)
        normed = center * rate * vec_ref[0:1] + vec_ref[1:2]
        n2_ref[at] = own_first(normed, place).astype(BF16)
    n2t_ref[...] = n2_ref[...].T


def hidden_rows(scal, tokens, mixed, vec, w_out, pieces):
    rows, width = tokens.shape
    shape = jax.ShapeDtypeStruct
    return pl.pallas_call(
        hidden_kernel,
        in_specs=[pl.BlockSpec(memory_space=pltpu.SMEM)] + [vmem()] * 3 + [anywhere()] * 5,
        out_specs=[vmem()] * 4,
        out_shape=[
            shape((rows, width), F32),
            shape((rows, width), BF16),
            shape((width, rows), BF16),
            shape((width, width), BF16),
        ],
        scratch_shapes=[pltpu.SemaphoreType.DMA((5,))],
        compiler_params=params(),
        cost_estimate=COST,
        name="hidden_rows",
    )(scal, tokens, mixed, vec, w_out, *pieces)


def ffn_kernel(
    scal, o_ref, dy_ref, vec_ref, bup_ref, h_ref, n2_ref, n2t_ref, up_own, down_own, *refs
):
    pieces, refs = refs[:16], refs[16:]
    (
        out_ref, dh_ref, branch_ref, sdown_ref, sup_ref, kdown_ref, kup_ref, gbup_ref, small_ref,
        u_s, da_s, a_s, du_s, up_s, down_s, g_s, acc_s, dacc_s, go_s, sems,
    ) = refs
    place, bit, core, deep = scal[0], scal[1], scal[2], scal[4]
    rows, width = dy_ref.shape
    half = width // 2
    block = rows // 8
    order = [(part, t) for t in range(2) for part in range(2)]
    waits = []
    for chunk, (part, t) in enumerate(order):
        ups, downs = pieces[4 * part : 4 * part + 4], pieces[8 + 4 * part : 12 + 4 * part]
        copies = load_chunk(
            scal, part, t, up_own, down_own, ups, downs, chunk, up_s, down_s
        )
        waits.append(start_all(copies, sems, 15 * chunk))
    acc_s[...] = h_ref[...] + vec_ref[3:4]
    dacc_s[...] = jnp.zeros_like(dacc_s)
    def products(chunk):
        wait_all(waits[chunk])
        return product_tasks(chunk % 2, chunk, dy_ref, n2_ref, up_s, down_s, u_s, da_s)

    def grads(chunk):
        part, t = order[chunk]
        down_out, up_out = (kdown_ref, kup_ref) if t == 1 else (sdown_ref, sup_ref)
        return grad_tasks(
            scal, chunk % 2, chunk, part, dy_ref, n2t_ref, up_s, down_s, acc_s, dacc_s, a_s, du_s,
            down_out, up_out, g_s,
        )

    for task in products(0):
        task()
    for chunk, (part, t) in enumerate(order):
        tasks = products(chunk + 1) if chunk + 1 < len(order) else []
        tasks = tasks + (grads(chunk - 1) if chunk > 0 else [])
        interleave(
            element_tasks(scal, chunk % 2, t, part, bup_ref, u_s, da_s, a_s, du_s, gbup_ref), tasks
        )
    for task in grads(len(order) - 1):
        task()
    sums = [jnp.zeros((1, width), F32) for _ in range(4)]
    for r in range(0, rows, block):
        at = slice(r, r + block)
        out_ref[at] = acc_s[at].astype(BF16)
        grad = own_first(dacc_s[at], place)
        dy = dy_ref[at].astype(F32)
        part, gain_sum, shift_sum = norm_back(h_ref[at], grad, vec_ref[0:1])
        dh = dy + part
        dh_ref[at] = dh
        branch = dh.astype(BF16)
        branch_ref[at] = branch
        terms = (
            gain_sum,
            shift_sum,
            jnp.sum(branch.astype(F32), axis=0, keepdims=True),
            jnp.sum(dy, axis=0, keepdims=True),
        )
        sums = [old + new for old, new in zip(sums, terms)]
    for n, item in enumerate(sums):
        small_ref[n : n + 1] = item
    go_s[...] = dot(own_first(o_ref[...], place), branch_ref[...], 0, 0)
    size = half // 8
    for s in range(2):
        for k in range(2):
            column = pl.multiple_of((bit if k == 0 else 1 - bit) * half, 128)
            for d in range(4):
                row = s * half + (deep ^ deep_of(d)) * size
                for out, mine in ((sdown_ref, 1 - core), (kdown_ref, core)):
                    at = pl.multiple_of(row + mine * 4 * size, 16)
                    out[k, s, d, 4 * size :] = go_s[pl.ds(at, size), pl.ds(column, half)].astype(BF16)


def ffn(scal, mixed, dy, vec, bup, hidden, normed, normed_t, w_up, w_down, pieces):
    rows, width = mixed.shape
    half = width // 2
    shape = jax.ShapeDtypeStruct
    down = shape((2, 2, 4, half // 2 + half // 8, half), BF16)
    up = shape((2, 2, 4, half // 2, half), BF16)
    return pl.pallas_call(
        ffn_kernel,
        in_specs=[pl.BlockSpec(memory_space=pltpu.SMEM)] + [vmem()] * 7 + [anywhere()] * 18,
        out_specs=[vmem()] * 9,
        out_shape=[
            shape((rows, width), BF16),
            shape((rows, width), F32),
            shape((rows, width), BF16),
            down,
            up,
            down,
            up,
            shape((8, half), F32),
            shape((8, width), F32),
        ],
        scratch_shapes=[
            pltpu.VMEM((2, rows, width), F32),
            pltpu.VMEM((2, rows, width), F32),
            pltpu.VMEM((2, rows, width), BF16),
            pltpu.VMEM((2, rows, width), BF16),
            pltpu.VMEM((4, width, width), BF16),
            pltpu.VMEM((4, width, width), BF16),
            pltpu.VMEM((2, width, width), BF16),
            pltpu.VMEM((rows, width), F32),
            pltpu.VMEM((rows, width), F32),
            pltpu.VMEM((width, width), F32),
            pltpu.SemaphoreType.DMA((60,)),
        ],
        compiler_params=params(),
        cost_estimate=COST,
        name="ffn",
    )(scal, mixed, dy, vec, bup, hidden, normed, normed_t, w_up, w_down, *pieces)


def out_back_kernel(scal, branch_ref, wo_ref, do_ref):
    do_ref[...] = own_first(dot(branch_ref[...], wo_ref[...], 1, 1), scal[0]).astype(BF16)


def out_back(scal, branch, wo):
    return pl.pallas_call(
        out_back_kernel,
        in_specs=[pl.BlockSpec(memory_space=pltpu.SMEM), vmem(), vmem()],
        out_specs=vmem(),
        out_shape=jax.ShapeDtypeStruct(branch.shape, BF16),
        compiler_params=params(),
        cost_estimate=COST,
        name="out_back",
    )(scal, branch, wo)


def columns_of(scal, theirs, half):
    return pl.ds(pl.multiple_of((1 - scal[1] if theirs else scal[1]) * half, 128), half)


def norm_products(scal, w_ref, parts, first):
    total = 0.0
    for theirs in range(2):
        for n, ref in enumerate(parts[theirs]):
            at = columns_of(scal, theirs, ref.shape[1])
            total = total + dot(ref[...], w_ref[first + n, :, at], 1, 1)
    return own_first(total, scal[0])


def norm_sums(x_ref, grad):
    block = grad.shape[0] // 4
    gain, shift = 0.0, 0.0
    for r in range(0, grad.shape[0], block):
        center, rate = norm_stats(x_ref[r : r + block].astype(F32))
        part = grad[r : r + block]
        gain = gain + jnp.sum(part * (center * rate), axis=0, keepdims=True)
        shift = shift + jnp.sum(part, axis=0, keepdims=True)
    return gain, shift


def fixed_spec(shape):
    return pl.BlockSpec(shape, lambda i, s: tuple(0 for _ in shape))


def other_kernel(scal, w_ref, dk_ref, dv_ref, *refs):
    theirs = len(refs) == 1
    at = columns_of(scal, theirs, dk_ref.shape[1])
    total = dot(dk_ref[...], w_ref[1, :, at], 1, 1) + dot(dv_ref[...], w_ref[2, :, at], 1, 1)
    if theirs:
        refs[0][...] = total
    else:
        earlier_ref, x_ref, out_ref, sum_ref = refs
        grad = own_first(total + earlier_ref[...], scal[0])
        out_ref[...] = grad.astype(BF16)
        gain, shift = norm_sums(x_ref, grad)
        sum_ref[0:1] = gain
        sum_ref[1:2] = shift


def other_rows(scal, wall, back, *rest):
    width = wall.shape[2]
    rows = back[1].shape[0] // 2
    part = pl.BlockSpec((rows, width // 2), lambda i, s: (1, 0))
    shapes = [((rows, width), BF16), ((8, width), F32)] if rest else [((rows, width), F32)]
    return pl.pallas_call(
        other_kernel,
        grid_spec=pltpu.PrefetchScalarGridSpec(
            num_scalar_prefetch=1,
            grid=(1,),
            in_specs=[fixed_spec(wall.shape), part, part] + [fixed_spec(item.shape) for item in rest],
            out_specs=[fixed_spec(item) for item, _ in shapes],
        ),
        out_shape=[jax.ShapeDtypeStruct(*item) for item in shapes],
        compiler_params=params(),
        cost_estimate=COST,
        name="other_rows",
    )(scal, wall, back[1], back[2], *rest)


def own_kernel(
    scal, w_ref, q1, k1, v1, q0, k0, v0, x_ref, other_sum, bias_one, bias_two, two_ref, bup_ref,
    out_ref, small_ref, send_ref,
):
    place, bit = scal[0], scal[1]
    half = x_ref.shape[1] // 2
    grad = norm_products(scal, w_ref, ((q1, k1, v1), (q0, k0, v0)), 0)
    out_ref[...] = grad
    gain, shift = norm_sums(x_ref, grad)
    ends = jnp.concatenate([gain, shift], axis=0) + other_sum[0:2]
    blank = jnp.zeros((3, half), F32)
    sides = []
    for n in range(2):
        at = slice(n * half, (n + 1) * half)
        same = bias_two[0:3] if n == 0 else bias_one[0:3]
        swap = bias_one[0:3] if n == 0 else bias_two[0:3]
        bias = jnp.where(bit == 0, same, swap)
        sides.append(
            jnp.concatenate(
                [ends[:, at], bias, two_ref[0:4, at], bup_ref[4 * n : 4 * n + 4], blank], axis=0
            )
        )
    small_ref[...] = jnp.where(place == 0, sides[0], sides[1])
    send_ref[...] = jnp.where(place == 0, sides[1], sides[0])


def own_rows(scal, wall, mine, theirs, *rest):
    rows, width = rest[0].shape
    part = fixed_spec((rows, width // 2))
    shapes = [(rows, width), (16, width // 2), (16, width // 2)]
    return pl.pallas_call(
        own_kernel,
        grid_spec=pltpu.PrefetchScalarGridSpec(
            num_scalar_prefetch=1,
            grid=(1,),
            in_specs=[fixed_spec(wall.shape)] + [part] * 6 + [fixed_spec(item.shape) for item in rest],
            out_specs=[fixed_spec(item) for item in shapes],
        ),
        out_shape=[jax.ShapeDtypeStruct(item, F32) for item in shapes],
        compiler_params=params(),
        cost_estimate=COST,
        name="own_rows",
    )(scal, wall, *mine[:3], *theirs[:3], *rest)


def input_kernel(x_ref, own_ref, recv_ref, dh_ref, vec_ref, out_ref):
    grad = own_ref[...] + recv_ref[...].astype(F32)
    part, _, _ = norm_back(x_ref[...].astype(F32), grad, vec_ref[0:1])
    out_ref[...] = (dh_ref[...] + part).astype(BF16)


def input_grads(tokens, dn_own, dn_recv, dh, vec):
    rows, width = tokens.shape
    tile = pl.BlockSpec((rows // 4, width), lambda i: (i, 0))
    return pl.pallas_call(
        input_kernel,
        grid=(4,),
        in_specs=[tile, tile, tile, tile, pl.BlockSpec(vec.shape, lambda i: (0, 0))],
        out_specs=tile,
        out_shape=jax.ShapeDtypeStruct((rows, width), BF16),
        compiler_params=params(),
        cost_estimate=COST,
        name="input_grads",
    )(tokens, dn_own, dn_recv, dh, vec)


def spot_of(scal, i):
    bit = jnp.where(i % 2 == 0, scal[1], 1 - scal[1])
    core = jnp.where(i < 2, scal[2], 1 - scal[2])
    return core, bit


def finish_down_kernel(scal, *refs):
    parts, (down_ref, out_ref) = refs[:4], refs[4:]
    step = pl.program_id(0)
    deep = scal[4]
    half = down_ref.shape[1]
    size = half // 4
    count = 2 * size + size // 2
    for i in range(4):

        @pl.when(step == i)
        def _(i=i):
            for d in range(4):
                start = d * count
                for part in range(2):
                    row = pl.multiple_of(part * half + (deep ^ deep_of(d)) * size, 32)
                    at = start + part * size
                    down_ref[pl.ds(row, size)] = parts[i][at : at + size].astype(F32)
                row = pl.multiple_of((deep ^ deep_of(d)) * (size // 2), 16)
                at = start + 2 * size
                out_ref[pl.ds(row, size // 2)] = parts[i][at : at + size // 2].astype(F32)


def finish_up_kernel(scal, *refs):
    parts, up_ref = refs[:4], refs[4]
    step = pl.program_id(0)
    deep = scal[4]
    half = up_ref.shape[0]
    size = half // 4
    for i in range(4):

        @pl.when(step == i)
        def _(i=i):
            for d in range(4):
                row = pl.multiple_of((deep ^ deep_of(d)) * size, 32)
                for part in range(2):
                    at = (2 * d + part) * size
                    up_ref[pl.ds(row, size), part * half : (part + 1) * half] = parts[i][
                        at : at + size
                    ].astype(F32)


def finish_call(body, scal, parts, out_specs, out_shape, name):
    return pl.pallas_call(
        body,
        grid_spec=pltpu.PrefetchScalarGridSpec(
            num_scalar_prefetch=1,
            grid=(4,),
            in_specs=[pl.BlockSpec(item.shape, lambda i, s: (0, 0)) for item in parts],
            out_specs=out_specs,
        ),
        out_shape=[jax.ShapeDtypeStruct(item, F32) for item in out_shape],
        compiler_params=params(),
        cost_estimate=COST,
        name=name,
    )(scal, *parts)


def finish_down(scal, parts):
    half = parts[0].shape[1]
    specs = [pl.BlockSpec((count, half), lambda i, s: spot_of(s, i)) for count in (2 * half, half // 2)]
    shapes = [(4 * half, 2 * half), (half, 2 * half)]
    return finish_call(finish_down_kernel, scal, parts, specs, shapes, "finish_down")


def finish_up(scal, parts):
    half = parts[0].shape[1]

    def at(i, s):
        core, bit = spot_of(s, i)
        return (0, 2 * bit + core)

    specs = [pl.BlockSpec((half, 2 * half), at)]
    return finish_call(finish_up_kernel, scal, parts, specs, [(half, 8 * half)], "finish_up")[0]


def finish_proj_kernel(scal, *refs):
    parts, outs = refs[:4], refs[4:]
    step = pl.program_id(0)
    deep = scal[4]
    size = outs[0].shape[0] // 4
    for i in range(4):

        @pl.when(step == i)
        def _(i=i):
            for d in range(4):
                row = pl.multiple_of((deep ^ deep_of(d)) * size, 16)
                for n, out in enumerate(outs):
                    out[pl.ds(row, size)] = parts[i][d, n].astype(F32)


def finish_proj(scal, parts):
    half = parts[0].shape[3]
    spec = pl.BlockSpec((half // 2, half), lambda i, s: spot_of(s, i))
    grid_spec = pltpu.PrefetchScalarGridSpec(
        num_scalar_prefetch=1,
        grid=(4,),
        in_specs=[pl.BlockSpec(item.shape, lambda i, s: (0, 0, 0, 0)) for item in parts],
        out_specs=[spec] * 3,
    )
    return pl.pallas_call(
        finish_proj_kernel,
        grid_spec=grid_spec,
        out_shape=[jax.ShapeDtypeStruct((half, 2 * half), F32)] * 3,
        compiler_params=params(),
        cost_estimate=COST,
        name="finish_proj",
    )(scal, *parts)


def add_low(*terms):
    total = terms[0].astype(F32)
    for term in terms[1:]:
        total = total + term.astype(F32)
    return total.astype(BF16)


def to_span(rows):
    return lax.ppermute(rows, "span", [(0, 1), (1, 0)])


def to_seq(rows, bit):
    size = lax.axis_size("seq")
    return lax.ppermute(rows, "seq", [(i, i ^ bit) for i in range(size)])


def after(value, *others):
    return lax.optimization_barrier((value, *others))[0]


class Parts:
    def __init__(self, *arrays):
        self.items = [(item, 0) for item in arrays]

    def terms(self, got):
        arrays = [item for item, _ in self.items]
        if got is not None:
            *arrays, got = lax.optimization_barrier((*arrays, got))
            self.items = [(new, depth) for new, (_, depth) in zip(arrays, self.items)] + [(got, -1)]
        return [item[(0,) * max(depth, 0)] if depth > 0 else item for item, depth in self.items]

    def split(self, got=None):
        terms = self.terms(got)
        self.items = [(item, max(depth, 0) + 1) for item, depth in self.items]
        return add_low(*[term[1] for term in terms])

    def total(self, got=None):
        return add_low(*self.terms(got))


def high_low(total):
    low = total - lax.reduce_precision(total, 8, 7)
    return jnp.concatenate([total.astype(BF16), low.astype(BF16)])


def sum_of(rows):
    half = rows.shape[0] // 2
    return rows[:half].astype(F32) + rows[half:].astype(F32)


def rest_links():
    link, links = 16, []
    while link < lax.axis_size("seq"):
        links.append(link)
        link *= 2
    return links


def reduce_rest(rows):
    shape = rows.shape
    rows = rows.reshape(-1, shape[-1])
    seq = lax.axis_index("seq")
    for link in rest_links():
        bit = (seq // link) % 2
        two = rows.reshape(2, -1, shape[-1])
        send = lax.dynamic_index_in_dim(two, 1 - bit, 0, False)
        rows = add_low(lax.dynamic_index_in_dim(two, bit, 0, False), to_seq(send, link))
    for link in rest_links()[::-1]:
        bit = (seq // link) % 2
        got = to_seq(rows, link)
        rows = jnp.concatenate([jnp.where(bit == 0, rows, got), jnp.where(bit == 0, got, rows)])
    return rows.reshape(shape)


class Line:
    def __init__(self):
        self.last = None

    def take(self, value):
        return value if self.last is None else after(value, self.last)

    def put(self, value):
        self.last = value
        return value


def shards(
    tokens,
    out_cotangent,
    crop_offset,
    start_kept,
    norm1_gain,
    norm1_bias,
    w_query,
    b_query,
    w_key,
    b_key,
    w_value,
    b_value,
    w_out,
    b_out,
    norm2_gain,
    norm2_bias,
    w_up,
    b_up,
    w_down,
    b_down,
):
    rows, width = tokens.shape[1], tokens.shape[2]
    half = width // 2
    quarter = half // 4
    seqs = lax.axis_size("seq")
    place = lax.axis_index("span")
    seq = lax.axis_index("seq")
    core = seq % 2
    bit = (seq // 2) % 2
    deep = (seq // 4) % 4
    first = (crop_offset * start_kept)[0, 0]
    scal = jnp.stack([place, bit, core, first, deep]).astype(jnp.int32)
    start = (2 * bit + core) * quarter

    tok = tokens[0]
    dy = out_cotangent[0]

    piece = jnp.stack(
        [
            lax.dynamic_slice_in_dim(w, start, quarter, 0)
            for w in (w_query, w_key, w_value)
        ]
    )
    piece0 = to_span(piece)
    piece1 = to_seq(piece0, 2)
    pieces = (piece0, piece1, to_seq(piece0, 1), to_seq(piece1, 1))
    tok_oth = to_span(tok)

    small = jnp.concatenate(
        [
            jnp.stack(
                [
                    after(norm1_gain, piece),
                    norm1_bias,
                    b_query,
                    b_key,
                    b_value,
                    norm2_gain,
                    norm2_bias,
                    b_out,
                    b_down,
                ]
            ),
            b_up.reshape(4, half),
        ]
    )
    small_oth = to_span(small)
    small_full = jnp.where(
        place == 0,
        jnp.concatenate([small, small_oth], axis=1),
        jnp.concatenate([small_oth, small], axis=1),
    ).astype(F32)
    vec_one = jnp.pad(small_full[:5], ((0, 3), (0, 0)))
    vec_two = jnp.pad(small_full[5:9], ((0, 4), (0, 0)))
    bup = jnp.concatenate([small_full[9:, :half], small_full[9:, half:]])

    out_piece = lax.dynamic_slice_in_dim(after(w_out, piece0), start, quarter, 0)
    up_piece = lax.dynamic_slice_in_dim(after(w_up, piece0), start, quarter, 0)
    up_piece = up_piece.reshape(quarter, 4, 2, half).transpose(2, 1, 0, 3)
    down_piece = lax.dynamic_slice_in_dim(
        after(w_down, piece0).reshape(4, half, width), start, quarter, 1
    )
    down_piece = [down_piece[0::2], down_piece[1::2]]
    out0 = to_span(out_piece)
    up0 = [to_span(up_piece[0]), None]
    down0 = [to_span(down_piece[0]), None]
    up_b, down_b = to_span(after(up_piece[1], tok_oth)), to_span(after(down_piece[1], tok_oth))

    quarter_dim = HEAD_DIM // 2
    here = jnp.arange(rows, dtype=jnp.int32)
    places = jnp.concatenate([place * rows + here, (1 - place) * rows + here]) - first
    rates = jnp.power(
        jnp.float32(10000.0), -jnp.arange(quarter_dim, dtype=F32) / quarter_dim
    )
    angle = places.astype(F32)[:, None] * jnp.tile(rates, 4)[None, :]
    sign = jnp.tile(jnp.repeat(jnp.array([-1.0, 1.0], F32), quarter_dim), 2)
    cos = jnp.cos(angle)
    sin = jnp.sin(angle) * sign[None, :]

    n1t, query, keys, values, wall = qkv(
        scal, tok, tok_oth, vec_one, cos, sin, (w_query, w_key, w_value), pieces
    )
    out0, up_a = after(out0, n1t), after(up0[0], n1t)
    out_x, up_x = to_seq(out0, 2), to_seq(up_a, 2)
    part = attend(scal, after(query, out0, up_a), keys, values, 0)
    out_x, down_a = after(out_x, part[0]), after(down0[0], part[0])
    down_x = to_seq(down_a, 2)
    outs = (out0, out_x, to_seq(after(out0, part[0]), 1), to_seq(out_x, 1))
    up_core, down_core = to_seq(after(up_a, part[0]), 1), to_seq(down_a, 1)
    up_b, down_b = after(up_b, part[0]), after(down_b, part[0])
    up_bx, down_bx = to_seq(up_b, 2), to_seq(down_b, 2)
    up_bc, down_bc = to_seq(up_b, 1), to_seq(down_b, 1)
    mixed, lse = attend(
        scal, after(query, out_x, down_a, up_b, down_b), keys, values, width // 256, part
    )
    up_x, down_x, up_bx = (after(item, mixed) for item in (up_x, down_x, up_bx))
    ups = (up_a, up_x, up_core, to_seq(up_x, 1))
    downs = (down_a, down_x, down_core, to_seq(down_x, 1))
    hidden, normed, normed_t, wo = hidden_rows(
        scal, after(tok, up_x, down_x, up_bx), mixed, vec_two, w_out, outs
    )
    down_bx = after(down_bx, hidden)
    ups = ups + (up_b, up_bx, up_bc, to_seq(up_bx, 1))
    downs = downs + (down_b, down_bx, down_bc, to_seq(down_bx, 1))
    layer_out, dh, branch, sdown, sup, kdown, kup, gbup, small_two = ffn(
        scal, mixed, dy, vec_two, bup, hidden, normed, normed_t, w_up, w_down, (*ups, *downs)
    )

    def deeper(item):
        return item.reshape(2, 2, 2, 2, *item.shape[3:])

    got_up, got_down = to_seq(sup, 1), to_seq(sdown, 1)
    do = out_back(scal, branch, wo)
    ups = Parts(deeper(kup), deeper(after(got_up, do)))
    send_up = ups.split()
    got_up = to_span(send_up)
    downs = Parts(deeper(kdown), deeper(after(got_down, send_up)))
    send_down = downs.split()
    got_down = to_seq(send_down, 2)

    def back(theirs, dout):
        return attend_back(
            scal, query, keys, values, mixed, dout, lse, cos, sin, n1t, theirs
        )

    split = (2, 2, 2, 3, half // 8, half)
    back_one = back(1, after(do, send_up, send_down))
    send, keep_one = back_one[4:]
    recv = to_seq(send, 1)
    (other,) = other_rows(scal, wall, back_one)
    over = Parts(keep_one.reshape(split), after(recv, other).reshape(split))
    send_over = over.split()
    got_over = to_span(send_over)
    send_up = ups.split(after(got_up, send_over))
    got_up = to_seq(send_up, 2)
    back_two = back(0, after(do, send_over, send_up))
    send, keep = back_two[4:]
    recv = to_seq(send, 1)
    send_over = over.total(after(got_over, send))
    over_x = to_seq(send_over, 2)
    send_down = downs.split(after(got_down, send_over))
    got_down = to_span(send_down)
    send_up = ups.split(after(got_up, send_down))
    got_up = to_seq(send_up, 4)
    dn_oth, other_sum = other_rows(scal, after(wall, send_up), back_two, other, tok_oth)
    line = Line()
    line.put(dn_oth)
    projs = Parts(*[item.reshape(split) for item in (keep, line.take(recv))])
    send_proj = projs.split()
    got_proj = to_span(line.put(send_proj))
    send_up = ups.split(line.take(got_up))
    got_up = to_seq(line.put(send_up), 8)
    dn_own, small, small_oth = own_rows(
        scal, after(wall, send_up), back_two, back_one, tok,
        other_sum, back_one[3], back_two[3], small_two, gbup,
    )
    line.put(dn_own)
    dn_recv = to_span(after(dn_oth, dn_own))
    got_small = to_span(small_oth)

    send_down = downs.split(line.take(got_down))
    got_down = to_seq(line.put(send_down), 4)
    projs = [*projs.terms(line.take(got_proj)), over_x]
    projs = [item.reshape(4, *split[3:]) for item in projs]
    sends = [add_low(*[item[d] for item in projs]) for d in range(1, 4)]
    got_proj = [to_seq(line.put(item), link) for item, link in zip(sends, (8, 4, 12))]
    up = line.put(reduce_rest(ups.total(line.take(got_up))))
    got_up = to_seq(up, 8)
    small = line.put(small + line.take(got_small))
    got_small = to_seq(small, 1)
    send_down = downs.split(line.take(got_down))
    got_down = to_seq(line.put(send_down), 8)
    proj = [item[0] for item in projs] + [line.take(got_proj[0]), *got_proj[1:]]
    proj = line.put(reduce_rest(add_low(*proj)))
    got_proj = [to_seq(proj, 8), to_seq(proj, 4), to_seq(proj, 12)]
    up = line.put(jnp.concatenate([up, line.take(got_up)]))
    got_up = to_seq(up, 4)
    small = small + line.take(got_small)
    for link in rest_links():
        small = small + to_seq(small, link)
    small = high_low(small)
    down = reduce_rest(downs.total(line.take(got_down)))
    down = line.put(jnp.concatenate([down, small]))
    got_down = to_seq(down, 8)
    up = line.put(jnp.concatenate([up, line.take(got_up)]))
    up_x, up_core = to_seq(up, 2), to_seq(up, 1)
    proj = line.put(jnp.stack([proj, line.take(got_proj[0]), *got_proj[1:]]))
    proj_x, proj_core = to_seq(proj, 2), to_seq(proj, 1)

    def ride(mine, got):
        count = mine.shape[0] - small.shape[0]
        total = high_low(sum_of(mine[count:]) + sum_of(got[count:]))
        return jnp.concatenate([mine[:count], got[:count], total])

    down = line.put(ride(down, line.take(got_down)))
    got_down = to_seq(down, 4)
    input_grad = line.put(input_grads(tok, dn_own, line.take(dn_recv), dh, vec_one))
    up_x = line.put(line.take(up_x))
    ups = (up, up_x, up_core, to_seq(up_x, 1))
    proj_x = line.put(line.take(proj_x))
    projs = (proj, proj_x, proj_core, to_seq(proj_x, 1))
    down = line.put(ride(down, line.take(got_down)))
    down_x, down_core = to_seq(down, 2), to_seq(down, 1)
    up_grad = finish_up(scal, ups)
    proj = finish_proj(scal, [line.take(projs[0]), *projs[1:]])
    down_x = after(line.take(down_x), up_grad, proj[0])
    count = down.shape[0] - small.shape[0]
    total = sum_of(down[count:]) + sum_of(down_x[count:])
    down_grad, out_grad = finish_down(scal, (down, down_x, down_core, to_seq(down_x, 1)))

    return (
        layer_out[None],
        input_grad[None],
        total[0],
        total[1],
        proj[0],
        total[2],
        proj[1],
        total[3],
        proj[2],
        total[4],
        out_grad,
        total[7],
        total[5],
        total[6],
        up_grad,
        total[9:13].reshape(-1),
        down_grad,
        total[8],
    )


def solution(mesh):
    row, col = P(None, ("seq", "span"), None), P(None, "seq")
    vec, mat = P("span"), P("span", None)
    weights = (vec, vec, mat, vec, mat, vec, mat, vec, mat, vec, vec, vec, mat, vec, mat, vec)
    return jax.shard_map(
        shards,
        mesh=mesh,
        in_specs=(row, row, col, col) + weights,
        out_specs=(row, row) + weights,
        check_vma=False,
    )
```
